256 devices in a mesh: dp: 4 (over y), gx: 8 (over z_lo, core), gy: 8 (over x, z_hi).
Axes of the slice: x: 4, y: 4, z: 8 (z_hi: 2, z_lo: 4; z = z_hi * 4 + z_lo), core: 2. Of those that a mesh axis runs over, the one named last changes fastest.
Arguments:
- volume: bfloat16 [4, 64, 128, 1024], P('dp', 'gx', 'gy'), may hold values from -6 to 6
- cotangent: bfloat16 [4, 64, 128, 1024], P('dp', 'gx', 'gy'), may hold values from -0.01953125 to 0.01953125
- first_kernel: bfloat16 [3, 3, 3, 64, 64], replicated, may hold values from -0.15625 to 0.15625
- second_kernel: bfloat16 [3, 3, 3, 64, 64], replicated, may hold values from -0.15625 to 0.15625
- coarse_kernel: bfloat16 [3, 3, 3, 64, 64], replicated, may hold values from -0.15625 to 0.15625
Outputs:
- field: bfloat16 [4, 64, 128, 1024], P('dp', 'gx', 'gy')
- first_grad: float32 [3, 3, 3, 64, 64], replicated
- second_grad: float32 [3, 3, 3, 64, 64], replicated
- coarse_grad: float32 [3, 3, 3, 64, 64], replicated
The draws below stay inside these ranges and needn't reach their ends.
All inputs are finite; a program needn't handle non-finite values.
Results may differ from the reference program's by a relative error of at most 0.015.
Values may be sent and summed in bfloat16 or wider, within the bound.
A program may use at most 64 MiB of HBM per device.

```python
import jax
import jax.numpy as jnp
from jax import lax

C = 64
NZ = 16
BATCH = 4
NX = 64
NY = 128


def block_scale(stream_key, dims, split, low, top_value):
    def one(axis_at, blocks):
        draws = jax.random.uniform(jax.random.fold_in(jax.random.fold_in(stream_key, 6), axis_at), (blocks,), jnp.float32, low / len(split), top_value / len(split))
        return jnp.repeat(jnp.exp(draws), dims[axis_at] // blocks).reshape((-1,) + (1,) * (len(dims) - axis_at - 1))

    loudness = one(*split[0])
    for cut in split[1:]:
        loudness = loudness * one(*cut)
    return loudness


def noise(own_key, extent, width, limit, cuts=(), dtype=jnp.bfloat16):
    entries = jax.random.normal(own_key, extent, jnp.float32) * width
    if len(cuts) > 0:
        entries = block_scale(own_key, extent, cuts, -0.22, 0.18) * entries
    return jnp.clip(entries, min=-limit, max=limit).astype(dtype)


def setup_inputs(seed: int = 0) -> dict:
    key_of = jax.random.split(jax.random.key(seed), 6)
    return {
        "volume": noise(key_of[0], (BATCH, NX, NY, NZ * C), 1.0, 6.0, ((0, 4), (1, 8), (2, 8))),
        "cotangent": noise(key_of[1], (BATCH, NX, NY, NZ * C), (1.0 / (BATCH * NX * NY * NZ) ** 0.5), 0.01953125, ((0, 4), (1, 8), (2, 8))),
        "first_kernel": noise(key_of[2], (3, 3, 3, C, C), (27 * C) ** -0.5, 0.15625),
        "second_kernel": noise(key_of[3], (3, 3, 3, C, C), (27 * C) ** -0.5, 0.15625),
        "coarse_kernel": noise(key_of[4], (3, 3, 3, C, C), (27 * C) ** -0.5, 0.15625),
    }


def convolve(values, kernel, pad_side):
    return lax.conv_general_dilated(values, kernel, (1, 1, 1), [(pad_side, pad_side), (pad_side, pad_side), (1, 1)], dimension_numbers=('NDHWC', 'DHWIO', 'NDHWC'), preferred_element_type=jnp.float32)

def kernel_grad(values, slopes, pad_side):
    return lax.conv_general_dilated(values, slopes, (1, 1, 1), [(pad_side, pad_side), (pad_side, pad_side), (1, 1)], dimension_numbers=('CDHWN', 'IDHWO', 'DHWNC'), preferred_element_type=jnp.float32)

def flipped(kernel):
    return jnp.transpose(kernel[::-1, ::-1, ::-1], (0, 1, 2, 4, 3))

def swish_slope(values):
    sigma = jax.nn.sigmoid(values)
    return sigma * (1.0 + values * (1.0 - sigma))

def block_sum(values):
    shape = values.shape
    return values.reshape(shape[0], shape[1] // 2, 2, shape[2] // 2, 2, shape[3] // 2, 2, shape[4]).sum(axis=(2, 4, 6))

def upsampled(values):
    return jnp.repeat(jnp.repeat(jnp.repeat(values, 2, axis=1), 2, axis=2), 2, axis=3)

def reference(volume, cotangent, first_kernel, second_kernel, coarse_kernel):
    inputs = volume.reshape(BATCH, NX, NY, NZ, C)
    upstream = cotangent.reshape(BATCH, NX, NY, NZ, C)
    first = convolve(inputs, first_kernel, 1)
    hidden = jax.nn.silu(first).astype(jnp.bfloat16)
    second = convolve(hidden, second_kernel, 1)
    fine = jax.nn.silu(second).astype(jnp.bfloat16)
    pooled = (block_sum(fine.astype(jnp.float32)) / 8.0).astype(jnp.bfloat16)
    coarse = convolve(pooled, coarse_kernel, 1).astype(jnp.bfloat16)
    field = (fine.astype(jnp.float32) + upsampled(coarse.astype(jnp.float32))).astype(jnp.bfloat16)
    coarse_slope = block_sum(upstream.astype(jnp.float32)).astype(jnp.bfloat16)
    coarse_grad = kernel_grad(pooled, coarse_slope, 1)
    pooled_slope = convolve(coarse_slope, flipped(coarse_kernel), 1)
    fine_slope = (upstream.astype(jnp.float32) + upsampled(pooled_slope) / 8.0).astype(jnp.bfloat16)
    second_slope = (fine_slope.astype(jnp.float32) * swish_slope(second)).astype(jnp.bfloat16)
    second_grad = kernel_grad(hidden, second_slope, 1)
    hidden_slope = convolve(second_slope, flipped(second_kernel), 1)
    first_slope = (hidden_slope * swish_slope(first)).astype(jnp.bfloat16)
    first_grad = kernel_grad(inputs, first_slope, 1)
    return (field.reshape(BATCH, NX, NY, NZ * C), first_grad, second_grad, coarse_grad)
```

```python
import jax
import jax.numpy as jnp
from jax import lax
from jax.experimental import pallas as pl
from jax.experimental.pallas import tpu as pltpu
from jax.sharding import PartitionSpec as P

MESH = pl.DeviceIdType.MESH
F32 = jnp.float32
BF16 = jnp.bfloat16

NI, NJ, LANES = 8, 16, 1024
CI, CJ, CLANES = 4, 8, 512
PAD = 128
GROUP = 256
WINDOW = 512
TAPS = 9


def dot(a, b, dims=((1,), (0,))):
    return lax.dot_general(a, b, (dims, ((), ())), preferred_element_type=F32)


def sigmoid(v):
    return 1.0 / (1.0 + jnp.exp(-v))


def kernel(
    vol, cot, k1, k2, kc,
    field, out_sc, out_f,
    fine_st, coarse_st, xv, xh, xs, xp, xc, slope1, upstream, fine_keep, slopes_t, acc,
    w1, w2, w2b, wc, wcb,
    s_e, r_e, s_n, r_n, s_c, r_c, col, colr, cor, corr,
    part_sc, part_f, in1_sc, in1_f, b2_sc, b2_f, in2_sc, in2_f, in3_sc, in3_f, res_sc, res_f, half,
    se_sem, re_sem, sn_sem, rn_sem, sc_sem, rc_sem,
    s_sc, g_sc, s_f, g_f,
):
    gx, gy, dp = lax.axis_index("gx"), lax.axis_index("gy"), lax.axis_index("dp")
    x_at, z_hi = lax.div(gy, 2), lax.rem(gy, 2)
    z_lo, core = lax.div(gx, 2), lax.rem(gx, 2)
    p_at = x_at * 2 + core
    z_at = z_hi * 4 + z_lo

    def side(at, step):
        return lax.rem(at + step + 8, 8)

    def near(di, dj):
        return {"gx": side(gx, di), "gy": side(gy, dj)}

    def p_peer(r):
        p = lax.rem(p_at + r, 8)
        return p, {"gx": z_lo * 2 + lax.rem(p, 2), "gy": lax.div(p, 2) * 2 + z_hi}

    def y_peer(r):
        q = lax.rem(dp + r, 4)
        return q, {"dp": q}

    def z_peer(r):
        z = lax.rem(z_at + r, 8)
        return z, {"gx": lax.rem(z, 4) * 2 + core, "gy": x_at * 2 + lax.div(z, 4)}

    steps = (-1, 1)
    barrier = pltpu.get_barrier_semaphore()
    partners = [near(s, 0) for s in steps] + [near(0, s) for s in steps]
    partners += [near(s, t) for s in steps for t in steps]
    partners += [p_peer(r)[1] for r in range(1, 8)] + [y_peer(r)[1] for r in range(1, 4)]
    partners += [z_peer(r)[1] for r in range(1, 8)]
    for partner in partners:
        pl.semaphore_signal(barrier, inc=1, device_id=partner, device_id_type=MESH)

    def pack(stage, with_coarse):
        for e in range(2):
            i, ci = e * (NI - 1), e * (CI - 1)
            s_e[stage, e, :, 0:LANES] = fine_st[i].astype(BF16)
            if with_coarse:
                row = coarse_st[ci]
                s_e[stage, e, :, LANES:] = jnp.concatenate([row[:, :256], row[:, 256:]], axis=0).astype(BF16)
        for n in range(2):
            j, cj = n * (NJ - 1), n * (CJ - 1)
            for i in range(NI):
                col[i : i + 1, 0:512] = fine_st[i, j : j + 1, 0:512]
                col[NI + i : NI + i + 1, 0:512] = fine_st[i, j : j + 1, 512:1024]
            if with_coarse:
                for i in range(CI):
                    for k in range(4):
                        col[4 * k + i : 4 * k + i + 1, 512:640] = coarse_st[i, cj : cj + 1, 128 * k : 128 * k + 128]
            s_n[stage, n] = col[...].astype(BF16)
        for e in range(2):
            for n in range(2):
                i, j = e * (NI - 1), n * (NJ - 1)
                for k in range(8):
                    cor[k : k + 1] = fine_st[i, j : j + 1, 128 * k : 128 * k + 128]
                if with_coarse:
                    for k in range(4):
                        cor[8 + k : 9 + k] = coarse_st[e * (CI - 1), n * (CJ - 1) : n * (CJ - 1) + 1, 128 * k : 128 * k + 128]
                s_c[stage, 2 * e + n] = cor[...].astype(BF16)

    def rim_copies(stage, with_coarse):
        copies = []
        wide_e, wide_n = (1280, 640) if with_coarse else (1024, 512)
        for n in range(2):
            copies.append(pltpu.make_async_remote_copy(
                s_n.at[stage, n, :, pl.ds(0, wide_n)], r_n.at[stage, n, :, pl.ds(0, wide_n)],
                sn_sem.at[stage, n], rn_sem.at[stage, n], device_id=near(0, steps[n]), device_id_type=MESH))
        for e in range(2):
            for n in range(2):
                c = 2 * e + n
                copies.append(pltpu.make_async_remote_copy(
                    s_c.at[stage, c], r_c.at[stage, c],
                    sc_sem.at[stage, c], rc_sem.at[stage, c], device_id=near(steps[e], steps[n]), device_id_type=MESH))
        for e in range(2):
            copies.append(pltpu.make_async_remote_copy(
                s_e.at[stage, e, :, pl.ds(0, wide_e)], r_e.at[stage, e, :, pl.ds(0, wide_e)],
                se_sem.at[stage, e], re_sem.at[stage, e], device_id=near(steps[e], 0), device_id_type=MESH))
        return copies

    gx_low, gx_high, gy_low, gy_high = gx > 0, gx < 7, gy > 0, gy < 7

    def place(dst, index, value, low, high, rows):
        at = lax.broadcasted_iota(jnp.int32, value.shape, 0)
        dst[0, index, :, PAD : PAD + value.shape[1]] = jnp.where(
            at == 0, jnp.broadcast_to(low, value.shape), pltpu.roll(value, 1, 0)).astype(dst.dtype)
        dst[1, index, :, PAD : PAD + value.shape[1]] = value.astype(dst.dtype)
        dst[2, index, :, PAD : PAD + value.shape[1]] = jnp.where(
            at == rows - 1, jnp.broadcast_to(high, value.shape), pltpu.roll(value, rows - 1, 0)).astype(dst.dtype)

    def keep(here, value):
        return jnp.where(here, value, 0.0)

    def unpack_rims(stage):
        for n in range(2):
            colr[n] = r_n[stage, n].astype(F32)
        for c in range(4):
            corr[c] = r_c[stage, c].astype(F32)

    def corner(c, first, count):
        return jnp.concatenate([corr[c, first + k : first + k + 1, :] for k in range(count)], axis=1)

    def assemble_fine(stage, dst):
        def body(i, carry):
            low = jnp.concatenate([colr[1, pl.ds(i, 1), 0:512], colr[1, pl.ds(i + NI, 1), 0:512]], axis=1)
            high = jnp.concatenate([colr[0, pl.ds(i, 1), 0:512], colr[0, pl.ds(i + NI, 1), 0:512]], axis=1)
            place(dst, i + 1, fine_st[i], keep(gy_low, low), keep(gy_high, high), NJ)
            return carry

        lax.fori_loop(0, NI, body, 0)
        for e, index, here in ((1, 0, gx_low), (0, NI + 1, gx_high)):
            value = keep(here, r_e[stage, e, :, 0:LANES].astype(F32))
            low = keep(here & gy_low, corner(2 * e + 1, 0, 8))
            high = keep(here & gy_high, corner(2 * e, 0, 8))
            place(dst, index, value, low, high, NJ)

    def assemble_coarse(stage, dst):
        for i in range(CI):
            low = jnp.concatenate([colr[1, 4 * k + i : 4 * k + i + 1, 512:640] for k in range(4)], axis=1)
            high = jnp.concatenate([colr[0, 4 * k + i : 4 * k + i + 1, 512:640] for k in range(4)], axis=1)
            place(dst, i + 1, coarse_st[i], keep(gy_low, low), keep(gy_high, high), CJ)
        for e, index, here in ((1, 0, gx_low), (0, CI + 1, gx_high)):
            row = r_e[stage, e, :, LANES:].astype(F32)
            value = keep(here, jnp.concatenate([row[:CJ], row[CJ:]], axis=1))
            low = keep(here & gy_low, corner(2 * e + 1, 8, 4))
            high = keep(here & gy_high, corner(2 * e, 8, 4))
            place(dst, index, value, low, high, CJ)

    def fine_window(src, t):
        a, b = t // 3, t % 3
        return jnp.concatenate(
            [src[b, a : a + NI, :, GROUP * g : GROUP * g + WINDOW].reshape(NI * NJ, WINDOW) for g in range(4)], axis=0)

    def coarse_window(src, t):
        a, b = t // 3, t % 3
        return jnp.concatenate(
            [src[b, a : a + CI, :, GROUP * g : GROUP * g + WINDOW].reshape(CI * CJ, WINDOW) for g in range(2)],
            axis=0).astype(BF16)

    def fine_conv(src, weights, dims):
        total = dot(fine_window(src, 0), weights[0], dims)
        for t in range(1, TAPS):
            total = total + dot(fine_window(src, t), weights[t], dims)
        return total

    def coarse_conv(src, weights, dims):
        total = dot(coarse_window(src, 0), weights[0], dims)
        for t in range(1, TAPS):
            total = total + dot(coarse_window(src, t), weights[t], dims)
        return total

    forward, backward = ((1,), (0,)), ((1,), (1,))

    def grads(window, slopes, store):
        for t in range(TAPS):
            g = dot(slopes, window(t))
            even = g[0:64, 0:384] + g[128:192, 128:512]
            odd = g[64:128, 128:384] + g[192:256, 256:512]
            shifted = jnp.concatenate([even[:, 64:192], even[:, 192:320]], axis=1)
            total = odd + shifted
            store(t, total[:, 0:128].astype(BF16))
            half[t] = total[:, 128:256]
        lane = lax.broadcasted_iota(jnp.int32, (64, 128), 1)
        for u in range(5):
            left = half[2 * u]
            right = pltpu.roll(half[2 * u + 1], 64, 1) if u < 4 else jnp.zeros_like(left)
            store(TAPS + u, jnp.where(lane < 64, left, right).astype(BF16))

    def pool_matrix(rows, columns, flip):
        r = lax.broadcasted_iota(jnp.int32, (rows, columns), 1 if flip else 0)
        s = lax.broadcasted_iota(jnp.int32, (rows, columns), 0 if flip else 1)
        r = r & 31
        return jnp.where(r == (s >> 5) * 8 + ((s & 15) >> 1), 1.0, 0.0).astype(BF16)

    def pool(value):
        sums = dot(pool_matrix(32, 128, False), value)
        lane = lax.broadcasted_iota(jnp.int32, (32, 128), 1)
        tiles = []
        for k in range(4):
            pair = []
            for m in range(2):
                tile = sums[:, 256 * k + 128 * m : 256 * k + 128 * m + 128]
                pair.append(tile + pltpu.roll(tile, 64, 1))
            tiles.append(jnp.where(lane < 64, pair[0], pair[1]))
        return jnp.concatenate(tiles, axis=1).reshape(CI, CJ, CLANES)

    def spread(value):
        lane = lax.broadcasted_iota(jnp.int32, (32, 128), 1)
        tiles = []
        for k in range(4):
            tile = value[:, 128 * k : 128 * k + 128]
            turned = pltpu.roll(tile, 64, 1)
            tiles += [jnp.where(lane < 64, tile, turned), jnp.where(lane < 64, turned, tile)]
        return jnp.concatenate(tiles, axis=1)

    def ungroup(value, rows):
        return jnp.concatenate([value[rows * g : rows * (g + 1)] for g in range(value.shape[0] // rows)], axis=1)

    def make_sum(part, in1, b2, in2, in3, res, send, got):
        def c1(r):
            p, peer = p_peer(r)
            return pltpu.make_async_remote_copy(part.at[pl.ds(p * 4, 4)], in1.at[pl.ds((r - 1) * 4, 4)], send.at[r - 1], got.at[r - 1],
                                                device_id=peer, device_id_type=MESH)

        def c2(r):
            q, peer = y_peer(r)
            return pltpu.make_async_remote_copy(b2.at[q], in2.at[r - 1], send.at[6 + r], got.at[6 + r],
                                                device_id=peer, device_id_type=MESH)

        def c3(r):
            _, peer = z_peer(r)
            return pltpu.make_async_remote_copy(in3.at[z_at], in3.at[z_at], send.at[9 + r], got.at[9 + r],
                                                device_id=peer, device_id_type=MESH)

        def c4(r):
            _, peer = y_peer(r)
            mine = p_at * 4 + dp
            return pltpu.make_async_remote_copy(res.at[mine], res.at[mine], send.at[16 + r], got.at[16 + r],
                                                device_id=peer, device_id_type=MESH)

        def c5(r):
            _, peer = p_peer(r)
            mine = pl.ds(p_at * 4, 4)
            return pltpu.make_async_remote_copy(res.at[mine], res.at[mine], send.at[19 + r], got.at[19 + r],
                                                device_id=peer, device_id_type=MESH)

        def start(make, count):
            for r in range(1, count):
                make(r).start()

        def finish(make, count):
            for r in range(1, count):
                make(r).wait_recv()

        def s1():
            start(c1, 8)

        def s2():
            finish(c1, 8)
            total = part[pl.ds(p_at * 4, 4)].astype(F32)
            for r in range(7):
                total = total + in1[4 * r : 4 * r + 4].astype(F32)
            b2[...] = total.astype(BF16)
            start(c2, 4)

        def s3():
            finish(c2, 4)
            total = b2[dp].astype(F32)
            for r in range(3):
                total = total + in2[r].astype(F32)
            in3[z_at] = total.astype(BF16)
            start(c3, 8)

        def s4():
            finish(c3, 8)
            total = in3[0].astype(F32)
            for r in range(1, 8):
                total = total + in3[r].astype(F32)
            res[p_at * 4 + dp] = total.astype(BF16)
            start(c4, 4)

        def s5():
            finish(c4, 4)
            start(c5, 8)

        def s6(out):
            finish(c5, 8)
            out[...] = res[...]
            for make, count in ((c1, 8), (c2, 4), (c3, 8), (c4, 4), (c5, 8)):
                for r in range(1, count):
                    make(r).wait_send()

        return s1, s2, s3, s4, s5, s6

    sum_sc = make_sum(part_sc, in1_sc, b2_sc, in2_sc, in3_sc, res_sc, s_sc, g_sc)
    sum_f = make_sum(part_f, in1_f, b2_f, in2_f, in3_f, res_f, s_f, g_f)

    fine_st[...] = vol[...].astype(F32)
    coarse_slope = pool(cot[...].reshape(NI * NJ, LANES))
    coarse_st[...] = coarse_slope.astype(BF16).astype(F32)
    cor[...] = jnp.zeros_like(cor)
    pack(0, True)
    pl.semaphore_wait(barrier, len(partners))
    for copy in rim_copies(0, True):
        copy.start()

    def build(k, fwd, bwd):
        if fwd is not None:
            fwd[...] = jnp.zeros_like(fwd)
        if bwd is not None:
            bwd[...] = jnp.zeros_like(bwd)

        def body(t, carry):
            c0, c1, c2 = (k[3 * t + c] for c in range(3))
            zero = jnp.zeros_like(c0)
            ta = jnp.concatenate([c2, c1], axis=1)
            tb = jnp.concatenate([c0, zero], axis=1)
            tc = jnp.concatenate([zero, c2], axis=1)
            td = jnp.concatenate([c1, c0], axis=1)
            if fwd is not None:
                for pair in range(2):
                    for m, tile in enumerate((tb, td, ta, tc)):
                        row = 64 * (2 * pair + 1 + m)
                        fwd[t, row : row + 64, 128 * pair : 128 * pair + 128] = tile
            if bwd is not None:
                u = 8 - t
                for pair in range(2):
                    row, lane = 128 * pair, 128 * pair
                    bwd[u, row : row + 64, lane : lane + 128] = tc
                    bwd[u, row : row + 64, lane + 128 : lane + 256] = td
                    bwd[u, row + 64 : row + 128, lane + 128 : lane + 256] = ta
                    bwd[u, row + 64 : row + 128, lane + 256 : lane + 384] = tb
            return carry

        lax.fori_loop(0, TAPS, body, 0)

    build(k1, w1, None)
    build(k2, w2, w2b)
    build(kc, wc, wcb)
    for padded in (xv, xh, xs, xp, xc):
        rows, tail = padded.shape[2], padded.shape[3] - PAD
        padded[:, :, :, 0:PAD] = jnp.zeros((3, padded.shape[1], rows, PAD), padded.dtype)
        padded[:, :, :, tail:] = jnp.zeros((3, padded.shape[1], rows, PAD), padded.dtype)
    part_sc[28:32] = jnp.zeros((4, 64, 128), BF16)
    part_f[28:32] = jnp.zeros((4, 32, 128), BF16)

    for copy in rim_copies(0, True):
        copy.wait_recv()
    unpack_rims(0)
    assemble_fine(0, xv)
    assemble_coarse(0, xc)

    first = ungroup(fine_conv(xv, w1, forward), NI * NJ)
    sigma = sigmoid(first)
    slope1[...] = sigma * (1.0 + first * (1.0 - sigma))
    fine_st[...] = (first * sigma).astype(BF16).astype(F32).reshape(NI, NJ, LANES)
    pack(1, False)
    for copy in rim_copies(1, False):
        copy.start()

    def widen(value):
        wide = spread(value)
        top = wide.astype(BF16)
        rest = (wide - top.astype(F32)).astype(BF16)
        return dot(pool_matrix(128, 64, True), jnp.concatenate([top, rest], axis=0))

    pooled_slope = ungroup(coarse_conv(xc, wcb, backward), CI * CJ)
    upstream[...] = (cot[...].reshape(NI * NJ, LANES).astype(F32) + widen(pooled_slope) * 0.125).astype(BF16).astype(F32)

    for copy in rim_copies(1, False):
        copy.wait_recv()
    unpack_rims(1)
    assemble_fine(1, xh)

    second = ungroup(fine_conv(xh, w2, forward), NI * NJ)
    sigma = sigmoid(second)
    fine = (second * sigma).astype(BF16)
    fine_keep[...] = fine
    coarse_st[...] = (pool(fine) * 0.125).astype(BF16).astype(F32)
    second_slope = (upstream[...] * (sigma * (1.0 + second * (1.0 - sigma)))).astype(BF16).astype(F32)
    fine_st[...] = second_slope.reshape(NI, NJ, LANES)
    pack(2, True)
    for copy in rim_copies(2, True):
        copy.start()

    def grouped_t(value, groups):
        return jnp.concatenate([value[:, GROUP * g : GROUP * (g + 1)] for g in range(groups)], axis=0).T.astype(BF16)

    slopes_t[...] = grouped_t(fine_st[...].reshape(NI * NJ, LANES), 4)

    def store_second(n, value):
        part_sc[n] = value

    def store_coarse(n, value):
        part_sc[14 + n] = value

    def store_first(n, value):
        part_f[2 * n : 2 * n + 2] = value.reshape(2, 32, 128)

    grads(lambda t: fine_window(xh, t), slopes_t[...], store_second)

    for copy in rim_copies(2, True):
        copy.wait_recv()
    unpack_rims(2)
    assemble_coarse(2, xp)
    centre = xc[1, 1 : CI + 1, :, PAD : PAD + CLANES].reshape(CI * CJ, CLANES)
    grads(lambda t: coarse_window(xp, t), grouped_t(centre, 2), store_coarse)
    sum_sc[0]()
    assemble_fine(2, xs)

    hidden_slope = ungroup(fine_conv(xs, w2b, backward), NI * NJ)
    first_slope = (hidden_slope * slope1[...]).astype(BF16).astype(F32)
    slopes_t[...] = grouped_t(first_slope, 4)
    sum_sc[1]()
    grads(lambda t: fine_window(xv, t), slopes_t[...], store_first)
    sum_f[0]()
    sum_sc[2]()

    coarse = ungroup(coarse_conv(xp, wc, forward), CI * CJ).astype(BF16)
    wide = spread(coarse.astype(F32)).astype(BF16)
    repeated = dot(pool_matrix(128, 32, True), wide)
    field[...] = (fine_keep[...].astype(F32) + repeated).astype(BF16).reshape(NI, NJ, LANES)

    sum_f[1]()
    sum_sc[3]()
    sum_f[2]()
    sum_sc[4]()
    sum_f[3]()
    sum_f[4]()
    sum_sc[5](out_sc)
    sum_f[5](out_f)
    for stage in range(3):
        for copy in rim_copies(stage, stage != 1):
            copy.wait_send()


def unpack_kernel(field_in, sc, f, field, first_grad, second_grad, coarse_grad):
    field[...] = field_in[...]

    def place(read, out):
        for t in range(TAPS):
            block = read(t).astype(F32).T
            out[3 * t] = block[0:64]
            out[3 * t + 1] = block[64:128]
        for u in range(5):
            block = read(TAPS + u).astype(F32).T
            out[6 * u + 2] = block[0:64]
            if u < 4:
                out[6 * u + 5] = block[64:128]

    place(lambda n: sc[n], second_grad)
    place(lambda n: sc[14 + n], coarse_grad)
    place(lambda n: f[2 * n : 2 * n + 2].reshape(64, 128), first_grad)


def per_device(volume, cotangent, first_kernel, second_kernel, coarse_kernel):
    in_vmem = pl.BlockSpec(memory_space=pltpu.VMEM)
    dma = pltpu.SemaphoreType.DMA

    def sum_buffers(rows):
        return [
            pltpu.VMEM((32, rows, 128), BF16), pltpu.VMEM((28, rows, 128), BF16), pltpu.VMEM((4, rows, 128), BF16),
            pltpu.VMEM((3, rows, 128), BF16), pltpu.VMEM((8, rows, 128), BF16), pltpu.VMEM((32, rows, 128), BF16),
        ]

    sc_bufs, f_bufs = sum_buffers(64), sum_buffers(32)
    mixed = [b for pair in zip(sc_bufs, f_bufs) for b in pair]
    scratch = [
        pltpu.VMEM((NI, NJ, LANES), F32),
        pltpu.VMEM((CI, CJ, CLANES), F32),
        pltpu.VMEM((3, NI + 2, NJ, LANES + 2 * PAD), BF16),
        pltpu.VMEM((3, NI + 2, NJ, LANES + 2 * PAD), BF16),
        pltpu.VMEM((3, NI + 2, NJ, LANES + 2 * PAD), BF16),
        pltpu.VMEM((3, CI + 2, CJ, CLANES + 2 * PAD), F32),
        pltpu.VMEM((3, CI + 2, CJ, CLANES + 2 * PAD), F32),
        pltpu.VMEM((NI * NJ, LANES), F32),
        pltpu.VMEM((NI * NJ, LANES), F32),
        pltpu.VMEM((NI * NJ, LANES), BF16),
        pltpu.VMEM((GROUP, 4 * NI * NJ), BF16),
        pltpu.VMEM((4 * NI * NJ, GROUP), F32),
        pltpu.VMEM((TAPS, WINDOW, GROUP), BF16),
        pltpu.VMEM((TAPS, WINDOW, GROUP), BF16),
        pltpu.VMEM((TAPS, GROUP, WINDOW), BF16),
        pltpu.VMEM((TAPS, WINDOW, GROUP), BF16),
        pltpu.VMEM((TAPS, GROUP, WINDOW), BF16),
        pltpu.VMEM((3, 2, 16, 1280), BF16), pltpu.VMEM((3, 2, 16, 1280), BF16),
        pltpu.VMEM((3, 2, 16, 640), BF16), pltpu.VMEM((3, 2, 16, 640), BF16),
        pltpu.VMEM((3, 4, 16, 128), BF16), pltpu.VMEM((3, 4, 16, 128), BF16),
        pltpu.VMEM((16, 640), F32), pltpu.VMEM((2, 16, 640), F32),
        pltpu.VMEM((16, 128), F32), pltpu.VMEM((4, 16, 128), F32),
        *mixed,
        pltpu.VMEM((TAPS, 64, 128), F32),
        dma((3, 2)), dma((3, 2)), dma((3, 2)), dma((3, 2)), dma((3, 4)), dma((3, 4)),
        dma((27,)), dma((27,)), dma((27,)), dma((27,)),
    ]
    block = volume.shape[1:]
    taps = (27, 64, 64)
    field, sc, f = pl.pallas_call(
        kernel,
        out_shape=(
            jax.ShapeDtypeStruct(block, BF16),
            jax.ShapeDtypeStruct((32, 64, 128), BF16),
            jax.ShapeDtypeStruct((32, 32, 128), BF16),
        ),
        in_specs=[in_vmem] * 5,
        out_specs=(in_vmem,) * 3,
        scratch_shapes=scratch,
        compiler_params=pltpu.CompilerParams(
            collective_id=0, has_side_effects=True, vmem_limit_bytes=48 * 1024 * 1024
        ),
        name="block",
    )(volume[0], cotangent[0], first_kernel.reshape(taps), second_kernel.reshape(taps), coarse_kernel.reshape(taps))
    field, first_grad, second_grad, coarse_grad = pl.pallas_call(
        unpack_kernel,
        out_shape=(jax.ShapeDtypeStruct(block, BF16),) + (jax.ShapeDtypeStruct(taps, F32),) * 3,
        in_specs=[in_vmem] * 3,
        out_specs=(in_vmem,) * 4,
        compiler_params=pltpu.CompilerParams(vmem_limit_bytes=32 * 1024 * 1024),
        name="unpack",
    )(field, sc, f)
    kernel_shape = first_kernel.shape
    return (
        field[None],
        first_grad.reshape(kernel_shape),
        second_grad.reshape(kernel_shape),
        coarse_grad.reshape(kernel_shape),
    )


def solution(mesh):
    in_specs = (P("dp", "gx", "gy", None), P("dp", "gx", "gy", None), P(), P(), P())
    out_specs = (P("dp", "gx", "gy", None), P(), P(), P())
    return jax.shard_map(
        per_device, mesh=mesh, in_specs=in_specs, out_specs=out_specs, check_vma=False
    )
```

```python
import jax
import jax.numpy as jnp
from jax import lax
from jax.experimental import pallas as pl
from jax.experimental.pallas import tpu as pltpu
from jax.sharding import PartitionSpec as P

MESH = pl.DeviceIdType.MESH
F32 = jnp.float32
BF16 = jnp.bfloat16

NI, NJ, LANES = 8, 16, 1024
CI, CJ, CLANES = 4, 8, 512
PAD = 128
GROUP = 256
WINDOW = 512
TAPS = 9


def dot(a, b, dims=((1,), (0,))):
    return lax.dot_general(a, b, (dims, ((), ())), preferred_element_type=F32)


def sigmoid(v):
    return 1.0 / (1.0 + jnp.exp(-v))


def kernel(
    vol_in, cot_in, k1_in, k2_in, kc_in,
    field, out_sc, out_f,
    fine_st, coarse_st, xv, xh, xs, xp, xc, slope1, upstream, fine_keep, slopes_t, acc,
    w1, w2, w2b, wc, wcb,
    s_e, r_e, s_n, r_n, s_c, r_c, col, colr, cor, corr,
    part_sc, part_f, in1_sc, in1_f, b2_sc, b2_f, in2_sc, in2_f, in3_sc, in3_f, res_sc, res_f, half,
    se_sem, re_sem, sn_sem, rn_sem, sc_sem, rc_sem,
    s_sc, g_sc, s_f, g_f, in_sem,
    vol, cot, k1, k2, kc,
):
    loads = [
        pltpu.make_async_copy(src, dst, in_sem.at[n])
        for n, (src, dst) in enumerate(((vol_in, vol), (cot_in, cot), (k1_in, k1), (k2_in, k2), (kc_in, kc)))
    ]
    for load in loads:
        load.start()

    gx, gy, dp = lax.axis_index("gx"), lax.axis_index("gy"), lax.axis_index("dp")
    x_at, z_hi = lax.div(gy, 2), lax.rem(gy, 2)
    z_lo, core = lax.div(gx, 2), lax.rem(gx, 2)
    w_at = x_at * 4 + dp
    z_at = z_hi * 4 + z_lo

    def side(at, step):
        return lax.rem(at + step + 8, 8)

    def near(di, dj):
        return {"gx": side(gx, di), "gy": side(gy, dj)}

    def w_peer(r):
        x, y = lax.rem(x_at + r // 4, 4), lax.rem(dp + r % 4, 4)
        return x * 4 + y, {"gy": x * 2 + z_hi, "dp": y}

    other_core = {"gx": z_lo * 2 + 1 - core}

    def z_peer(r):
        z = lax.rem(z_at + r, 8)
        return z, {"gx": lax.rem(z, 4) * 2 + core, "gy": x_at * 2 + lax.div(z, 4)}

    steps = (-1, 1)
    barrier = pltpu.get_barrier_semaphore()
    partners = [near(s, 0) for s in steps] + [near(0, s) for s in steps]
    partners += [near(s, t) for s in steps for t in steps]
    partners += [other_core] + [w_peer(r)[1] for r in range(1, 16)] + [z_peer(r)[1] for r in range(1, 8)]
    for partner in partners:
        pl.semaphore_signal(barrier, inc=1, device_id=partner, device_id_type=MESH)

    def pack(stage, with_coarse):
        for e in range(2):
            i, ci = e * (NI - 1), e * (CI - 1)
            s_e[stage, e, :, 0:LANES] = fine_st[i].astype(BF16)
            if with_coarse:
                row = coarse_st[ci]
                s_e[stage, e, :, LANES:] = jnp.concatenate([row[:, :256], row[:, 256:]], axis=0).astype(BF16)
        for n in range(2):
            j, cj = n * (NJ - 1), n * (CJ - 1)
            for i in range(NI):
                col[i : i + 1, 0:512] = fine_st[i, j : j + 1, 0:512]
                col[NI + i : NI + i + 1, 0:512] = fine_st[i, j : j + 1, 512:1024]
            if with_coarse:
                for i in range(CI):
                    for k in range(4):
                        col[4 * k + i : 4 * k + i + 1, 512:640] = coarse_st[i, cj : cj + 1, 128 * k : 128 * k + 128]
            s_n[stage, n] = col[...].astype(BF16)
        for e in range(2):
            for n in range(2):
                i, j = e * (NI - 1), n * (NJ - 1)
                for k in range(8):
                    cor[k : k + 1] = fine_st[i, j : j + 1, 128 * k : 128 * k + 128]
                if with_coarse:
                    for k in range(4):
                        cor[8 + k : 9 + k] = coarse_st[e * (CI - 1), n * (CJ - 1) : n * (CJ - 1) + 1, 128 * k : 128 * k + 128]
                s_c[stage, 2 * e + n] = cor[...].astype(BF16)

    gx_low, gx_high, gy_low, gy_high = gx > 0, gx < 7, gy > 0, gy < 7
    to_x, to_y = (gx_low, gx_high), (gy_low, gy_high)

    def rim_copies(stage, with_coarse):
        wide_e, wide_n = (1280, 640) if with_coarse else (1024, 512)
        copies = []
        for n in range(2):
            copies.append((to_y[n], to_y[1 - n], pltpu.make_async_remote_copy(
                s_n.at[stage, n, :, pl.ds(0, wide_n)], r_n.at[stage, n, :, pl.ds(0, wide_n)],
                sn_sem.at[stage, n], rn_sem.at[stage, n], device_id=near(0, steps[n]), device_id_type=MESH)))
        for e in range(2):
            for n in range(2):
                c = 2 * e + n
                copies.append((to_x[e] & to_y[n], to_x[1 - e] & to_y[1 - n], pltpu.make_async_remote_copy(
                    s_c.at[stage, c], r_c.at[stage, c],
                    sc_sem.at[stage, c], rc_sem.at[stage, c], device_id=near(steps[e], steps[n]), device_id_type=MESH)))
        for e in range(2):
            copies.append((to_x[e], to_x[1 - e], pltpu.make_async_remote_copy(
                s_e.at[stage, e, :, pl.ds(0, wide_e)], r_e.at[stage, e, :, pl.ds(0, wide_e)],
                se_sem.at[stage, e], re_sem.at[stage, e], device_id=near(steps[e], 0), device_id_type=MESH)))
        return copies

    def send_rims(stage, with_coarse):
        for there, _, copy in rim_copies(stage, with_coarse):
            pl.when(there)(copy.start)

    def await_rims(stage, with_coarse):
        for _, there, copy in rim_copies(stage, with_coarse):
            pl.when(there)(copy.wait_recv)

    def place(dst, index, value, low, high, rows):
        at = lax.broadcasted_iota(jnp.int32, value.shape, 0)
        dst[0, index, :, PAD : PAD + value.shape[1]] = jnp.where(
            at == 0, jnp.broadcast_to(low, value.shape), pltpu.roll(value, 1, 0)).astype(dst.dtype)
        dst[1, index, :, PAD : PAD + value.shape[1]] = value.astype(dst.dtype)
        dst[2, index, :, PAD : PAD + value.shape[1]] = jnp.where(
            at == rows - 1, jnp.broadcast_to(high, value.shape), pltpu.roll(value, rows - 1, 0)).astype(dst.dtype)

    def keep(here, value):
        return jnp.where(here, value, 0.0)

    def unpack_rims(stage):
        for n in range(2):
            colr[n] = r_n[stage, n].astype(F32)
        for c in range(4):
            corr[c] = r_c[stage, c].astype(F32)

    def corner(c, first, count):
        return jnp.concatenate([corr[c, first + k : first + k + 1, :] for k in range(count)], axis=1)

    def assemble_fine(stage, dst):
        def body(i, carry):
            low = jnp.concatenate([colr[1, pl.ds(i, 1), 0:512], colr[1, pl.ds(i + NI, 1), 0:512]], axis=1)
            high = jnp.concatenate([colr[0, pl.ds(i, 1), 0:512], colr[0, pl.ds(i + NI, 1), 0:512]], axis=1)
            place(dst, i + 1, fine_st[i], keep(gy_low, low), keep(gy_high, high), NJ)
            return carry

        lax.fori_loop(0, NI, body, 0)
        for e, index, here in ((1, 0, gx_low), (0, NI + 1, gx_high)):
            value = keep(here, r_e[stage, e, :, 0:LANES].astype(F32))
            low = keep(here & gy_low, corner(2 * e + 1, 0, 8))
            high = keep(here & gy_high, corner(2 * e, 0, 8))
            place(dst, index, value, low, high, NJ)

    def assemble_coarse(stage, dst):
        for i in range(CI):
            low = jnp.concatenate([colr[1, 4 * k + i : 4 * k + i + 1, 512:640] for k in range(4)], axis=1)
            high = jnp.concatenate([colr[0, 4 * k + i : 4 * k + i + 1, 512:640] for k in range(4)], axis=1)
            place(dst, i + 1, coarse_st[i], keep(gy_low, low), keep(gy_high, high), CJ)
        for e, index, here in ((1, 0, gx_low), (0, CI + 1, gx_high)):
            row = r_e[stage, e, :, LANES:].astype(F32)
            value = keep(here, jnp.concatenate([row[:CJ], row[CJ:]], axis=1))
            low = keep(here & gy_low, corner(2 * e + 1, 8, 4))
            high = keep(here & gy_high, corner(2 * e, 8, 4))
            place(dst, index, value, low, high, CJ)

    def fine_window(src, t):
        a, b = t // 3, t % 3
        return jnp.concatenate(
            [src[b, a : a + NI, :, GROUP * g : GROUP * g + WINDOW].reshape(NI * NJ, WINDOW) for g in range(4)], axis=0)

    def coarse_window(src, t):
        a, b = t // 3, t % 3
        return jnp.concatenate(
            [src[b, a : a + CI, :, GROUP * g : GROUP * g + WINDOW].reshape(CI * CJ, WINDOW) for g in range(2)],
            axis=0).astype(BF16)

    def fine_conv(src, weights):
        total = dot(fine_window(src, 0), weights[0])
        for t in range(1, TAPS):
            total = total + dot(fine_window(src, t), weights[t])
        return total

    def coarse_conv(src, weights):
        total = dot(coarse_window(src, 0), weights[0])
        for t in range(1, TAPS):
            total = total + dot(coarse_window(src, t), weights[t])
        return total

    def grads(window, slopes, store):
        for t in range(TAPS):
            g = dot(slopes, window(t))
            even = g[0:64, 0:384] + g[128:192, 128:512]
            odd = g[64:128, 128:384] + g[192:256, 256:512]
            shifted = jnp.concatenate([even[:, 64:192], even[:, 192:320]], axis=1)
            total = odd + shifted
            store(t, total[:, 0:128].astype(BF16))
            half[t] = total[:, 128:256]
        lane = lax.broadcasted_iota(jnp.int32, (64, 128), 1)
        for u in range(5):
            left = half[2 * u]
            right = pltpu.roll(half[2 * u + 1], 64, 1) if u < 4 else jnp.zeros_like(left)
            store(TAPS + u, jnp.where(lane < 64, left, right).astype(BF16))

    def pool_matrix(rows, columns, flip):
        r = lax.broadcasted_iota(jnp.int32, (rows, columns), 1 if flip else 0)
        s = lax.broadcasted_iota(jnp.int32, (rows, columns), 0 if flip else 1)
        r = r & 31
        return jnp.where(r == (s >> 5) * 8 + ((s & 15) >> 1), 1.0, 0.0).astype(BF16)

    def pool(value):
        sums = dot(pool_matrix(32, 128, False), value)
        lane = lax.broadcasted_iota(jnp.int32, (32, 128), 1)
        tiles = []
        for k in range(4):
            pair = []
            for m in range(2):
                tile = sums[:, 256 * k + 128 * m : 256 * k + 128 * m + 128]
                pair.append(tile + pltpu.roll(tile, 64, 1))
            tiles.append(jnp.where(lane < 64, pair[0], pair[1]))
        return jnp.concatenate(tiles, axis=1).reshape(CI, CJ, CLANES)

    def spread(value):
        lane = lax.broadcasted_iota(jnp.int32, (32, 128), 1)
        tiles = []
        for k in range(4):
            tile = value[:, 128 * k : 128 * k + 128]
            turned = pltpu.roll(tile, 64, 1)
            tiles += [jnp.where(lane < 64, tile, turned), jnp.where(lane < 64, turned, tile)]
        return jnp.concatenate(tiles, axis=1)

    def ungroup(value, rows):
        return jnp.concatenate([value[rows * g : rows * (g + 1)] for g in range(value.shape[0] // rows)], axis=1)

    def make_sum(part, in1, b2, in2, in3, res, send, got):
        def c1(r):
            return pltpu.make_async_remote_copy(part.at[pl.ds((1 - core) * 16, 16)], in1, send.at[0], got.at[0],
                                                device_id=other_core, device_id_type=MESH)

        def c2(r):
            w, peer = w_peer(r)
            return pltpu.make_async_remote_copy(b2.at[w], in2.at[r - 1], send.at[r], got.at[r],
                                                device_id=peer, device_id_type=MESH)

        def c3(r):
            _, peer = z_peer(r)
            return pltpu.make_async_remote_copy(in3.at[z_at], in3.at[z_at], send.at[15 + r], got.at[15 + r],
                                                device_id=peer, device_id_type=MESH)

        mine = core * 16 + w_at

        def c4(r):
            _, peer = w_peer(r)
            return pltpu.make_async_remote_copy(res.at[mine], res.at[mine], send.at[22 + r], got.at[22 + r],
                                                device_id=peer, device_id_type=MESH)

        def c5(r):
            own = pl.ds(core * 16, 16)
            return pltpu.make_async_remote_copy(res.at[own], res.at[own], send.at[38], got.at[38],
                                                device_id=other_core, device_id_type=MESH)

        def start(make, count):
            for r in range(1, count):
                make(r).start()

        def finish(make, count):
            for r in range(1, count):
                make(r).wait_recv()

        def s1():
            start(c1, 2)

        def s2():
            finish(c1, 2)
            b2[...] = (part[pl.ds(core * 16, 16)].astype(F32) + in1[...].astype(F32)).astype(BF16)
            start(c2, 16)

        def s3():
            finish(c2, 16)
            total = b2[w_at].astype(F32)
            for r in range(15):
                total = total + in2[r].astype(F32)
            in3[z_at] = total.astype(BF16)
            start(c3, 8)

        def s4():
            finish(c3, 8)
            total = in3[0].astype(F32)
            for r in range(1, 8):
                total = total + in3[r].astype(F32)
            res[mine] = total.astype(BF16)
            start(c4, 16)

        def s5():
            finish(c4, 16)
            start(c5, 2)

        def s6(out):
            finish(c5, 2)
            out[...] = res[...]
            for make, count in ((c1, 2), (c2, 16), (c3, 8), (c4, 16), (c5, 2)):
                for r in range(1, count):
                    make(r).wait_send()

        return s1, s2, s3, s4, s5, s6

    sum_sc = make_sum(part_sc, in1_sc, b2_sc, in2_sc, in3_sc, res_sc, s_sc, g_sc)
    sum_f = make_sum(part_f, in1_f, b2_f, in2_f, in3_f, res_f, s_f, g_f)

    loads[0].wait()
    fine_st[...] = vol[...].astype(F32)
    loads[1].wait()
    coarse_slope = pool(cot[...].reshape(NI * NJ, LANES))
    coarse_st[...] = coarse_slope.astype(BF16).astype(F32)
    cor[...] = jnp.zeros_like(cor)
    pack(0, True)
    pl.semaphore_wait(barrier, len(partners))
    send_rims(0, True)

    def build(k, fwd, bwd):
        for w in (fwd, bwd):
            if w is not None:
                w[...] = jnp.zeros_like(w)

        def band(w, t, c0, c1, c2):
            zero = jnp.zeros_like(c0)
            pairs = ((c0, zero), (c1, c0), (c2, c1), (zero, c2))
            for m, tile in enumerate(jnp.concatenate(pair, axis=1) for pair in pairs):
                for pair in range(2):
                    row = 64 * (2 * pair + 1 + m)
                    w[t, row : row + 64, 128 * pair : 128 * pair + 128] = tile

        def body(t, carry):
            taps = [k[3 * t + c] for c in range(3)]
            band(fwd, t, *taps)
            if bwd is not None:
                c0, c1, c2 = (v.astype(F32).T.astype(BF16) for v in taps)
                band(bwd, 8 - t, c2, c1, c0)
            return carry

        lax.fori_loop(0, TAPS, body, 0)

    loads[2].wait()
    build(k1, w1, None)
    loads[3].wait()
    build(k2, w2, w2b)
    loads[4].wait()
    build(kc, wc, wcb)
    for padded in (xv, xh, xs, xp, xc):
        rows, tail = padded.shape[2], padded.shape[3] - PAD
        padded[:, :, :, 0:PAD] = jnp.zeros((3, padded.shape[1], rows, PAD), padded.dtype)
        padded[:, :, :, tail:] = jnp.zeros((3, padded.shape[1], rows, PAD), padded.dtype)
    part_sc[28:32] = jnp.zeros((4, 64, 128), BF16)
    part_f[28:32] = jnp.zeros((4, 32, 128), BF16)

    await_rims(0, True)
    unpack_rims(0)
    assemble_fine(0, xv)
    assemble_coarse(0, xc)

    first = ungroup(fine_conv(xv, w1), NI * NJ)
    sigma = sigmoid(first)
    slope1[...] = sigma * (1.0 + first * (1.0 - sigma))
    fine_st[...] = (first * sigma).astype(BF16).astype(F32).reshape(NI, NJ, LANES)
    pack(1, False)
    send_rims(1, False)

    def widen(value):
        wide = spread(value)
        top = wide.astype(BF16)
        rest = (wide - top.astype(F32)).astype(BF16)
        return dot(pool_matrix(128, 64, True), jnp.concatenate([top, rest], axis=0))

    pooled_slope = ungroup(coarse_conv(xc, wcb), CI * CJ)
    upstream[...] = (cot[...].reshape(NI * NJ, LANES).astype(F32) + widen(pooled_slope) * 0.125).astype(BF16).astype(F32)

    await_rims(1, False)
    unpack_rims(1)
    assemble_fine(1, xh)

    second = ungroup(fine_conv(xh, w2), NI * NJ)
    sigma = sigmoid(second)
    fine = (second * sigma).astype(BF16)
    fine_keep[...] = fine
    coarse_st[...] = (pool(fine) * 0.125).astype(BF16).astype(F32)
    second_slope = (upstream[...] * (sigma * (1.0 + second * (1.0 - sigma)))).astype(BF16).astype(F32)
    fine_st[...] = second_slope.reshape(NI, NJ, LANES)
    pack(2, True)
    send_rims(2, True)

    def grouped_t(value, groups):
        return jnp.concatenate([value[:, GROUP * g : GROUP * (g + 1)] for g in range(groups)], axis=0).T.astype(BF16)

    slopes_t[...] = grouped_t(fine_st[...].reshape(NI * NJ, LANES), 4)

    def store_second(n, value):
        part_sc[n] = value

    def store_coarse(n, value):
        part_sc[14 + n] = value

    def store_first(n, value):
        part_f[2 * n : 2 * n + 2] = value.reshape(2, 32, 128)

    grads(lambda t: fine_window(xh, t), slopes_t[...], store_second)

    await_rims(2, True)
    unpack_rims(2)
    assemble_coarse(2, xp)
    centre = xc[1, 1 : CI + 1, :, PAD : PAD + CLANES].reshape(CI * CJ, CLANES)
    grads(lambda t: coarse_window(xp, t), grouped_t(centre, 2), store_coarse)
    sum_sc[0]()
    assemble_fine(2, xs)

    hidden_slope = ungroup(fine_conv(xs, w2b), NI * NJ)
    first_slope = (hidden_slope * slope1[...]).astype(BF16).astype(F32)
    slopes_t[...] = grouped_t(first_slope, 4)
    sum_sc[1]()
    grads(lambda t: fine_window(xv, t), slopes_t[...], store_first)
    sum_f[0]()
    sum_sc[2]()

    coarse = ungroup(coarse_conv(xp, wc), CI * CJ).astype(BF16)
    wide = spread(coarse.astype(F32)).astype(BF16)
    repeated = dot(pool_matrix(128, 32, True), wide)
    field[...] = (fine_keep[...].astype(F32) + repeated).astype(BF16).reshape(NI, NJ, LANES)

    sum_f[1]()
    sum_sc[3]()
    sum_f[2]()
    sum_sc[4]()
    sum_f[3]()
    sum_f[4]()
    sum_sc[5](out_sc)
    sum_f[5](out_f)
    for stage in range(3):
        for there, _, copy in rim_copies(stage, stage != 1):
            pl.when(there)(copy.wait_send)


def unpack_kernel(field_in, sc, f, field, first_grad, second_grad, coarse_grad):
    field[...] = field_in[...]

    def place(read, out):
        for t in range(TAPS):
            block = read(t).astype(F32).T
            out[3 * t] = block[0:64]
            out[3 * t + 1] = block[64:128]
        for u in range(5):
            block = read(TAPS + u).astype(F32).T
            out[6 * u + 2] = block[0:64]
            if u < 4:
                out[6 * u + 5] = block[64:128]

    place(lambda n: sc[n], second_grad)
    place(lambda n: sc[14 + n], coarse_grad)
    place(lambda n: f[2 * n : 2 * n + 2].reshape(64, 128), first_grad)


def per_device(volume, cotangent, first_kernel, second_kernel, coarse_kernel):
    in_vmem = pl.BlockSpec(memory_space=pltpu.VMEM)
    dma = pltpu.SemaphoreType.DMA

    def sum_buffers(rows):
        return [
            pltpu.VMEM((32, rows, 128), BF16), pltpu.VMEM((16, rows, 128), BF16), pltpu.VMEM((16, rows, 128), BF16),
            pltpu.VMEM((15, rows, 128), BF16), pltpu.VMEM((8, rows, 128), BF16), pltpu.VMEM((32, rows, 128), BF16),
        ]

    sc_bufs, f_bufs = sum_buffers(64), sum_buffers(32)
    mixed = [b for pair in zip(sc_bufs, f_bufs) for b in pair]
    scratch = [
        pltpu.VMEM((NI, NJ, LANES), F32),
        pltpu.VMEM((CI, CJ, CLANES), F32),
        pltpu.VMEM((3, NI + 2, NJ, LANES + 2 * PAD), BF16),
        pltpu.VMEM((3, NI + 2, NJ, LANES + 2 * PAD), BF16),
        pltpu.VMEM((3, NI + 2, NJ, LANES + 2 * PAD), BF16),
        pltpu.VMEM((3, CI + 2, CJ, CLANES + 2 * PAD), F32),
        pltpu.VMEM((3, CI + 2, CJ, CLANES + 2 * PAD), F32),
        pltpu.VMEM((NI * NJ, LANES), F32),
        pltpu.VMEM((NI * NJ, LANES), F32),
        pltpu.VMEM((NI * NJ, LANES), BF16),
        pltpu.VMEM((GROUP, 4 * NI * NJ), BF16),
        pltpu.VMEM((4 * NI * NJ, GROUP), F32),
        pltpu.VMEM((TAPS, WINDOW, GROUP), BF16),
        pltpu.VMEM((TAPS, WINDOW, GROUP), BF16),
        pltpu.VMEM((TAPS, WINDOW, GROUP), BF16),
        pltpu.VMEM((TAPS, WINDOW, GROUP), BF16),
        pltpu.VMEM((TAPS, WINDOW, GROUP), BF16),
        pltpu.VMEM((3, 2, 16, 1280), BF16), pltpu.VMEM((3, 2, 16, 1280), BF16),
        pltpu.VMEM((3, 2, 16, 640), BF16), pltpu.VMEM((3, 2, 16, 640), BF16),
        pltpu.VMEM((3, 4, 16, 128), BF16), pltpu.VMEM((3, 4, 16, 128), BF16),
        pltpu.VMEM((16, 640), F32), pltpu.VMEM((2, 16, 640), F32),
        pltpu.VMEM((16, 128), F32), pltpu.VMEM((4, 16, 128), F32),
        *mixed,
        pltpu.VMEM((TAPS, 64, 128), F32),
        dma((3, 2)), dma((3, 2)), dma((3, 2)), dma((3, 2)), dma((3, 4)), dma((3, 4)),
        dma((39,)), dma((39,)), dma((39,)), dma((39,)), dma((5,)),
        pltpu.VMEM(volume.shape[1:], BF16), pltpu.VMEM(volume.shape[1:], BF16),
        *[pltpu.VMEM((27, 64, 64), BF16)] * 3,
    ]
    block = volume.shape[1:]
    taps = (27, 64, 64)
    field, sc, f = pl.pallas_call(
        kernel,
        out_shape=(
            jax.ShapeDtypeStruct(block, BF16),
            jax.ShapeDtypeStruct((32, 64, 128), BF16),
            jax.ShapeDtypeStruct((32, 32, 128), BF16),
        ),
        in_specs=[pl.BlockSpec(memory_space=pltpu.HBM)] * 5,
        out_specs=(in_vmem,) * 3,
        scratch_shapes=scratch,
        compiler_params=pltpu.CompilerParams(
            collective_id=0, has_side_effects=True, vmem_limit_bytes=48 * 1024 * 1024
        ),
        name="block",
    )(volume[0], cotangent[0], first_kernel.reshape(taps), second_kernel.reshape(taps), coarse_kernel.reshape(taps))
    field, first_grad, second_grad, coarse_grad = pl.pallas_call(
        unpack_kernel,
        out_shape=(jax.ShapeDtypeStruct(block, BF16),) + (jax.ShapeDtypeStruct(taps, F32),) * 3,
        in_specs=[in_vmem] * 3,
        out_specs=(in_vmem,) * 4,
        compiler_params=pltpu.CompilerParams(vmem_limit_bytes=32 * 1024 * 1024),
        name="unpack",
    )(field, sc, f)
    kernel_shape = first_kernel.shape
    return (
        field[None],
        first_grad.reshape(kernel_shape),
        second_grad.reshape(kernel_shape),
        coarse_grad.reshape(kernel_shape),
    )


def solution(mesh):
    in_specs = (P("dp", "gx", "gy", None), P("dp", "gx", "gy", None), P(), P(), P())
    out_specs = (P("dp", "gx", "gy", None), P(), P(), P())
    return jax.shard_map(
        per_device, mesh=mesh, in_specs=in_specs, out_specs=out_specs, check_vma=False
    )
```

```python
import jax
import jax.numpy as jnp
from jax import lax
from jax.experimental import pallas as pl
from jax.experimental.pallas import tpu as pltpu
from jax.sharding import PartitionSpec as P

MESH = pl.DeviceIdType.MESH
F32 = jnp.float32
BF16 = jnp.bfloat16

NI, NJ, LANES = 8, 16, 1024
CI, CJ, CLANES = 4, 8, 512
PAD = 128
GROUP = 256
WINDOW = 512
TAPS = 9


def dot(a, b, dims=((1,), (0,))):
    return lax.dot_general(a, b, (dims, ((), ())), preferred_element_type=F32)


def sigmoid(v):
    return 1.0 / (1.0 + jnp.exp(-v))


def kernel(
    vol_in, cot_in, k1_in, k2_in, kc_in,
    field, out_sc, out_f,
    fine_st, coarse_st, xv, xh, xs, xp, xc, slope1, upstream, fine_keep, slopes_t, acc,
    w1, w2, w2b, wc, wcb,
    s_e, r_e, s_n, r_n, s_c, r_c, col, colr, cor, corr,
    part_sc, part_f, in1_sc, in1_f, b2_sc, b2_f, in2_sc, in2_f, in3_sc, in3_f, res_sc, res_f, half,
    se_sem, re_sem, sn_sem, rn_sem, sc_sem, rc_sem,
    s_sc, g_sc, s_f, g_f, in_sem,
    vol, cot, k1, k2, kc, field_st, out_sem,
):
    loads = [
        pltpu.make_async_copy(src, dst, in_sem.at[n])
        for n, (src, dst) in enumerate(((vol_in, vol), (cot_in, cot), (k1_in, k1), (k2_in, k2), (kc_in, kc)))
    ]
    for load in loads:
        load.start()

    gx, gy, dp = lax.axis_index("gx"), lax.axis_index("gy"), lax.axis_index("dp")
    x_at, z_hi = lax.div(gy, 2), lax.rem(gy, 2)
    z_lo, core = lax.div(gx, 2), lax.rem(gx, 2)
    w_at = x_at * 4 + dp
    z_at = z_hi * 4 + z_lo

    def side(at, step):
        return lax.rem(at + step + 8, 8)

    def near(di, dj):
        return {"gx": side(gx, di), "gy": side(gy, dj)}

    def w_peer(r):
        x, y = lax.rem(x_at + r // 4, 4), lax.rem(dp + r % 4, 4)
        return x * 4 + y, {"gy": x * 2 + z_hi, "dp": y}

    other_core = {"gx": z_lo * 2 + 1 - core}

    def z_peer(r):
        z = lax.rem(z_at + r, 8)
        return z, {"gx": lax.rem(z, 4) * 2 + core, "gy": x_at * 2 + lax.div(z, 4)}

    steps = (-1, 1)
    barrier = pltpu.get_barrier_semaphore()
    partners = [near(s, 0) for s in steps] + [near(0, s) for s in steps]
    partners += [near(s, t) for s in steps for t in steps]
    partners += [other_core] + [w_peer(r)[1] for r in range(1, 16)] + [z_peer(r)[1] for r in range(1, 8)]
    for partner in partners:
        pl.semaphore_signal(barrier, inc=1, device_id=partner, device_id_type=MESH)

    def pack(stage, with_coarse):
        for e in range(2):
            i, ci = e * (NI - 1), e * (CI - 1)
            s_e[stage, e, :, 0:LANES] = fine_st[i].astype(BF16)
            if with_coarse:
                row = coarse_st[ci]
                s_e[stage, e, :, LANES:] = jnp.concatenate([row[:, :256], row[:, 256:]], axis=0).astype(BF16)
        for n in range(2):
            j, cj = n * (NJ - 1), n * (CJ - 1)
            for i in range(NI):
                col[i : i + 1, 0:512] = fine_st[i, j : j + 1, 0:512]
                col[NI + i : NI + i + 1, 0:512] = fine_st[i, j : j + 1, 512:1024]
            if with_coarse:
                for i in range(CI):
                    for k in range(4):
                        col[4 * k + i : 4 * k + i + 1, 512:640] = coarse_st[i, cj : cj + 1, 128 * k : 128 * k + 128]
            s_n[stage, n] = col[...].astype(BF16)
        for e in range(2):
            for n in range(2):
                i, j = e * (NI - 1), n * (NJ - 1)
                for k in range(8):
                    cor[k : k + 1] = fine_st[i, j : j + 1, 128 * k : 128 * k + 128]
                if with_coarse:
                    for k in range(4):
                        cor[8 + k : 9 + k] = coarse_st[e * (CI - 1), n * (CJ - 1) : n * (CJ - 1) + 1, 128 * k : 128 * k + 128]
                s_c[stage, 2 * e + n] = cor[...].astype(BF16)

    gx_low, gx_high, gy_low, gy_high = gx > 0, gx < 7, gy > 0, gy < 7
    to_x, to_y = (gx_low, gx_high), (gy_low, gy_high)

    def rim_copies(stage, with_coarse):
        wide_e, wide_n = (1280, 640) if with_coarse else (1024, 512)
        copies = []
        for n in range(2):
            copies.append((to_y[n], to_y[1 - n], pltpu.make_async_remote_copy(
                s_n.at[stage, n, :, pl.ds(0, wide_n)], r_n.at[stage, n, :, pl.ds(0, wide_n)],
                sn_sem.at[stage, n], rn_sem.at[stage, n], device_id=near(0, steps[n]), device_id_type=MESH)))
        for e in range(2):
            for n in range(2):
                c = 2 * e + n
                copies.append((to_x[e] & to_y[n], to_x[1 - e] & to_y[1 - n], pltpu.make_async_remote_copy(
                    s_c.at[stage, c], r_c.at[stage, c],
                    sc_sem.at[stage, c], rc_sem.at[stage, c], device_id=near(steps[e], steps[n]), device_id_type=MESH)))
        for e in range(2):
            copies.append((to_x[e], to_x[1 - e], pltpu.make_async_remote_copy(
                s_e.at[stage, e, :, pl.ds(0, wide_e)], r_e.at[stage, e, :, pl.ds(0, wide_e)],
                se_sem.at[stage, e], re_sem.at[stage, e], device_id=near(steps[e], 0), device_id_type=MESH)))
        return copies

    def send_rims(stage, with_coarse):
        for there, _, copy in rim_copies(stage, with_coarse):
            pl.when(there)(copy.start)

    def await_rims(stage, with_coarse):
        for _, there, copy in rim_copies(stage, with_coarse):
            pl.when(there)(copy.wait_recv)

    def place(dst, index, value, low, high, rows):
        at = lax.broadcasted_iota(jnp.int32, value.shape, 0)
        dst[0, index, :, PAD : PAD + value.shape[1]] = jnp.where(
            at == 0, jnp.broadcast_to(low, value.shape), pltpu.roll(value, 1, 0)).astype(dst.dtype)
        dst[1, index, :, PAD : PAD + value.shape[1]] = value.astype(dst.dtype)
        dst[2, index, :, PAD : PAD + value.shape[1]] = jnp.where(
            at == rows - 1, jnp.broadcast_to(high, value.shape), pltpu.roll(value, rows - 1, 0)).astype(dst.dtype)

    def keep(here, value):
        return jnp.where(here, value, 0.0)

    def unpack_rims(stage):
        for n in range(2):
            colr[n] = r_n[stage, n].astype(F32)
        for c in range(4):
            corr[c] = r_c[stage, c].astype(F32)

    def corner(c, first, count):
        return jnp.concatenate([corr[c, first + k : first + k + 1, :] for k in range(count)], axis=1)

    def assemble_fine(stage, dst):
        def body(i, carry):
            low = jnp.concatenate([colr[1, pl.ds(i, 1), 0:512], colr[1, pl.ds(i + NI, 1), 0:512]], axis=1)
            high = jnp.concatenate([colr[0, pl.ds(i, 1), 0:512], colr[0, pl.ds(i + NI, 1), 0:512]], axis=1)
            place(dst, i + 1, fine_st[i], keep(gy_low, low), keep(gy_high, high), NJ)
            return carry

        lax.fori_loop(0, NI, body, 0)
        for e, index, here in ((1, 0, gx_low), (0, NI + 1, gx_high)):
            value = keep(here, r_e[stage, e, :, 0:LANES].astype(F32))
            low = keep(here & gy_low, corner(2 * e + 1, 0, 8))
            high = keep(here & gy_high, corner(2 * e, 0, 8))
            place(dst, index, value, low, high, NJ)

    def assemble_coarse(stage, dst):
        for i in range(CI):
            low = jnp.concatenate([colr[1, 4 * k + i : 4 * k + i + 1, 512:640] for k in range(4)], axis=1)
            high = jnp.concatenate([colr[0, 4 * k + i : 4 * k + i + 1, 512:640] for k in range(4)], axis=1)
            place(dst, i + 1, coarse_st[i], keep(gy_low, low), keep(gy_high, high), CJ)
        for e, index, here in ((1, 0, gx_low), (0, CI + 1, gx_high)):
            row = r_e[stage, e, :, LANES:].astype(F32)
            value = keep(here, jnp.concatenate([row[:CJ], row[CJ:]], axis=1))
            low = keep(here & gy_low, corner(2 * e + 1, 8, 4))
            high = keep(here & gy_high, corner(2 * e, 8, 4))
            place(dst, index, value, low, high, CJ)

    def fine_window(src, t):
        a, b = t // 3, t % 3
        return jnp.concatenate(
            [src[b, a : a + NI, :, GROUP * g : GROUP * g + WINDOW].reshape(NI * NJ, WINDOW) for g in range(4)], axis=0)

    def coarse_window(src, t):
        a, b = t // 3, t % 3
        return jnp.concatenate(
            [src[b, a : a + CI, :, GROUP * g : GROUP * g + WINDOW].reshape(CI * CJ, WINDOW) for g in range(2)],
            axis=0).astype(BF16)

    def fine_conv(src, weights):
        total = dot(fine_window(src, 0), weights[0])
        for t in range(1, TAPS):
            total = total + dot(fine_window(src, t), weights[t])
        return total

    def coarse_conv(src, weights):
        total = dot(coarse_window(src, 0), weights[0])
        for t in range(1, TAPS):
            total = total + dot(coarse_window(src, t), weights[t])
        return total

    def grads(window, slopes, store):
        for t in range(TAPS):
            g = dot(slopes, window(t))
            even = g[0:64, 0:384] + g[128:192, 128:512]
            odd = g[64:128, 128:384] + g[192:256, 256:512]
            shifted = jnp.concatenate([even[:, 64:192], even[:, 192:320]], axis=1)
            total = odd + shifted
            store(t, total[:, 0:128].astype(BF16))
            half[t] = total[:, 128:256]
        lane = lax.broadcasted_iota(jnp.int32, (64, 128), 1)
        for u in range(5):
            left = half[2 * u]
            right = pltpu.roll(half[2 * u + 1], 64, 1) if u < 4 else jnp.zeros_like(left)
            store(TAPS + u, jnp.where(lane < 64, left, right).astype(BF16))

    def pool_matrix(rows, columns, flip):
        r = lax.broadcasted_iota(jnp.int32, (rows, columns), 1 if flip else 0)
        s = lax.broadcasted_iota(jnp.int32, (rows, columns), 0 if flip else 1)
        r = r & 31
        return jnp.where(r == (s >> 5) * 8 + ((s & 15) >> 1), 1.0, 0.0).astype(BF16)

    def pool(value):
        sums = dot(pool_matrix(32, 128, False), value)
        lane = lax.broadcasted_iota(jnp.int32, (32, 128), 1)
        tiles = []
        for k in range(4):
            pair = []
            for m in range(2):
                tile = sums[:, 256 * k + 128 * m : 256 * k + 128 * m + 128]
                pair.append(tile + pltpu.roll(tile, 64, 1))
            tiles.append(jnp.where(lane < 64, pair[0], pair[1]))
        return jnp.concatenate(tiles, axis=1).reshape(CI, CJ, CLANES)

    def spread(value):
        lane = lax.broadcasted_iota(jnp.int32, (32, 128), 1)
        tiles = []
        for k in range(4):
            tile = value[:, 128 * k : 128 * k + 128]
            turned = pltpu.roll(tile, 64, 1)
            tiles += [jnp.where(lane < 64, tile, turned), jnp.where(lane < 64, turned, tile)]
        return jnp.concatenate(tiles, axis=1)

    def ungroup(value, rows):
        return jnp.concatenate([value[rows * g : rows * (g + 1)] for g in range(value.shape[0] // rows)], axis=1)

    def make_sum(part, in1, b2, in2, in3, res, send, got):
        def c1(r):
            return pltpu.make_async_remote_copy(part.at[pl.ds((1 - core) * 16, 16)], in1, send.at[0], got.at[0],
                                                device_id=other_core, device_id_type=MESH)

        def c2(r):
            w, peer = w_peer(r)
            return pltpu.make_async_remote_copy(b2.at[w], in2.at[r - 1], send.at[r], got.at[r],
                                                device_id=peer, device_id_type=MESH)

        def c3(r):
            _, peer = z_peer(r)
            return pltpu.make_async_remote_copy(in3.at[z_at], in3.at[z_at], send.at[15 + r], got.at[15 + r],
                                                device_id=peer, device_id_type=MESH)

        mine = core * 16 + w_at

        def c4(r):
            _, peer = w_peer(r)
            return pltpu.make_async_remote_copy(res.at[mine], res.at[mine], send.at[22 + r], got.at[22 + r],
                                                device_id=peer, device_id_type=MESH)

        def c5(r):
            own = pl.ds(core * 16, 16)
            return pltpu.make_async_remote_copy(res.at[own], res.at[own], send.at[38], got.at[38],
                                                device_id=other_core, device_id_type=MESH)

        def start(make, count):
            for r in range(1, count):
                make(r).start()

        def finish(make, count):
            for r in range(1, count):
                make(r).wait_recv()

        def s1():
            start(c1, 2)

        def s2():
            finish(c1, 2)
            b2[...] = (part[pl.ds(core * 16, 16)].astype(F32) + in1[...].astype(F32)).astype(BF16)
            start(c2, 16)

        def s3():
            finish(c2, 16)
            total = b2[w_at].astype(F32)
            for r in range(15):
                total = total + in2[r].astype(F32)
            in3[z_at] = total.astype(BF16)
            start(c3, 8)

        def s4():
            finish(c3, 8)
            total = in3[0].astype(F32)
            for r in range(1, 8):
                total = total + in3[r].astype(F32)
            res[mine] = total.astype(BF16)
            start(c4, 16)

        def s5():
            finish(c4, 16)
            start(c5, 2)

        def s6():
            finish(c5, 2)

        def s7():
            for make, count in ((c1, 2), (c2, 16), (c3, 8), (c4, 16), (c5, 2)):
                for r in range(1, count):
                    make(r).wait_send()

        return s1, s2, s3, s4, s5, s6, s7

    sum_sc = make_sum(part_sc, in1_sc, b2_sc, in2_sc, in3_sc, res_sc, s_sc, g_sc)
    sum_f = make_sum(part_f, in1_f, b2_f, in2_f, in3_f, res_f, s_f, g_f)

    loads[0].wait()
    fine_st[...] = vol[...].astype(F32)
    loads[1].wait()
    coarse_slope = pool(cot[...].reshape(NI * NJ, LANES))
    coarse_st[...] = coarse_slope.astype(BF16).astype(F32)
    cor[...] = jnp.zeros_like(cor)
    pack(0, True)
    pl.semaphore_wait(barrier, len(partners))
    send_rims(0, True)

    def build(k, fwd, bwd):
        for w in (fwd, bwd):
            if w is not None:
                w[...] = jnp.zeros_like(w)

        def band(w, t, c0, c1, c2):
            zero = jnp.zeros_like(c0)
            pairs = ((c0, zero), (c1, c0), (c2, c1), (zero, c2))
            for m, tile in enumerate(jnp.concatenate(pair, axis=1) for pair in pairs):
                for pair in range(2):
                    row = 64 * (2 * pair + 1 + m)
                    w[t, row : row + 64, 128 * pair : 128 * pair + 128] = tile

        def body(t, carry):
            taps = [k[3 * t + c] for c in range(3)]
            band(fwd, t, *taps)
            if bwd is not None:
                c0, c1, c2 = (v.astype(F32).T.astype(BF16) for v in taps)
                band(bwd, 8 - t, c2, c1, c0)
            return carry

        lax.fori_loop(0, TAPS, body, 0)

    loads[2].wait()
    build(k1, w1, None)
    loads[3].wait()
    build(k2, w2, w2b)
    loads[4].wait()
    build(kc, wc, wcb)
    for padded in (xv, xh, xs, xp, xc):
        rows, tail = padded.shape[2], padded.shape[3] - PAD
        padded[:, :, :, 0:PAD] = jnp.zeros((3, padded.shape[1], rows, PAD), padded.dtype)
        padded[:, :, :, tail:] = jnp.zeros((3, padded.shape[1], rows, PAD), padded.dtype)
    part_sc[28:32] = jnp.zeros((4, 64, 128), BF16)
    part_f[28:32] = jnp.zeros((4, 32, 128), BF16)

    await_rims(0, True)
    unpack_rims(0)
    assemble_fine(0, xv)
    assemble_coarse(0, xc)

    first = ungroup(fine_conv(xv, w1), NI * NJ)
    sigma = sigmoid(first)
    slope1[...] = sigma * (1.0 + first * (1.0 - sigma))
    fine_st[...] = (first * sigma).astype(BF16).astype(F32).reshape(NI, NJ, LANES)
    pack(1, False)
    send_rims(1, False)

    def widen(value):
        wide = spread(value)
        top = wide.astype(BF16)
        rest = (wide - top.astype(F32)).astype(BF16)
        return dot(pool_matrix(128, 64, True), jnp.concatenate([top, rest], axis=0))

    pooled_slope = ungroup(coarse_conv(xc, wcb), CI * CJ)
    upstream[...] = (cot[...].reshape(NI * NJ, LANES).astype(F32) + widen(pooled_slope) * 0.125).astype(BF16).astype(F32)

    await_rims(1, False)
    unpack_rims(1)
    assemble_fine(1, xh)

    second = ungroup(fine_conv(xh, w2), NI * NJ)
    sigma = sigmoid(second)
    fine = (second * sigma).astype(BF16)
    fine_keep[...] = fine
    coarse_st[...] = (pool(fine) * 0.125).astype(BF16).astype(F32)
    second_slope = (upstream[...] * (sigma * (1.0 + second * (1.0 - sigma)))).astype(BF16).astype(F32)
    fine_st[...] = second_slope.reshape(NI, NJ, LANES)
    pack(2, True)
    send_rims(2, True)

    def grouped_t(value, groups):
        return jnp.concatenate([value[:, GROUP * g : GROUP * (g + 1)] for g in range(groups)], axis=0).T.astype(BF16)

    slopes_t[...] = grouped_t(fine_st[...].reshape(NI * NJ, LANES), 4)

    def store_second(n, value):
        part_sc[n] = value

    def store_coarse(n, value):
        part_sc[14 + n] = value

    def store_first(n, value):
        part_f[2 * n : 2 * n + 2] = value.reshape(2, 32, 128)

    grads(lambda t: fine_window(xh, t), slopes_t[...], store_second)
    grads(lambda t: coarse_window(xc, t), grouped_t(coarse_st[...].reshape(CI * CJ, CLANES), 2), store_coarse)
    sum_sc[0]()

    await_rims(2, True)
    unpack_rims(2)
    sum_sc[1]()
    assemble_fine(2, xs)

    hidden_slope = ungroup(fine_conv(xs, w2b), NI * NJ)
    first_slope = (hidden_slope * slope1[...]).astype(BF16).astype(F32)
    slopes_t[...] = grouped_t(first_slope, 4)
    grads(lambda t: fine_window(xv, t), slopes_t[...], store_first)
    sum_f[0]()
    sum_sc[2]()
    sum_f[1]()

    assemble_coarse(2, xp)
    coarse = ungroup(coarse_conv(xp, wc), CI * CJ).astype(BF16)
    wide = spread(coarse.astype(F32)).astype(BF16)
    repeated = dot(pool_matrix(128, 32, True), wide)
    field_st[...] = (fine_keep[...].astype(F32) + repeated).astype(BF16).reshape(NI, NJ, LANES)
    stores = [
        pltpu.make_async_copy(src, dst, out_sem.at[n])
        for n, (src, dst) in enumerate(((field_st, field), (res_sc, out_sc), (res_f, out_f)))
    ]
    stores[0].start()

    sum_sc[3]()
    sum_f[2]()
    sum_sc[4]()
    sum_f[3]()
    sum_sc[5]()
    stores[1].start()
    sum_f[4]()
    sum_f[5]()
    stores[2].start()
    sum_sc[6]()
    sum_f[6]()
    for stage in range(3):
        for there, _, copy in rim_copies(stage, stage != 1):
            pl.when(there)(copy.wait_send)
    for store in stores:
        store.wait()


def unpack_kernel(
    field_in, sc_in, f_in, field, first_out, second_out, coarse_out,
    sc, f, held, first_grad, second_grad, coarse_grad, sem,
):
    copies = [
        pltpu.make_async_copy(src, dst, sem.at[n])
        for n, (src, dst) in enumerate((
            (sc_in, sc), (f_in, f), (field_in, held), (held, field),
            (second_grad, second_out), (coarse_grad, coarse_out), (first_grad, first_out),
        ))
    ]
    for copy in copies[:3]:
        copy.start()

    def place(read, out):
        for t in range(TAPS):
            block = read(t).astype(F32).T
            out[3 * t] = block[0:64]
            out[3 * t + 1] = block[64:128]
        for u in range(5):
            block = read(TAPS + u).astype(F32).T
            out[6 * u + 2] = block[0:64]
            if u < 4:
                out[6 * u + 5] = block[64:128]

    copies[0].wait()
    place(lambda n: sc[n], second_grad)
    copies[4].start()
    copies[2].wait()
    copies[3].start()
    for t in range(TAPS):
        block = sc[14 + t].astype(F32)
        coarse_grad[26 - 3 * t] = block[:, 0:64]
        coarse_grad[25 - 3 * t] = block[:, 64:128]
    for u in range(5):
        block = sc[14 + TAPS + u].astype(F32)
        coarse_grad[24 - 6 * u] = block[:, 0:64]
        if u < 4:
            coarse_grad[21 - 6 * u] = block[:, 64:128]
    copies[5].start()
    copies[1].wait()
    place(lambda n: f[2 * n : 2 * n + 2].reshape(64, 128), first_grad)
    copies[6].start()
    for copy in copies[3:]:
        copy.wait()


def per_device(volume, cotangent, first_kernel, second_kernel, coarse_kernel):
    in_hbm = pl.BlockSpec(memory_space=pltpu.HBM)
    dma = pltpu.SemaphoreType.DMA

    def sum_buffers(rows):
        return [
            pltpu.VMEM((32, rows, 128), BF16), pltpu.VMEM((16, rows, 128), BF16), pltpu.VMEM((16, rows, 128), BF16),
            pltpu.VMEM((15, rows, 128), BF16), pltpu.VMEM((8, rows, 128), BF16), pltpu.VMEM((32, rows, 128), BF16),
        ]

    sc_bufs, f_bufs = sum_buffers(64), sum_buffers(32)
    mixed = [b for pair in zip(sc_bufs, f_bufs) for b in pair]
    scratch = [
        pltpu.VMEM((NI, NJ, LANES), F32),
        pltpu.VMEM((CI, CJ, CLANES), F32),
        pltpu.VMEM((3, NI + 2, NJ, LANES + 2 * PAD), BF16),
        pltpu.VMEM((3, NI + 2, NJ, LANES + 2 * PAD), BF16),
        pltpu.VMEM((3, NI + 2, NJ, LANES + 2 * PAD), BF16),
        pltpu.VMEM((3, CI + 2, CJ, CLANES + 2 * PAD), F32),
        pltpu.VMEM((3, CI + 2, CJ, CLANES + 2 * PAD), F32),
        pltpu.VMEM((NI * NJ, LANES), F32),
        pltpu.VMEM((NI * NJ, LANES), F32),
        pltpu.VMEM((NI * NJ, LANES), BF16),
        pltpu.VMEM((GROUP, 4 * NI * NJ), BF16),
        pltpu.VMEM((4 * NI * NJ, GROUP), F32),
        pltpu.VMEM((TAPS, WINDOW, GROUP), BF16),
        pltpu.VMEM((TAPS, WINDOW, GROUP), BF16),
        pltpu.VMEM((TAPS, WINDOW, GROUP), BF16),
        pltpu.VMEM((TAPS, WINDOW, GROUP), BF16),
        pltpu.VMEM((TAPS, WINDOW, GROUP), BF16),
        pltpu.VMEM((3, 2, 16, 1280), BF16), pltpu.VMEM((3, 2, 16, 1280), BF16),
        pltpu.VMEM((3, 2, 16, 640), BF16), pltpu.VMEM((3, 2, 16, 640), BF16),
        pltpu.VMEM((3, 4, 16, 128), BF16), pltpu.VMEM((3, 4, 16, 128), BF16),
        pltpu.VMEM((16, 640), F32), pltpu.VMEM((2, 16, 640), F32),
        pltpu.VMEM((16, 128), F32), pltpu.VMEM((4, 16, 128), F32),
        *mixed,
        pltpu.VMEM((TAPS, 64, 128), F32),
        dma((3, 2)), dma((3, 2)), dma((3, 2)), dma((3, 2)), dma((3, 4)), dma((3, 4)),
        dma((39,)), dma((39,)), dma((39,)), dma((39,)), dma((5,)),
        pltpu.VMEM(volume.shape[1:], BF16), pltpu.VMEM(volume.shape[1:], BF16),
        *[pltpu.VMEM((27, 64, 64), BF16)] * 3,
        pltpu.VMEM(volume.shape[1:], BF16), dma((3,)),
    ]
    block = volume.shape[1:]
    taps = (27, 64, 64)
    field, sc, f = pl.pallas_call(
        kernel,
        out_shape=(
            jax.ShapeDtypeStruct(block, BF16),
            jax.ShapeDtypeStruct((32, 64, 128), BF16),
            jax.ShapeDtypeStruct((32, 32, 128), BF16),
        ),
        in_specs=[in_hbm] * 5,
        out_specs=(in_hbm,) * 3,
        scratch_shapes=scratch,
        compiler_params=pltpu.CompilerParams(
            collective_id=0, has_side_effects=True, vmem_limit_bytes=63 * 1024 * 1024
        ),
        name="block",
    )(volume[0], cotangent[0], first_kernel.reshape(taps), second_kernel.reshape(taps), coarse_kernel.reshape(taps))
    field, first_grad, second_grad, coarse_grad = pl.pallas_call(
        unpack_kernel,
        out_shape=(jax.ShapeDtypeStruct(block, BF16),) + (jax.ShapeDtypeStruct(taps, F32),) * 3,
        in_specs=[in_hbm] * 3,
        out_specs=(in_hbm,) * 4,
        scratch_shapes=[
            pltpu.VMEM((32, 64, 128), BF16), pltpu.VMEM((32, 32, 128), BF16), pltpu.VMEM(block, BF16),
            *[pltpu.VMEM(taps, F32)] * 3, dma((7,)),
        ],
        compiler_params=pltpu.CompilerParams(vmem_limit_bytes=63 * 1024 * 1024),
        name="unpack",
    )(field, sc, f)
    kernel_shape = first_kernel.shape
    return (
        field[None],
        first_grad.reshape(kernel_shape),
        second_grad.reshape(kernel_shape),
        coarse_grad.reshape(kernel_shape),
    )


def solution(mesh):
    in_specs = (P("dp", "gx", "gy", None), P("dp", "gx", "gy", None), P(), P(), P())
    out_specs = (P("dp", "gx", "gy", None), P(), P(), P())
    return jax.shard_map(
        per_device, mesh=mesh, in_specs=in_specs, out_specs=out_specs, check_vma=False
    )
```

```python
import jax
import jax.numpy as jnp
from jax import lax
from jax.experimental import pallas as pl
from jax.experimental.pallas import tpu as pltpu
from jax.sharding import PartitionSpec as P

MESH = pl.DeviceIdType.MESH
F32 = jnp.float32
BF16 = jnp.bfloat16

NI, NJ, LANES = 8, 16, 1024
CI, CJ, CLANES = 4, 8, 512
PAD = 128
GROUP = 256
WINDOW = 512
TAPS = 9
LOOPED = ('c2', 'g1')


def dot(a, b, dims=((1,), (0,))):
    return lax.dot_general(a, b, (dims, ((), ())), preferred_element_type=F32)


def sigmoid(v):
    return 1.0 / (1.0 + jnp.exp(-v))


def kernel(
    vol_in, cot_in, k1_in, k2_in, kc_in,
    field, out_sc, out_f,
    fine_st, coarse_st, xv, xh, xs, xp, xc, slope1, upstream, fine_keep, slopes_t, acc,
    w1, w2, w2b, wc, wcb,
    s_e, r_e, s_n, r_n, s_c, r_c, col, colr, cor, corr,
    part_sc, part_f, in1_sc, in1_f, b2_sc, b2_f, in2_sc, in2_f, in3_sc, in3_f, res_sc, res_f, half,
    se_sem, re_sem, sn_sem, rn_sem, sc_sem, rc_sem,
    s_sc, g_sc, s_f, g_f, in_sem,
    vol, cot, k1, k2, kc,
    pooled_t, hid, xvc, colw, corw, colv, corv, colx, sv_n, rv_n, sv_c, rv_c, rv_e,
):
    loads = [
        pltpu.make_async_copy(src, dst, in_sem.at[n])
        for n, (src, dst) in enumerate(((vol_in, vol), (cot_in, cot), (k1_in, k1), (k2_in, k2), (kc_in, kc)))
    ]
    for load in loads:
        load.start()

    gx, gy, dp = lax.axis_index("gx"), lax.axis_index("gy"), lax.axis_index("dp")
    x_at, z_hi = lax.div(gy, 2), lax.rem(gy, 2)
    z_lo, core = lax.div(gx, 2), lax.rem(gx, 2)
    w_at = x_at * 4 + dp
    z_at = z_hi * 4 + z_lo

    def side(at, step):
        return lax.rem(at + step + 8, 8)

    def near(di, dj):
        return {"gx": side(gx, di), "gy": side(gy, dj)}

    def w_peer(r):
        x, y = lax.rem(x_at + r // 4, 4), lax.rem(dp + r % 4, 4)
        return x * 4 + y, {"gy": x * 2 + z_hi, "dp": y}

    other_core = {"gx": z_lo * 2 + 1 - core}

    def z_peer(r):
        z = lax.rem(z_at + r, 8)
        return z, {"gx": lax.rem(z, 4) * 2 + core, "gy": x_at * 2 + lax.div(z, 4)}

    steps = (-1, 1)
    barrier = pltpu.get_barrier_semaphore()
    partners = [near(s, 0) for s in steps] + [near(0, s) for s in steps]
    partners += [near(s, t) for s in steps for t in steps]
    partners += [other_core] + [w_peer(r)[1] for r in range(1, 16)] + [z_peer(r)[1] for r in range(1, 8)]
    for partner in partners:
        pl.semaphore_signal(barrier, inc=1, device_id=partner, device_id_type=MESH)

    def pack(stage, with_fine):
        for e in range(2):
            row = coarse_st[e * (CI - 1)]
            if with_fine:
                s_e[stage, e, :, 0:LANES] = fine_st[e * (NI - 1)].astype(BF16)
            s_e[stage, e, :, LANES:] = jnp.concatenate([row[:, :256], row[:, 256:]], axis=0).astype(BF16)
        for n in range(2):
            j, cj = n * (NJ - 1), n * (CJ - 1)
            if with_fine:
                for i in range(NI):
                    col[i : i + 1, 0:512] = fine_st[i, j : j + 1, 0:512]
                    col[NI + i : NI + i + 1, 0:512] = fine_st[i, j : j + 1, 512:1024]
            for i in range(CI):
                for k in range(4):
                    col[4 * k + i : 4 * k + i + 1, 512:640] = coarse_st[i, cj : cj + 1, 128 * k : 128 * k + 128]
            s_n[stage, n] = col[...].astype(BF16)
        for e in range(2):
            for n in range(2):
                i, j, cj = e * (NI - 1), n * (NJ - 1), n * (CJ - 1)
                if with_fine:
                    for k in range(8):
                        cor[k : k + 1] = fine_st[i, j : j + 1, 128 * k : 128 * k + 128]
                for k in range(4):
                    cor[8 + k : 9 + k] = coarse_st[e * (CI - 1), cj : cj + 1, 128 * k : 128 * k + 128]
                s_c[stage, 2 * e + n] = cor[...].astype(BF16)

    def pack_volume():
        for n in range(2):
            for i in range(NI):
                for m in range(2):
                    j = n * (NJ - 2) + m
                    colw[NI * m + i : NI * m + i + 1, :] = fine_st[i, j : j + 1, :]
            sv_n[n] = colw[...].astype(BF16)
        for e in range(2):
            for n in range(2):
                for cell in range(4):
                    i, j = e * (NI - 2) + cell // 2, n * (NJ - 2) + cell % 2
                    for k in range(4):
                        corw[4 * k + cell : 4 * k + cell + 1, :] = fine_st[i, j : j + 1, 256 * k : 256 * k + 256]
                sv_c[2 * e + n] = corw[...].astype(BF16)

    gx_low, gx_high, gy_low, gy_high = gx > 0, gx < 7, gy > 0, gy < 7
    to_x, to_y = (gx_low, gx_high), (gy_low, gy_high)

    def to_sides(n_src, n_dst, n_sems, c_src, c_dst, c_sems, e_src, e_dst, e_sems):
        copies = []
        for n in range(2):
            copies.append((to_y[n], to_y[1 - n], pltpu.make_async_remote_copy(
                n_src(n), n_dst(n), n_sems[0].at[n], n_sems[1].at[n],
                device_id=near(0, steps[n]), device_id_type=MESH)))
        for e in range(2):
            for n in range(2):
                c = 2 * e + n
                copies.append((to_x[e] & to_y[n], to_x[1 - e] & to_y[1 - n], pltpu.make_async_remote_copy(
                    c_src(c), c_dst(c), c_sems[0].at[c], c_sems[1].at[c],
                    device_id=near(steps[e], steps[n]), device_id_type=MESH)))
        for e in range(2):
            copies.append((to_x[e], to_x[1 - e], pltpu.make_async_remote_copy(
                e_src(e), e_dst(e), e_sems[0].at[e], e_sems[1].at[e],
                device_id=near(steps[e], 0), device_id_type=MESH)))
        return copies

    def rim_copies(stage, with_fine):
        lanes_e, lanes_n = (pl.ds(0, 1280), pl.ds(0, 640)) if with_fine else (pl.ds(1024, 256), pl.ds(512, 128))
        return to_sides(
            lambda n: s_n.at[stage, n, :, lanes_n], lambda n: r_n.at[stage, n, :, lanes_n], (sn_sem.at[stage], rn_sem.at[stage]),
            lambda c: s_c.at[stage, c], lambda c: r_c.at[stage, c], (sc_sem.at[stage], rc_sem.at[stage]),
            lambda e: s_e.at[stage, e, :, lanes_e], lambda e: r_e.at[stage, e, :, lanes_e], (se_sem.at[stage], re_sem.at[stage]))

    def volume_copies():
        return to_sides(
            lambda n: sv_n.at[n], lambda n: rv_n.at[n], (sn_sem.at[2], rn_sem.at[2]),
            lambda c: sv_c.at[c], lambda c: rv_c.at[c], (sc_sem.at[2], rc_sem.at[2]),
            lambda e: vol.at[pl.ds(e * (NI - 2), 2)], lambda e: rv_e.at[e], (se_sem.at[2], re_sem.at[2]))

    def send(copies):
        for there, _, copy in copies:
            pl.when(there)(copy.start)

    def receive(copies):
        for _, there, copy in copies:
            pl.when(there)(copy.wait_recv)

    def place(dst, index, value, low, high, rows):
        at = lax.broadcasted_iota(jnp.int32, value.shape, 0)
        dst[0, index, :, PAD : PAD + value.shape[1]] = jnp.where(
            at == 0, jnp.broadcast_to(low, value.shape), pltpu.roll(value, 1, 0)).astype(dst.dtype)
        dst[1, index, :, PAD : PAD + value.shape[1]] = value.astype(dst.dtype)
        dst[2, index, :, PAD : PAD + value.shape[1]] = jnp.where(
            at == rows - 1, jnp.broadcast_to(high, value.shape), pltpu.roll(value, rows - 1, 0)).astype(dst.dtype)

    def keep(here, value):
        return jnp.where(here, value, 0.0)

    def unpack_rims(stage):
        for n in range(2):
            colr[n] = r_n[stage, n].astype(F32)
        for c in range(4):
            corr[c] = r_c[stage, c].astype(F32)

    def corner(c, first, count):
        return jnp.concatenate([corr[c, first + k : first + k + 1, :] for k in range(count)], axis=1)

    def assemble_fine(stage, dst):
        def body(i, carry):
            low = jnp.concatenate([colr[1, pl.ds(i, 1), 0:512], colr[1, pl.ds(i + NI, 1), 0:512]], axis=1)
            high = jnp.concatenate([colr[0, pl.ds(i, 1), 0:512], colr[0, pl.ds(i + NI, 1), 0:512]], axis=1)
            place(dst, i + 1, fine_st[i], keep(gy_low, low), keep(gy_high, high), NJ)
            return carry

        lax.fori_loop(0, NI, body, 0)
        for e, index, here in ((1, 0, gx_low), (0, NI + 1, gx_high)):
            value = keep(here, r_e[stage, e, :, 0:LANES].astype(F32))
            low = keep(here & gy_low, corner(2 * e + 1, 0, 8))
            high = keep(here & gy_high, corner(2 * e, 0, 8))
            place(dst, index, value, low, high, NJ)

    def assemble_volume():
        for n in range(2):
            colv[n] = rv_n[n].astype(F32)
        for c in range(4):
            corv[c] = rv_c[c].astype(F32)

        def body(i, carry):
            low, high = colv[1, pl.ds(i + NI, 1), :], colv[0, pl.ds(i, 1), :]
            place(xv, i + 2, fine_st[i], keep(gy_low, low), keep(gy_high, high), NJ)
            return carry

        lax.fori_loop(0, NI, body, 0)

        def cells(c, cell):
            return jnp.concatenate([corv[c, 4 * k + cell : 4 * k + cell + 1, :] for k in range(4)], axis=1)

        for m in range(2):
            colx[0, m, 2:10, :] = keep(gy_low, colv[1, NI * m : NI * m + NI, :])
            colx[1, 1 + m, 2:10, :] = keep(gy_high, colv[0, NI * m : NI * m + NI, :])
        for i in range(NI):
            colx[0, 2, i + 2 : i + 3, :] = fine_st[i, 0:1, :]
            colx[1, 0, i + 2 : i + 3, :] = fine_st[i, NJ - 1 : NJ, :]
        for e, first_row, here in ((1, 0, gx_low), (0, NI + 2, gx_high)):
            for m in range(2):
                at = first_row + m
                value = keep(here, rv_e[e, m].astype(F32))
                low = [keep(here & gy_low, cells(2 * e + 1, 2 * m + j)) for j in range(2)]
                high = [keep(here & gy_high, cells(2 * e, 2 * m + j)) for j in range(2)]
                place(xv, at, value, low[1], high[0], NJ)
                for j in range(2):
                    colx[0, j, at : at + 1, :] = low[j]
                    colx[1, 1 + j, at : at + 1, :] = high[j]
                colx[0, 2, at : at + 1, :] = value[0:1]
                colx[1, 0, at : at + 1, :] = value[NJ - 1 : NJ]
        for a in range(3):
            for b in range(3):
                for m in range(2):
                    strip = colx[m, b]
                    strip = strip if a == 0 else pltpu.roll(strip, 16 - a, 0)
                    xvc[3 * a + b, 16 * m : 16 * m + 16, PAD : PAD + LANES] = strip.astype(BF16)

    def assemble_hidden():
        def body(at, carry):
            here = ((at > 0) | gx_low) & ((at < NI + 1) | gx_high)
            low, high = hid[NI + 2, pl.ds(at, 1), :], hid[NI + 3, pl.ds(at, 1), :]
            place(xh, at, keep(here, hid[at]), keep(here & gy_low, low), keep(here & gy_high, high), NJ)
            return carry

        lax.fori_loop(0, NI + 2, body, 0)

    def assemble_coarse(stage, dst):
        for i in range(CI):
            low = jnp.concatenate([colr[1, 4 * k + i : 4 * k + i + 1, 512:640] for k in range(4)], axis=1)
            high = jnp.concatenate([colr[0, 4 * k + i : 4 * k + i + 1, 512:640] for k in range(4)], axis=1)
            place(dst, i + 1, coarse_st[i], keep(gy_low, low), keep(gy_high, high), CJ)
        for e, index, here in ((1, 0, gx_low), (0, CI + 1, gx_high)):
            row = r_e[stage, e, :, LANES:].astype(F32)
            value = keep(here, jnp.concatenate([row[:CJ], row[CJ:]], axis=1))
            low = keep(here & gy_low, corner(2 * e + 1, 8, 4))
            high = keep(here & gy_high, corner(2 * e, 8, 4))
            place(dst, index, value, low, high, CJ)

    def wide_window(a, b):
        parts = []
        for g in range(4):
            lanes = slice(GROUP * g, GROUP * g + WINDOW)
            parts += [xv[b, pl.ds(a, NI + 2), :, lanes].reshape((NI + 2) * NJ, WINDOW), xvc[3 * a + b, :, lanes]]
        return jnp.concatenate(parts, axis=0)

    def fine_window(src, a, b):
        return jnp.concatenate(
            [src[b, pl.ds(a, NI), :, GROUP * g : GROUP * g + WINDOW].reshape(NI * NJ, WINDOW) for g in range(4)], axis=0)

    def coarse_window(src, a, b):
        return jnp.concatenate(
            [src[b, pl.ds(a, CI), :, GROUP * g : GROUP * g + WINDOW].reshape(CI * CJ, WINDOW) for g in range(2)],
            axis=0).astype(BF16)

    def three(body, looped):
        if looped:
            lax.fori_loop(0, 3, body, 0)
        else:
            for a in range(3):
                body(a, 0)

    def conv(window, weights, rows, looped):
        if not looped:
            total = dot(window(0, 0), weights[0])
            for t in range(1, TAPS):
                total = total + dot(window(t // 3, t % 3), weights[t])
            return total
        acc[0:rows] = jnp.zeros((rows, GROUP), F32)

        def body(a, carry):
            total = acc[0:rows]
            for b in range(3):
                total = total + dot(window(a, b), weights[3 * a + b])
            acc[0:rows] = total
            return carry

        lax.fori_loop(0, 3, body, 0)
        return acc[0:rows]

    def grads(window, slopes, store, looped):
        def body(a, carry):
            for b in range(3):
                g = dot(slopes[...], window(a, b))
                even = g[0:64, 0:384] + g[128:192, 128:512]
                odd = g[64:128, 128:384] + g[192:256, 256:512]
                shifted = jnp.concatenate([even[:, 64:192], even[:, 192:320]], axis=1)
                total = odd + shifted
                store(3 * a + b, total[:, 0:128].astype(BF16))
                half[3 * a + b] = total[:, 128:256]
            return carry

        three(body, looped)
        lane = lax.broadcasted_iota(jnp.int32, (64, 128), 1)
        for u in range(5):
            left = half[2 * u]
            right = pltpu.roll(half[2 * u + 1], 64, 1) if u < 4 else jnp.zeros_like(left)
            store(TAPS + u, jnp.where(lane < 64, left, right).astype(BF16))

    def pool_matrix(rows, columns, flip):
        r = lax.broadcasted_iota(jnp.int32, (rows, columns), 1 if flip else 0)
        s = lax.broadcasted_iota(jnp.int32, (rows, columns), 0 if flip else 1)
        r = r & 31
        return jnp.where(r == (s >> 5) * 8 + ((s & 15) >> 1), 1.0, 0.0).astype(BF16)

    def pool(value):
        sums = dot(pool_matrix(32, 128, False), value)
        lane = lax.broadcasted_iota(jnp.int32, (32, 128), 1)
        tiles = []
        for k in range(4):
            pair = []
            for m in range(2):
                tile = sums[:, 256 * k + 128 * m : 256 * k + 128 * m + 128]
                pair.append(tile + pltpu.roll(tile, 64, 1))
            tiles.append(jnp.where(lane < 64, pair[0], pair[1]))
        return jnp.concatenate(tiles, axis=1).reshape(CI, CJ, CLANES)

    def spread(value):
        lane = lax.broadcasted_iota(jnp.int32, (32, 128), 1)
        tiles = []
        for k in range(4):
            tile = value[:, 128 * k : 128 * k + 128]
            turned = pltpu.roll(tile, 64, 1)
            tiles += [jnp.where(lane < 64, tile, turned), jnp.where(lane < 64, turned, tile)]
        return jnp.concatenate(tiles, axis=1)

    def ungroup(value, rows):
        return jnp.concatenate([value[rows * g : rows * (g + 1)] for g in range(value.shape[0] // rows)], axis=1)

    def make_sum(part, in1, b2, in2, in3, res, send, got):
        def c1(r):
            return pltpu.make_async_remote_copy(part.at[pl.ds((1 - core) * 16, 16)], in1, send.at[0], got.at[0],
                                                device_id=other_core, device_id_type=MESH)

        def c2(r):
            w, peer = w_peer(r)
            return pltpu.make_async_remote_copy(b2.at[w], in2.at[r - 1], send.at[r], got.at[r],
                                                device_id=peer, device_id_type=MESH)

        def c3(r):
            _, peer = z_peer(r)
            return pltpu.make_async_remote_copy(in3.at[z_at], in3.at[z_at], send.at[15 + r], got.at[15 + r],
                                                device_id=peer, device_id_type=MESH)

        mine = core * 16 + w_at

        def c4(r):
            _, peer = w_peer(r)
            return pltpu.make_async_remote_copy(res.at[mine], res.at[mine], send.at[22 + r], got.at[22 + r],
                                                device_id=peer, device_id_type=MESH)

        def c5(r):
            own = pl.ds(core * 16, 16)
            return pltpu.make_async_remote_copy(res.at[own], res.at[own], send.at[38], got.at[38],
                                                device_id=other_core, device_id_type=MESH)

        def start(make, count):
            for r in range(1, count):
                make(r).start()

        def finish(make, count):
            for r in range(1, count):
                make(r).wait_recv()

        def s1():
            start(c1, 2)

        def s2():
            finish(c1, 2)
            b2[...] = (part[pl.ds(core * 16, 16)].astype(F32) + in1[...].astype(F32)).astype(BF16)
            start(c2, 16)

        def s3():
            finish(c2, 16)
            total = b2[w_at].astype(F32)
            for r in range(15):
                total = total + in2[r].astype(F32)
            in3[z_at] = total.astype(BF16)
            start(c3, 8)

        def s4():
            finish(c3, 8)
            total = in3[0].astype(F32)
            for r in range(1, 8):
                total = total + in3[r].astype(F32)
            res[mine] = total.astype(BF16)
            start(c4, 16)

        def s5():
            finish(c4, 16)
            start(c5, 2)

        def s6():
            finish(c5, 2)

        def s7():
            for make, count in ((c1, 2), (c2, 16), (c3, 8), (c4, 16), (c5, 2)):
                for r in range(1, count):
                    make(r).wait_send()

        return s1, s2, s3, s4, s5, s6, s7

    sum_sc = make_sum(part_sc, in1_sc, b2_sc, in2_sc, in3_sc, res_sc, s_sc, g_sc)
    sum_f = make_sum(part_f, in1_f, b2_f, in2_f, in3_f, res_f, s_f, g_f)

    cor[...] = jnp.zeros_like(cor)
    col[...] = jnp.zeros_like(col)
    loads[1].wait()
    coarse_st[...] = pool(cot[...].reshape(NI * NJ, LANES)).astype(BF16).astype(F32)
    pack(0, False)
    loads[0].wait()
    fine_st[...] = vol[...].astype(F32)
    pack_volume()
    pl.semaphore_wait(barrier, len(partners))
    send(rim_copies(0, False))
    send(volume_copies())

    def build(k, fwd, bwd):
        for w in (fwd, bwd):
            if w is not None:
                w[...] = jnp.zeros_like(w)

        def band(w, t, c0, c1, c2):
            zero = jnp.zeros_like(c0)
            pairs = ((c0, zero), (c1, c0), (c2, c1), (zero, c2))
            for m, tile in enumerate(jnp.concatenate(pair, axis=1) for pair in pairs):
                for pair in range(2):
                    row = 64 * (2 * pair + 1 + m)
                    w[t, row : row + 64, 128 * pair : 128 * pair + 128] = tile

        def body(t, carry):
            taps = [k[3 * t + c] for c in range(3)]
            band(fwd, t, *taps)
            if bwd is not None:
                c0, c1, c2 = (v.astype(F32).T.astype(BF16) for v in taps)
                band(bwd, 8 - t, c2, c1, c0)
            return carry

        lax.fori_loop(0, TAPS, body, 0)

    loads[2].wait()
    build(k1, w1, None)
    loads[3].wait()
    build(k2, w2, w2b)
    loads[4].wait()
    build(kc, wc, wcb)
    for padded in (xv, xh, xs, xp, xc):
        rows, tail = padded.shape[2], padded.shape[3] - PAD
        padded[:, :, :, 0:PAD] = jnp.zeros((3, padded.shape[1], rows, PAD), padded.dtype)
        padded[:, :, :, tail:] = jnp.zeros((3, padded.shape[1], rows, PAD), padded.dtype)
    xvc[:, :, 0:PAD] = jnp.zeros((TAPS, 32, PAD), BF16)
    xvc[:, :, PAD + LANES :] = jnp.zeros((TAPS, 32, PAD), BF16)
    part_sc[28:32] = jnp.zeros((4, 64, 128), BF16)
    part_f[28:32] = jnp.zeros((4, 32, 128), BF16)

    def widen(value):
        wide = spread(value)
        top = wide.astype(BF16)
        rest = (wide - top.astype(F32)).astype(BF16)
        return dot(pool_matrix(128, 64, True), jnp.concatenate([top, rest], axis=0))

    receive(rim_copies(0, False))
    unpack_rims(0)
    assemble_coarse(0, xc)
    pooled_slope = ungroup(conv(lambda a, b: coarse_window(xc, a, b), wcb, 2 * CI * CJ, 'cc' in LOOPED), CI * CJ)
    upstream[...] = (cot[...].reshape(NI * NJ, LANES).astype(F32) + widen(pooled_slope) * 0.125).astype(BF16).astype(F32)

    receive(volume_copies())
    assemble_volume()

    first = ungroup(conv(wide_window, w1, 4 * (NI + 4) * NJ, 'c1' in LOOPED), (NI + 4) * NJ)
    sigma = sigmoid(first)
    hid[...] = (first * sigma).astype(BF16).astype(F32).reshape(NI + 4, NJ, LANES)
    own, own_sigma = first[NJ : NJ + NI * NJ], sigma[NJ : NJ + NI * NJ]
    slope1[...] = own_sigma * (1.0 + own * (1.0 - own_sigma))
    assemble_hidden()

    second = ungroup(conv(lambda a, b: fine_window(xh, a, b), w2, 4 * NI * NJ, 'c2' in LOOPED), NI * NJ)
    sigma = sigmoid(second)
    fine = (second * sigma).astype(BF16)
    fine_keep[...] = fine
    coarse_st[...] = (pool(fine) * 0.125).astype(BF16).astype(F32)
    second_slope = (upstream[...] * (sigma * (1.0 + second * (1.0 - sigma)))).astype(BF16).astype(F32)
    fine_st[...] = second_slope.reshape(NI, NJ, LANES)
    pack(1, True)
    send(rim_copies(1, True))

    def grouped_t(value, groups):
        return jnp.concatenate([value[:, GROUP * g : GROUP * (g + 1)] for g in range(groups)], axis=0).T.astype(BF16)

    slopes_t[...] = grouped_t(fine_st[...].reshape(NI * NJ, LANES), 4)

    def store_second(n, value):
        part_sc[n] = value

    def store_coarse(n, value):
        part_sc[14 + n] = value

    def store_first(n, value):
        part_f[pl.ds(2 * n, 2)] = value.reshape(2, 32, 128)

    grads(lambda a, b: fine_window(xh, a, b), slopes_t, store_second, 'g2' in LOOPED)
    pooled_t[...] = grouped_t(coarse_st[...].reshape(CI * CJ, CLANES), 2)
    grads(lambda a, b: coarse_window(xc, a, b), pooled_t, store_coarse, 'gc' in LOOPED)
    sum_sc[0]()

    receive(rim_copies(1, True))
    unpack_rims(1)
    sum_sc[1]()
    assemble_fine(1, xs)

    hidden_slope = ungroup(conv(lambda a, b: fine_window(xs, a, b), w2b, 4 * NI * NJ, 'c3' in LOOPED), NI * NJ)
    first_slope = (hidden_slope * slope1[...]).astype(BF16).astype(F32)
    slopes_t[...] = grouped_t(first_slope, 4)
    grads(lambda a, b: fine_window(xv, a + 1, b), slopes_t, store_first, 'g1' in LOOPED)
    sum_f[0]()
    sum_sc[2]()
    sum_f[1]()

    assemble_coarse(1, xp)
    coarse = ungroup(conv(lambda a, b: coarse_window(xp, a, b), wc, 2 * CI * CJ, 'cc' in LOOPED), CI * CJ).astype(BF16)
    wide = spread(coarse.astype(F32)).astype(BF16)
    repeated = dot(pool_matrix(128, 32, True), wide)
    field[...] = (fine_keep[...].astype(F32) + repeated).astype(BF16).reshape(NI, NJ, LANES)

    sum_sc[3]()
    sum_f[2]()
    sum_sc[4]()
    sum_f[3]()
    sum_sc[5]()
    out_sc[...] = res_sc[...]
    sum_f[4]()
    sum_f[5]()
    out_f[...] = res_f[...]
    sum_sc[6]()
    sum_f[6]()
    for there, _, copy in rim_copies(0, False) + volume_copies() + rim_copies(1, True):
        pl.when(there)(copy.wait_send)


def unpack_kernel(
    held, sc, f, field, first_out, second_out, coarse_out,
    first_grad, second_grad, coarse_grad, sem,
):
    copies = [
        pltpu.make_async_copy(src, dst, sem.at[n])
        for n, (src, dst) in enumerate((
            (held, field), (second_grad, second_out), (coarse_grad, coarse_out), (first_grad, first_out),
        ))
    ]
    copies[0].start()

    def place(read, out):
        for t in range(TAPS):
            block = read(t).astype(F32).T
            out[3 * t] = block[0:64]
            out[3 * t + 1] = block[64:128]
        for u in range(5):
            block = read(TAPS + u).astype(F32).T
            out[6 * u + 2] = block[0:64]
            if u < 4:
                out[6 * u + 5] = block[64:128]

    place(lambda n: sc[n], second_grad)
    copies[1].start()
    for t in range(TAPS):
        block = sc[14 + t].astype(F32)
        coarse_grad[26 - 3 * t] = block[:, 0:64]
        coarse_grad[25 - 3 * t] = block[:, 64:128]
    for u in range(5):
        block = sc[14 + TAPS + u].astype(F32)
        coarse_grad[24 - 6 * u] = block[:, 0:64]
        if u < 4:
            coarse_grad[21 - 6 * u] = block[:, 64:128]
    copies[2].start()
    place(lambda n: f[2 * n : 2 * n + 2].reshape(64, 128), first_grad)
    copies[3].start()
    for copy in copies:
        copy.wait()


def per_device(volume, cotangent, first_kernel, second_kernel, coarse_kernel):
    in_hbm, in_vmem = (pl.BlockSpec(memory_space=space) for space in (pltpu.HBM, pltpu.VMEM))
    dma = pltpu.SemaphoreType.DMA

    def sum_buffers(rows):
        return [
            pltpu.VMEM((32, rows, 128), BF16), pltpu.VMEM((16, rows, 128), BF16), pltpu.VMEM((16, rows, 128), BF16),
            pltpu.VMEM((15, rows, 128), BF16), pltpu.VMEM((8, rows, 128), BF16), pltpu.VMEM((32, rows, 128), BF16),
        ]

    sc_bufs, f_bufs = sum_buffers(64), sum_buffers(32)
    mixed = [b for pair in zip(sc_bufs, f_bufs) for b in pair]
    scratch = [
        pltpu.VMEM((NI, NJ, LANES), F32),
        pltpu.VMEM((CI, CJ, CLANES), F32),
        pltpu.VMEM((3, NI + 4, NJ, LANES + 2 * PAD), BF16),
        pltpu.VMEM((3, NI + 2, NJ, LANES + 2 * PAD), BF16),
        pltpu.VMEM((3, NI + 2, NJ, LANES + 2 * PAD), BF16),
        pltpu.VMEM((3, CI + 2, CJ, CLANES + 2 * PAD), F32),
        pltpu.VMEM((3, CI + 2, CJ, CLANES + 2 * PAD), F32),
        pltpu.VMEM((NI * NJ, LANES), F32),
        pltpu.VMEM((NI * NJ, LANES), F32),
        pltpu.VMEM((NI * NJ, LANES), BF16),
        pltpu.VMEM((GROUP, 4 * NI * NJ), BF16),
        pltpu.VMEM((4 * (NI + 4) * NJ, GROUP), F32),
        pltpu.VMEM((TAPS, WINDOW, GROUP), BF16),
        pltpu.VMEM((TAPS, WINDOW, GROUP), BF16),
        pltpu.VMEM((TAPS, WINDOW, GROUP), BF16),
        pltpu.VMEM((TAPS, WINDOW, GROUP), BF16),
        pltpu.VMEM((TAPS, WINDOW, GROUP), BF16),
        pltpu.VMEM((2, 2, 16, 1280), BF16), pltpu.VMEM((2, 2, 16, 1280), BF16),
        pltpu.VMEM((2, 2, 16, 640), BF16), pltpu.VMEM((2, 2, 16, 640), BF16),
        pltpu.VMEM((2, 4, 16, 128), BF16), pltpu.VMEM((2, 4, 16, 128), BF16),
        pltpu.VMEM((16, 640), F32), pltpu.VMEM((2, 16, 640), F32),
        pltpu.VMEM((16, 128), F32), pltpu.VMEM((4, 16, 128), F32),
        *mixed,
        pltpu.VMEM((TAPS, 64, 128), F32),
        dma((3, 2)), dma((3, 2)), dma((3, 2)), dma((3, 2)), dma((3, 4)), dma((3, 4)),
        dma((39,)), dma((39,)), dma((39,)), dma((39,)), dma((5,)),
        pltpu.VMEM(volume.shape[1:], BF16), pltpu.VMEM(volume.shape[1:], BF16),
        *[pltpu.VMEM((27, 64, 64), BF16)] * 3,
        pltpu.VMEM((GROUP, 2 * CI * CJ), BF16),
        pltpu.VMEM((NI + 4, NJ, LANES), F32),
        pltpu.VMEM((TAPS, 32, LANES + 2 * PAD), BF16),
        pltpu.VMEM((16, LANES), F32), pltpu.VMEM((16, 256), F32),
        pltpu.VMEM((2, 16, LANES), F32), pltpu.VMEM((4, 16, 256), F32),
        pltpu.VMEM((2, 3, 16, LANES), F32),
        pltpu.VMEM((2, 16, LANES), BF16), pltpu.VMEM((2, 16, LANES), BF16),
        pltpu.VMEM((4, 16, 256), BF16), pltpu.VMEM((4, 16, 256), BF16),
        pltpu.VMEM((2, 2, NJ, LANES), BF16),
    ]
    block = volume.shape[1:]
    taps = (27, 64, 64)
    kernels = (first_kernel, second_kernel, coarse_kernel)
    operands = (volume[0], cotangent[0], *(k.reshape(taps) for k in kernels))
    field, sc, f = pl.pallas_call(
        kernel,
        out_shape=(
            jax.ShapeDtypeStruct(block, BF16),
            jax.ShapeDtypeStruct((32, 64, 128), BF16),
            jax.ShapeDtypeStruct((32, 32, 128), BF16),
        ),
        in_specs=[in_hbm] * 5,
        out_specs=(in_vmem,) * 3,
        scratch_shapes=scratch,
        compiler_params=pltpu.CompilerParams(
            collective_id=0, has_side_effects=True, vmem_limit_bytes=48 * 1024 * 1024
        ),
        name="block",
    )(*(pltpu.with_memory_space_constraint(v, pltpu.HBM) for v in operands))
    field, first_grad, second_grad, coarse_grad = pl.pallas_call(
        unpack_kernel,
        out_shape=(jax.ShapeDtypeStruct(block, BF16),) + (jax.ShapeDtypeStruct(taps, F32),) * 3,
        in_specs=[in_vmem] * 3,
        out_specs=(in_hbm,) * 4,
        scratch_shapes=[
            *[pltpu.VMEM(taps, F32)] * 3, dma((4,)),
        ],
        compiler_params=pltpu.CompilerParams(vmem_limit_bytes=32 * 1024 * 1024),
        name="unpack",
    )(field, sc, f)
    kernel_shape = first_kernel.shape
    return (
        field[None],
        first_grad.reshape(kernel_shape),
        second_grad.reshape(kernel_shape),
        coarse_grad.reshape(kernel_shape),
    )


def solution(mesh):
    in_specs = (P("dp", "gx", "gy", None), P("dp", "gx", "gy", None), P(), P(), P())
    out_specs = (P("dp", "gx", "gy", None), P(), P(), P())
    return jax.shard_map(
        per_device, mesh=mesh, in_specs=in_specs, out_specs=out_specs, check_vma=False
    )
```

```python
import jax
import jax.numpy as jnp
from jax import lax
from jax.experimental import pallas as pl
from jax.experimental.pallas import tpu as pltpu
from jax.sharding import PartitionSpec as P

MESH = pl.DeviceIdType.MESH

FARTHEST = {
    2: (1,),
    16: sorted(range(1, 16), key=lambda r: -(min(r // 4, 4 - r // 4) + min(r % 4, 4 - r % 4))),
    8: sorted(range(1, 8), key=lambda r: -min(r, 8 - r)),
}
F32 = jnp.float32
BF16 = jnp.bfloat16

NI, NJ, LANES = 8, 16, 1024
CI, CJ, CLANES = 4, 8, 512
PAD = 128
GROUP = 256
WINDOW = 512
TAPS = 9
LOOPED = ('c2', 'g1')


def dot(a, b, dims=((1,), (0,))):
    return lax.dot_general(a, b, (dims, ((), ())), preferred_element_type=F32)


def sigmoid(v):
    return 1.0 / (1.0 + jnp.exp(-v))


def kernel(
    vol_in, cot_in, k1_in, k2_in, kc_in,
    field, out_sc, out_f,
    fine_st, coarse_st, xv, xh, xs, xp, xc, slope1, upstream, fine_keep, slopes_t, acc,
    w1, w2, w2b, wc, wcb,
    s_e, r_e, s_n, r_n, s_c, r_c, col, colr, cor, corr,
    part_sc, part_f, in1_sc, in1_f, b2_sc, b2_f, in2_sc, in2_f, in3_sc, in3_f, res_sc, res_f, half,
    se_sem, re_sem, sn_sem, rn_sem, sc_sem, rc_sem,
    s_sc, g_sc, s_f, g_f, in_sem,
    vol, cot, k1, k2, kc,
    pooled_t, hid, xvc, colw, corw, colv, corv, colx, sv_n, rv_n, sv_c, rv_c, rv_e,
):
    loads = [
        pltpu.make_async_copy(src, dst, in_sem.at[n])
        for n, (src, dst) in enumerate(((vol_in, vol), (cot_in, cot), (k1_in, k1), (k2_in, k2), (kc_in, kc)))
    ]
    for load in loads:
        load.start()

    gx, gy, dp = lax.axis_index("gx"), lax.axis_index("gy"), lax.axis_index("dp")
    x_at, z_hi = lax.div(gy, 2), lax.rem(gy, 2)
    z_lo, core = lax.div(gx, 2), lax.rem(gx, 2)
    w_at = x_at * 4 + dp
    z_at = z_hi * 4 + z_lo

    def side(at, step):
        return lax.rem(at + step + 8, 8)

    def near(di, dj):
        return {"gx": side(gx, di), "gy": side(gy, dj)}

    def w_peer(r):
        x, y = lax.rem(x_at + r // 4, 4), lax.rem(dp + r % 4, 4)
        return x * 4 + y, {"gy": x * 2 + z_hi, "dp": y}

    other_core = {"gx": z_lo * 2 + 1 - core}

    def z_peer(r):
        z = lax.rem(z_at + r, 8)
        return z, {"gx": lax.rem(z, 4) * 2 + core, "gy": x_at * 2 + lax.div(z, 4)}

    steps = (-1, 1)
    barrier = pltpu.get_barrier_semaphore()
    partners = [near(s, 0) for s in steps] + [near(0, s) for s in steps]
    partners += [near(s, t) for s in steps for t in steps]
    partners += [other_core] + [w_peer(r)[1] for r in range(1, 16)] + [z_peer(r)[1] for r in range(1, 8)]
    for partner in partners:
        pl.semaphore_signal(barrier, inc=1, device_id=partner, device_id_type=MESH)

    def pack(stage, with_fine):
        for e in range(2):
            row = coarse_st[e * (CI - 1)]
            if with_fine:
                s_e[stage, e, :, 0:LANES] = fine_st[e * (NI - 1)].astype(BF16)
            s_e[stage, e, :, LANES:] = jnp.concatenate([row[:, :256], row[:, 256:]], axis=0).astype(BF16)
        for n in range(2):
            j, cj = n * (NJ - 1), n * (CJ - 1)
            if with_fine:
                for i in range(NI):
                    col[i : i + 1, 0:512] = fine_st[i, j : j + 1, 0:512]
                    col[NI + i : NI + i + 1, 0:512] = fine_st[i, j : j + 1, 512:1024]
            for i in range(CI):
                for k in range(4):
                    col[4 * k + i : 4 * k + i + 1, 512:640] = coarse_st[i, cj : cj + 1, 128 * k : 128 * k + 128]
            s_n[stage, n] = col[...].astype(BF16)
        for e in range(2):
            for n in range(2):
                i, j, cj = e * (NI - 1), n * (NJ - 1), n * (CJ - 1)
                if with_fine:
                    for k in range(8):
                        cor[k : k + 1] = fine_st[i, j : j + 1, 128 * k : 128 * k + 128]
                for k in range(4):
                    cor[8 + k : 9 + k] = coarse_st[e * (CI - 1), cj : cj + 1, 128 * k : 128 * k + 128]
                s_c[stage, 2 * e + n] = cor[...].astype(BF16)

    def pack_volume():
        for n in range(2):
            for i in range(NI):
                for m in range(2):
                    j = n * (NJ - 2) + m
                    colw[NI * m + i : NI * m + i + 1, :] = fine_st[i, j : j + 1, :]
            sv_n[n] = colw[...].astype(BF16)
        for e in range(2):
            for n in range(2):
                for cell in range(4):
                    i, j = e * (NI - 2) + cell // 2, n * (NJ - 2) + cell % 2
                    for k in range(4):
                        corw[4 * k + cell : 4 * k + cell + 1, :] = fine_st[i, j : j + 1, 256 * k : 256 * k + 256]
                sv_c[2 * e + n] = corw[...].astype(BF16)

    gx_low, gx_high, gy_low, gy_high = gx > 0, gx < 7, gy > 0, gy < 7
    to_x, to_y = (gx_low, gx_high), (gy_low, gy_high)

    def to_sides(n_src, n_dst, n_sems, c_src, c_dst, c_sems, e_src, e_dst, e_sems):
        copies = []
        for n in range(2):
            copies.append((to_y[n], to_y[1 - n], pltpu.make_async_remote_copy(
                n_src(n), n_dst(n), n_sems[0].at[n], n_sems[1].at[n],
                device_id=near(0, steps[n]), device_id_type=MESH)))
        for e in range(2):
            for n in range(2):
                c = 2 * e + n
                copies.append((to_x[e] & to_y[n], to_x[1 - e] & to_y[1 - n], pltpu.make_async_remote_copy(
                    c_src(c), c_dst(c), c_sems[0].at[c], c_sems[1].at[c],
                    device_id=near(steps[e], steps[n]), device_id_type=MESH)))
        for e in range(2):
            copies.append((to_x[e], to_x[1 - e], pltpu.make_async_remote_copy(
                e_src(e), e_dst(e), e_sems[0].at[e], e_sems[1].at[e],
                device_id=near(steps[e], 0), device_id_type=MESH)))
        return copies

    def rim_copies(stage, with_fine):
        lanes_e, lanes_n = (pl.ds(0, 1280), pl.ds(0, 640)) if with_fine else (pl.ds(1024, 256), pl.ds(512, 128))
        return to_sides(
            lambda n: s_n.at[stage, n, :, lanes_n], lambda n: r_n.at[stage, n, :, lanes_n], (sn_sem.at[stage], rn_sem.at[stage]),
            lambda c: s_c.at[stage, c], lambda c: r_c.at[stage, c], (sc_sem.at[stage], rc_sem.at[stage]),
            lambda e: s_e.at[stage, e, :, lanes_e], lambda e: r_e.at[stage, e, :, lanes_e], (se_sem.at[stage], re_sem.at[stage]))

    def volume_copies():
        return to_sides(
            lambda n: sv_n.at[n], lambda n: rv_n.at[n], (sn_sem.at[2], rn_sem.at[2]),
            lambda c: sv_c.at[c], lambda c: rv_c.at[c], (sc_sem.at[2], rc_sem.at[2]),
            lambda e: vol.at[pl.ds(e * (NI - 2), 2)], lambda e: rv_e.at[e], (se_sem.at[2], re_sem.at[2]))

    def send(copies):
        for there, _, copy in copies:
            pl.when(there)(copy.start)

    def receive(copies):
        for _, there, copy in copies:
            pl.when(there)(copy.wait_recv)

    def place(dst, index, value, low, high, rows):
        at = lax.broadcasted_iota(jnp.int32, value.shape, 0)
        dst[0, index, :, PAD : PAD + value.shape[1]] = jnp.where(
            at == 0, jnp.broadcast_to(low, value.shape), pltpu.roll(value, 1, 0)).astype(dst.dtype)
        dst[1, index, :, PAD : PAD + value.shape[1]] = value.astype(dst.dtype)
        dst[2, index, :, PAD : PAD + value.shape[1]] = jnp.where(
            at == rows - 1, jnp.broadcast_to(high, value.shape), pltpu.roll(value, rows - 1, 0)).astype(dst.dtype)

    def keep(here, value):
        return jnp.where(here, value, 0.0)

    def unpack_rims(stage):
        for n in range(2):
            colr[n] = r_n[stage, n].astype(F32)
        for c in range(4):
            corr[c] = r_c[stage, c].astype(F32)

    def corner(c, first, count):
        return jnp.concatenate([corr[c, first + k : first + k + 1, :] for k in range(count)], axis=1)

    def assemble_fine(stage, dst):
        def body(i, carry):
            low = jnp.concatenate([colr[1, pl.ds(i, 1), 0:512], colr[1, pl.ds(i + NI, 1), 0:512]], axis=1)
            high = jnp.concatenate([colr[0, pl.ds(i, 1), 0:512], colr[0, pl.ds(i + NI, 1), 0:512]], axis=1)
            place(dst, i + 1, fine_st[i], keep(gy_low, low), keep(gy_high, high), NJ)
            return carry

        lax.fori_loop(0, NI, body, 0)
        for e, index, here in ((1, 0, gx_low), (0, NI + 1, gx_high)):
            value = keep(here, r_e[stage, e, :, 0:LANES].astype(F32))
            low = keep(here & gy_low, corner(2 * e + 1, 0, 8))
            high = keep(here & gy_high, corner(2 * e, 0, 8))
            place(dst, index, value, low, high, NJ)

    def assemble_volume():
        for n in range(2):
            colv[n] = rv_n[n].astype(F32)
        for c in range(4):
            corv[c] = rv_c[c].astype(F32)

        def body(i, carry):
            low, high = colv[1, pl.ds(i + NI, 1), :], colv[0, pl.ds(i, 1), :]
            place(xv, i + 2, fine_st[i], keep(gy_low, low), keep(gy_high, high), NJ)
            return carry

        lax.fori_loop(0, NI, body, 0)

        def cells(c, cell):
            return jnp.concatenate([corv[c, 4 * k + cell : 4 * k + cell + 1, :] for k in range(4)], axis=1)

        for m in range(2):
            colx[0, m, 2:10, :] = keep(gy_low, colv[1, NI * m : NI * m + NI, :])
            colx[1, 1 + m, 2:10, :] = keep(gy_high, colv[0, NI * m : NI * m + NI, :])
        for i in range(NI):
            colx[0, 2, i + 2 : i + 3, :] = fine_st[i, 0:1, :]
            colx[1, 0, i + 2 : i + 3, :] = fine_st[i, NJ - 1 : NJ, :]
        for e, first_row, here in ((1, 0, gx_low), (0, NI + 2, gx_high)):
            for m in range(2):
                at = first_row + m
                value = keep(here, rv_e[e, m].astype(F32))
                low = [keep(here & gy_low, cells(2 * e + 1, 2 * m + j)) for j in range(2)]
                high = [keep(here & gy_high, cells(2 * e, 2 * m + j)) for j in range(2)]
                place(xv, at, value, low[1], high[0], NJ)
                for j in range(2):
                    colx[0, j, at : at + 1, :] = low[j]
                    colx[1, 1 + j, at : at + 1, :] = high[j]
                colx[0, 2, at : at + 1, :] = value[0:1]
                colx[1, 0, at : at + 1, :] = value[NJ - 1 : NJ]
        for a in range(3):
            for b in range(3):
                for m in range(2):
                    strip = colx[m, b]
                    strip = strip if a == 0 else pltpu.roll(strip, 16 - a, 0)
                    xvc[3 * a + b, 16 * m : 16 * m + 16, PAD : PAD + LANES] = strip.astype(BF16)

    def assemble_hidden():
        def body(at, carry):
            here = ((at > 0) | gx_low) & ((at < NI + 1) | gx_high)
            low, high = hid[NI + 2, pl.ds(at, 1), :], hid[NI + 3, pl.ds(at, 1), :]
            place(xh, at, keep(here, hid[at]), keep(here & gy_low, low), keep(here & gy_high, high), NJ)
            return carry

        lax.fori_loop(0, NI + 2, body, 0)

    def assemble_coarse(stage, dst):
        for i in range(CI):
            low = jnp.concatenate([colr[1, 4 * k + i : 4 * k + i + 1, 512:640] for k in range(4)], axis=1)
            high = jnp.concatenate([colr[0, 4 * k + i : 4 * k + i + 1, 512:640] for k in range(4)], axis=1)
            place(dst, i + 1, coarse_st[i], keep(gy_low, low), keep(gy_high, high), CJ)
        for e, index, here in ((1, 0, gx_low), (0, CI + 1, gx_high)):
            row = r_e[stage, e, :, LANES:].astype(F32)
            value = keep(here, jnp.concatenate([row[:CJ], row[CJ:]], axis=1))
            low = keep(here & gy_low, corner(2 * e + 1, 8, 4))
            high = keep(here & gy_high, corner(2 * e, 8, 4))
            place(dst, index, value, low, high, CJ)

    def wide_window(a, b):
        parts = []
        for g in range(4):
            lanes = slice(GROUP * g, GROUP * g + WINDOW)
            parts += [xv[b, pl.ds(a, NI + 2), :, lanes].reshape((NI + 2) * NJ, WINDOW), xvc[3 * a + b, :, lanes]]
        return jnp.concatenate(parts, axis=0)

    def fine_window(src, a, b):
        return jnp.concatenate(
            [src[b, pl.ds(a, NI), :, GROUP * g : GROUP * g + WINDOW].reshape(NI * NJ, WINDOW) for g in range(4)], axis=0)

    def coarse_window(src, a, b):
        return jnp.concatenate(
            [src[b, pl.ds(a, CI), :, GROUP * g : GROUP * g + WINDOW].reshape(CI * CJ, WINDOW) for g in range(2)],
            axis=0).astype(BF16)

    def three(body, looped):
        if looped:
            lax.fori_loop(0, 3, body, 0)
        else:
            for a in range(3):
                body(a, 0)

    def conv(window, weights, rows, looped):
        if not looped:
            total = dot(window(0, 0), weights[0])
            for t in range(1, TAPS):
                total = total + dot(window(t // 3, t % 3), weights[t])
            return total
        acc[0:rows] = jnp.zeros((rows, GROUP), F32)

        def body(a, carry):
            total = acc[0:rows]
            for b in range(3):
                total = total + dot(window(a, b), weights[3 * a + b])
            acc[0:rows] = total
            return carry

        lax.fori_loop(0, 3, body, 0)
        return acc[0:rows]

    def joined(window, weights):
        wide = jnp.concatenate([window(t // 3, t % 3) for t in range(TAPS)], axis=1)
        return dot(wide, weights[...].reshape(TAPS * WINDOW, GROUP))

    def by_group(window, weights, rows):
        def body(g, carry):
            lanes = pl.ds(pl.multiple_of(g * GROUP, GROUP), WINDOW)
            total = dot(window(0, 0, lanes), weights[0])
            for t in range(1, TAPS):
                total = total + dot(window(t // 3, t % 3, lanes), weights[t])
            acc[pl.ds(pl.multiple_of(g * rows, 16), rows)] = total
            return carry

        lax.fori_loop(0, 4, body, 0)
        return acc[0 : 4 * rows]

    def group_window(src):
        return lambda a, b, lanes: src[b, a : a + NI, :, lanes].reshape(NI * NJ, WINDOW)

    def wide_group_window(a, b, lanes):
        own = xv[b, a : a + NI + 2, :, lanes].reshape((NI + 2) * NJ, WINDOW)
        return jnp.concatenate([own, xvc[3 * a + b, :, lanes]], axis=0)

    def grads(window, slopes, store, looped):
        def body(a, carry):
            for b in range(3):
                g = dot(slopes[...], window(a, b))
                even = g[0:64, 0:384] + g[128:192, 128:512]
                odd = g[64:128, 128:384] + g[192:256, 256:512]
                shifted = jnp.concatenate([even[:, 64:192], even[:, 192:320]], axis=1)
                total = odd + shifted
                store(3 * a + b, total[:, 0:128].astype(BF16))
                half[3 * a + b] = total[:, 128:256]
            return carry

        three(body, looped)
        lane = lax.broadcasted_iota(jnp.int32, (64, 128), 1)
        for u in range(5):
            left = half[2 * u]
            right = pltpu.roll(half[2 * u + 1], 64, 1) if u < 4 else jnp.zeros_like(left)
            store(TAPS + u, jnp.where(lane < 64, left, right).astype(BF16))

    def pool_matrix(rows, columns, flip):
        r = lax.broadcasted_iota(jnp.int32, (rows, columns), 1 if flip else 0)
        s = lax.broadcasted_iota(jnp.int32, (rows, columns), 0 if flip else 1)
        r = r & 31
        return jnp.where(r == (s >> 5) * 8 + ((s & 15) >> 1), 1.0, 0.0).astype(BF16)

    def pool(value):
        sums = dot(pool_matrix(32, 128, False), value)
        lane = lax.broadcasted_iota(jnp.int32, (32, 128), 1)
        tiles = []
        for k in range(4):
            pair = []
            for m in range(2):
                tile = sums[:, 256 * k + 128 * m : 256 * k + 128 * m + 128]
                pair.append(tile + pltpu.roll(tile, 64, 1))
            tiles.append(jnp.where(lane < 64, pair[0], pair[1]))
        return jnp.concatenate(tiles, axis=1).reshape(CI, CJ, CLANES)

    def spread(value):
        lane = lax.broadcasted_iota(jnp.int32, (32, 128), 1)
        tiles = []
        for k in range(4):
            tile = value[:, 128 * k : 128 * k + 128]
            turned = pltpu.roll(tile, 64, 1)
            tiles += [jnp.where(lane < 64, tile, turned), jnp.where(lane < 64, turned, tile)]
        return jnp.concatenate(tiles, axis=1)

    def ungroup(value, rows):
        return jnp.concatenate([value[rows * g : rows * (g + 1)] for g in range(value.shape[0] // rows)], axis=1)

    def make_sum(part, in1, b2, in2, in3, res, send, got):
        def c1(r):
            return pltpu.make_async_remote_copy(part.at[pl.ds((1 - core) * 16, 16)], in1, send.at[0], got.at[0],
                                                device_id=other_core, device_id_type=MESH)

        def c2(r):
            w, peer = w_peer(r)
            return pltpu.make_async_remote_copy(b2.at[w], in2.at[r - 1], send.at[r], got.at[r],
                                                device_id=peer, device_id_type=MESH)

        def c3(r):
            _, peer = z_peer(r)
            return pltpu.make_async_remote_copy(in3.at[z_at], in3.at[z_at], send.at[15 + r], got.at[15 + r],
                                                device_id=peer, device_id_type=MESH)

        mine = core * 16 + w_at

        def c4(r):
            _, peer = w_peer(r)
            return pltpu.make_async_remote_copy(res.at[mine], res.at[mine], send.at[22 + r], got.at[22 + r],
                                                device_id=peer, device_id_type=MESH)

        def c5(r):
            own = pl.ds(core * 16, 16)
            return pltpu.make_async_remote_copy(res.at[own], res.at[own], send.at[38], got.at[38],
                                                device_id=other_core, device_id_type=MESH)

        def start(make, count):
            for r in FARTHEST[count]:
                make(r).start()

        def finish(make, count):
            for r in range(1, count):
                make(r).wait_recv()

        def s1():
            start(c1, 2)

        def s2():
            finish(c1, 2)
            b2[...] = (part[pl.ds(core * 16, 16)].astype(F32) + in1[...].astype(F32)).astype(BF16)
            start(c2, 16)

        def s3():
            finish(c2, 16)
            total = b2[w_at].astype(F32)
            for r in range(15):
                total = total + in2[r].astype(F32)
            in3[z_at] = total.astype(BF16)
            start(c3, 8)

        def s4():
            finish(c3, 8)
            total = in3[0].astype(F32)
            for r in range(1, 8):
                total = total + in3[r].astype(F32)
            res[mine] = total.astype(BF16)
            start(c4, 16)

        def s5():
            finish(c4, 16)
            start(c5, 2)

        def s6():
            finish(c5, 2)

        def s7():
            for make, count in ((c1, 2), (c2, 16), (c3, 8), (c4, 16), (c5, 2)):
                for r in range(1, count):
                    make(r).wait_send()

        return s1, s2, s3, s4, s5, s6, s7

    sum_sc = make_sum(part_sc, in1_sc, b2_sc, in2_sc, in3_sc, res_sc, s_sc, g_sc)
    sum_f = make_sum(part_f, in1_f, b2_f, in2_f, in3_f, res_f, s_f, g_f)

    cor[...] = jnp.zeros_like(cor)
    col[...] = jnp.zeros_like(col)
    loads[1].wait()
    coarse_st[...] = pool(cot[...].reshape(NI * NJ, LANES)).astype(BF16).astype(F32)
    pack(0, False)
    loads[0].wait()
    fine_st[...] = vol[...].astype(F32)
    pack_volume()
    pl.semaphore_wait(barrier, len(partners))
    send(rim_copies(0, False))
    send(volume_copies())

    def build(k, fwd, bwd):
        for w in (fwd, bwd):
            if w is not None:
                w[...] = jnp.zeros_like(w)

        def band(w, t, c0, c1, c2):
            zero = jnp.zeros_like(c0)
            pairs = ((c0, zero), (c1, c0), (c2, c1), (zero, c2))
            for m, tile in enumerate(jnp.concatenate(pair, axis=1) for pair in pairs):
                for pair in range(2):
                    row = 64 * (2 * pair + 1 + m)
                    w[t, row : row + 64, 128 * pair : 128 * pair + 128] = tile

        def body(t, carry):
            taps = [k[3 * t + c] for c in range(3)]
            band(fwd, t, *taps)
            if bwd is not None:
                c0, c1, c2 = (v.astype(F32).T.astype(BF16) for v in taps)
                band(bwd, 8 - t, c2, c1, c0)
            return carry

        lax.fori_loop(0, TAPS, body, 0)

    loads[2].wait()
    build(k1, w1, None)
    loads[3].wait()
    build(k2, w2, w2b)
    loads[4].wait()
    build(kc, wc, wcb)
    for padded in (xv, xh, xs, xp, xc):
        rows, tail = padded.shape[2], padded.shape[3] - PAD
        padded[:, :, :, 0:PAD] = jnp.zeros((3, padded.shape[1], rows, PAD), padded.dtype)
        padded[:, :, :, tail:] = jnp.zeros((3, padded.shape[1], rows, PAD), padded.dtype)
    xvc[:, :, 0:PAD] = jnp.zeros((TAPS, 32, PAD), BF16)
    xvc[:, :, PAD + LANES :] = jnp.zeros((TAPS, 32, PAD), BF16)
    part_sc[28:32] = jnp.zeros((4, 64, 128), BF16)
    part_f[28:32] = jnp.zeros((4, 32, 128), BF16)

    def widen(value):
        wide = spread(value)
        top = wide.astype(BF16)
        rest = (wide - top.astype(F32)).astype(BF16)
        return dot(pool_matrix(128, 64, True), jnp.concatenate([top, rest], axis=0))

    receive(rim_copies(0, False))
    unpack_rims(0)
    assemble_coarse(0, xc)
    pooled_slope = ungroup(joined(lambda a, b: coarse_window(xc, a, b), wcb), CI * CJ)
    upstream[...] = (cot[...].reshape(NI * NJ, LANES).astype(F32) + widen(pooled_slope) * 0.125).astype(BF16).astype(F32)

    receive(volume_copies())
    assemble_volume()

    first = ungroup(conv(wide_window, w1, 4 * (NI + 4) * NJ, 'c1' in LOOPED), (NI + 4) * NJ)
    sigma = sigmoid(first)
    hid[...] = (first * sigma).astype(BF16).astype(F32).reshape(NI + 4, NJ, LANES)
    own, own_sigma = first[NJ : NJ + NI * NJ], sigma[NJ : NJ + NI * NJ]
    slope1[...] = own_sigma * (1.0 + own * (1.0 - own_sigma))
    assemble_hidden()

    second = ungroup(conv(lambda a, b: fine_window(xh, a, b), w2, 4 * NI * NJ, 'c2' in LOOPED), NI * NJ)
    sigma = sigmoid(second)
    fine = (second * sigma).astype(BF16)
    fine_keep[...] = fine
    coarse_st[...] = (pool(fine) * 0.125).astype(BF16).astype(F32)
    second_slope = (upstream[...] * (sigma * (1.0 + second * (1.0 - sigma)))).astype(BF16).astype(F32)
    fine_st[...] = second_slope.reshape(NI, NJ, LANES)
    pack(1, True)
    send(rim_copies(1, True))

    def grouped_t(value, groups):
        return jnp.concatenate([value[:, GROUP * g : GROUP * (g + 1)] for g in range(groups)], axis=0).T.astype(BF16)

    slopes_t[...] = grouped_t(fine_st[...].reshape(NI * NJ, LANES), 4)

    def store_second(n, value):
        part_sc[n] = value

    def store_coarse(n, value):
        part_sc[14 + n] = value

    def store_first(n, value):
        part_f[pl.ds(2 * n, 2)] = value.reshape(2, 32, 128)

    grads(lambda a, b: fine_window(xh, a, b), slopes_t, store_second, 'g2' in LOOPED)
    pooled_t[...] = grouped_t(coarse_st[...].reshape(CI * CJ, CLANES), 2)
    grads(lambda a, b: coarse_window(xc, a, b), pooled_t, store_coarse, 'gc' in LOOPED)
    sum_sc[0]()
    sum_sc[1]()

    receive(rim_copies(1, True))
    unpack_rims(1)
    assemble_fine(1, xs)

    hidden_slope = ungroup(conv(lambda a, b: fine_window(xs, a, b), w2b, 4 * NI * NJ, 'c3' in LOOPED), NI * NJ)
    first_slope = (hidden_slope * slope1[...]).astype(BF16).astype(F32)
    slopes_t[...] = grouped_t(first_slope, 4)
    grads(lambda a, b: fine_window(xv, a + 1, b), slopes_t, store_first, 'g1' in LOOPED)
    sum_f[0]()
    sum_sc[2]()
    sum_f[1]()

    assemble_coarse(1, xp)
    coarse = ungroup(joined(lambda a, b: coarse_window(xp, a, b), wc), CI * CJ).astype(BF16)
    wide = spread(coarse.astype(F32)).astype(BF16)
    repeated = dot(pool_matrix(128, 32, True), wide)
    field[...] = (fine_keep[...].astype(F32) + repeated).astype(BF16).reshape(NI, NJ, LANES)

    sum_sc[3]()
    sum_f[2]()
    sum_f[3]()
    sum_sc[4]()
    sum_f[4]()
    sum_sc[5]()
    out_sc[...] = res_sc[...]
    sum_f[5]()
    out_f[...] = res_f[...]
    sum_sc[6]()
    sum_f[6]()
    for there, _, copy in rim_copies(0, False) + volume_copies() + rim_copies(1, True):
        pl.when(there)(copy.wait_send)


def unpack_kernel(
    held, sc, f, field, first_out, second_out, coarse_out,
    first_grad, second_grad, coarse_grad, sem,
):
    copies = [
        pltpu.make_async_copy(src, dst, sem.at[n])
        for n, (src, dst) in enumerate((
            (held, field), (second_grad, second_out), (coarse_grad, coarse_out), (first_grad, first_out),
        ))
    ]
    copies[0].start()

    def place(read, out):
        for t in range(TAPS):
            block = read(t).astype(F32).T
            out[3 * t] = block[0:64]
            out[3 * t + 1] = block[64:128]
        for u in range(5):
            block = read(TAPS + u).astype(F32).T
            out[6 * u + 2] = block[0:64]
            if u < 4:
                out[6 * u + 5] = block[64:128]

    place(lambda n: sc[n], second_grad)
    copies[1].start()
    for t in range(TAPS):
        block = sc[14 + t].astype(F32)
        coarse_grad[26 - 3 * t] = block[:, 0:64]
        coarse_grad[25 - 3 * t] = block[:, 64:128]
    for u in range(5):
        block = sc[14 + TAPS + u].astype(F32)
        coarse_grad[24 - 6 * u] = block[:, 0:64]
        if u < 4:
            coarse_grad[21 - 6 * u] = block[:, 64:128]
    copies[2].start()
    place(lambda n: f[2 * n : 2 * n + 2].reshape(64, 128), first_grad)
    copies[3].start()
    for copy in copies:
        copy.wait()


def per_device(volume, cotangent, first_kernel, second_kernel, coarse_kernel):
    in_hbm, in_vmem = (pl.BlockSpec(memory_space=space) for space in (pltpu.HBM, pltpu.VMEM))
    dma = pltpu.SemaphoreType.DMA

    def sum_buffers(rows):
        return [
            pltpu.VMEM((32, rows, 128), BF16), pltpu.VMEM((16, rows, 128), BF16), pltpu.VMEM((16, rows, 128), BF16),
            pltpu.VMEM((15, rows, 128), BF16), pltpu.VMEM((8, rows, 128), BF16), pltpu.VMEM((32, rows, 128), BF16),
        ]

    sc_bufs, f_bufs = sum_buffers(64), sum_buffers(32)
    mixed = [b for pair in zip(sc_bufs, f_bufs) for b in pair]
    scratch = [
        pltpu.VMEM((NI, NJ, LANES), F32),
        pltpu.VMEM((CI, CJ, CLANES), F32),
        pltpu.VMEM((3, NI + 4, NJ, LANES + 2 * PAD), BF16),
        pltpu.VMEM((3, NI + 2, NJ, LANES + 2 * PAD), BF16),
        pltpu.VMEM((3, NI + 2, NJ, LANES + 2 * PAD), BF16),
        pltpu.VMEM((3, CI + 2, CJ, CLANES + 2 * PAD), F32),
        pltpu.VMEM((3, CI + 2, CJ, CLANES + 2 * PAD), F32),
        pltpu.VMEM((NI * NJ, LANES), F32),
        pltpu.VMEM((NI * NJ, LANES), F32),
        pltpu.VMEM((NI * NJ, LANES), BF16),
        pltpu.VMEM((GROUP, 4 * NI * NJ), BF16),
        pltpu.VMEM((4 * (NI + 4) * NJ, GROUP), F32),
        pltpu.VMEM((TAPS, WINDOW, GROUP), BF16),
        pltpu.VMEM((TAPS, WINDOW, GROUP), BF16),
        pltpu.VMEM((TAPS, WINDOW, GROUP), BF16),
        pltpu.VMEM((TAPS, WINDOW, GROUP), BF16),
        pltpu.VMEM((TAPS, WINDOW, GROUP), BF16),
        pltpu.VMEM((2, 2, 16, 1280), BF16), pltpu.VMEM((2, 2, 16, 1280), BF16),
        pltpu.VMEM((2, 2, 16, 640), BF16), pltpu.VMEM((2, 2, 16, 640), BF16),
        pltpu.VMEM((2, 4, 16, 128), BF16), pltpu.VMEM((2, 4, 16, 128), BF16),
        pltpu.VMEM((16, 640), F32), pltpu.VMEM((2, 16, 640), F32),
        pltpu.VMEM((16, 128), F32), pltpu.VMEM((4, 16, 128), F32),
        *mixed,
        pltpu.VMEM((TAPS, 64, 128), F32),
        dma((3, 2)), dma((3, 2)), dma((3, 2)), dma((3, 2)), dma((3, 4)), dma((3, 4)),
        dma((39,)), dma((39,)), dma((39,)), dma((39,)), dma((5,)),
        pltpu.VMEM(volume.shape[1:], BF16), pltpu.VMEM(volume.shape[1:], BF16),
        *[pltpu.VMEM((27, 64, 64), BF16)] * 3,
        pltpu.VMEM((GROUP, 2 * CI * CJ), BF16),
        pltpu.VMEM((NI + 4, NJ, LANES), F32),
        pltpu.VMEM((TAPS, 32, LANES + 2 * PAD), BF16),
        pltpu.VMEM((16, LANES), F32), pltpu.VMEM((16, 256), F32),
        pltpu.VMEM((2, 16, LANES), F32), pltpu.VMEM((4, 16, 256), F32),
        pltpu.VMEM((2, 3, 16, LANES), F32),
        pltpu.VMEM((2, 16, LANES), BF16), pltpu.VMEM((2, 16, LANES), BF16),
        pltpu.VMEM((4, 16, 256), BF16), pltpu.VMEM((4, 16, 256), BF16),
        pltpu.VMEM((2, 2, NJ, LANES), BF16),
    ]
    block = volume.shape[1:]
    taps = (27, 64, 64)
    kernels = (first_kernel, second_kernel, coarse_kernel)
    operands = (volume[0], cotangent[0], *(k.reshape(taps) for k in kernels))
    field, sc, f = pl.pallas_call(
        kernel,
        out_shape=(
            jax.ShapeDtypeStruct(block, BF16),
            jax.ShapeDtypeStruct((32, 64, 128), BF16),
            jax.ShapeDtypeStruct((32, 32, 128), BF16),
        ),
        in_specs=[in_hbm] * 5,
        out_specs=(in_vmem,) * 3,
        scratch_shapes=scratch,
        compiler_params=pltpu.CompilerParams(
            collective_id=0, has_side_effects=True, vmem_limit_bytes=48 * 1024 * 1024
        ),
        name="block",
    )(*(pltpu.with_memory_space_constraint(v, pltpu.HBM) for v in operands))
    field, first_grad, second_grad, coarse_grad = pl.pallas_call(
        unpack_kernel,
        out_shape=(jax.ShapeDtypeStruct(block, BF16),) + (jax.ShapeDtypeStruct(taps, F32),) * 3,
        in_specs=[in_vmem] * 3,
        out_specs=(in_hbm,) * 4,
        scratch_shapes=[
            *[pltpu.VMEM(taps, F32)] * 3, dma((4,)),
        ],
        compiler_params=pltpu.CompilerParams(vmem_limit_bytes=32 * 1024 * 1024),
        name="unpack",
    )(field, sc, f)
    kernel_shape = first_kernel.shape
    return (
        field[None],
        first_grad.reshape(kernel_shape),
        second_grad.reshape(kernel_shape),
        coarse_grad.reshape(kernel_shape),
    )


def solution(mesh):
    in_specs = (P("dp", "gx", "gy", None), P("dp", "gx", "gy", None), P(), P(), P())
    out_specs = (P("dp", "gx", "gy", None), P(), P(), P())
    return jax.shard_map(
        per_device, mesh=mesh, in_specs=in_specs, out_specs=out_specs, check_vma=False
    )
```

```python
import jax
import jax.numpy as jnp
from jax import lax
from jax.experimental import pallas as pl
from jax.experimental.pallas import tpu as pltpu
from jax.sharding import PartitionSpec as P

MESH = pl.DeviceIdType.MESH

FARTHEST = {
    2: (1,),
    16: sorted(range(1, 16), key=lambda r: -(min(r // 4, 4 - r // 4) + min(r % 4, 4 - r % 4))),
    8: sorted(range(1, 8), key=lambda r: -min(r, 8 - r)),
}
F32 = jnp.float32
BF16 = jnp.bfloat16

NI, NJ, LANES = 8, 16, 1024
CI, CJ, CLANES = 4, 8, 512
PAD = 128
GROUP = 256
WINDOW = 512
TAPS = 9
LOOPED = ('c2', 'g1')


def dot(a, b, dims=((1,), (0,))):
    return lax.dot_general(a, b, (dims, ((), ())), preferred_element_type=F32)


def sigmoid(v):
    return 1.0 / (1.0 + jnp.exp(-v))


def unpack_taps(read, out):
    for t in range(TAPS):
        block = read(t).astype(F32).T
        out[3 * t] = block[0:64]
        out[3 * t + 1] = block[64:128]
    for u in range(5):
        block = read(TAPS + u).astype(F32).T
        out[6 * u + 2] = block[0:64]
        if u < 4:
            out[6 * u + 5] = block[64:128]


def unpack_reversed(read, out):
    for t in range(TAPS):
        block = read(t).astype(F32)
        out[26 - 3 * t] = block[:, 0:64]
        out[25 - 3 * t] = block[:, 64:128]
    for u in range(5):
        block = read(TAPS + u).astype(F32)
        out[24 - 6 * u] = block[:, 0:64]
        if u < 4:
            out[21 - 6 * u] = block[:, 64:128]


def kernel(
    vol_in, cot_in, k1_in, k2_in, kc_in,
    field, out_second, out_coarse, out_f,
    fine_st, coarse_st, xv, xh, xs, xp, xc, slope1, upstream, fine_keep, slopes_t, acc,
    w1, w2, w2b, wc, wcb,
    s_e, r_e, s_n, r_n, s_c, r_c, col, colr, cor, corr,
    part_sc, part_f, in1_sc, in1_f, b2_sc, b2_f, in2_sc, in2_f, in3_sc, in3_f, res_sc, res_f, half,
    se_sem, re_sem, sn_sem, rn_sem, sc_sem, rc_sem,
    s_sc, g_sc, s_f, g_f, in_sem,
    vol, cot, k1, k2, kc,
    pooled_t, hid, xvc, colw, corw, colv, corv, colx, sv_n, rv_n, sv_c, rv_c, rv_e,
):
    loads = [
        pltpu.make_async_copy(src, dst, in_sem.at[n])
        for n, (src, dst) in enumerate(((vol_in, vol), (cot_in, cot), (k1_in, k1), (k2_in, k2), (kc_in, kc)))
    ]
    for load in loads:
        load.start()

    gx, gy, dp = lax.axis_index("gx"), lax.axis_index("gy"), lax.axis_index("dp")
    x_at, z_hi = lax.div(gy, 2), lax.rem(gy, 2)
    z_lo, core = lax.div(gx, 2), lax.rem(gx, 2)
    w_at = x_at * 4 + dp
    z_at = z_hi * 4 + z_lo

    def side(at, step):
        return lax.rem(at + step + 8, 8)

    def near(di, dj):
        return {"gx": side(gx, di), "gy": side(gy, dj)}

    def w_peer(r):
        x, y = lax.rem(x_at + r // 4, 4), lax.rem(dp + r % 4, 4)
        return x * 4 + y, {"gy": x * 2 + z_hi, "dp": y}

    other_core = {"gx": z_lo * 2 + 1 - core}

    def z_peer(r):
        z = lax.rem(z_at + r, 8)
        return z, {"gx": lax.rem(z, 4) * 2 + core, "gy": x_at * 2 + lax.div(z, 4)}

    steps = (-1, 1)
    barrier = pltpu.get_barrier_semaphore()
    partners = [near(s, t) for s in steps for t in steps] + [near(0, s) for s in steps]
    partners += [z_peer(r)[1] for r in FARTHEST[8]] + [w_peer(r)[1] for r in FARTHEST[16]]
    partners += [near(s, 0) for s in steps] + [other_core]
    for partner in partners:
        pl.semaphore_signal(barrier, inc=1, device_id=partner, device_id_type=MESH)

    def pack_coarse(stage):
        for e in range(2):
            row = coarse_st[e * (CI - 1)]
            s_e[stage, e, :, LANES:] = jnp.concatenate([row[:, :256], row[:, 256:]], axis=0).astype(BF16)
        for n in range(2):
            cj = n * (CJ - 1)
            for i in range(CI):
                for k in range(4):
                    col[4 * k + i : 4 * k + i + 1, 512:640] = coarse_st[i, cj : cj + 1, 128 * k : 128 * k + 128]
            s_n[stage, n, :, 512:640] = col[:, 512:640].astype(BF16)
        for e in range(2):
            for n in range(2):
                cj = n * (CJ - 1)
                for k in range(4):
                    cor[8 + k : 9 + k] = coarse_st[e * (CI - 1), cj : cj + 1, 128 * k : 128 * k + 128]
                s_c[stage, 2 * e + n] = cor[...].astype(BF16)

    def pack_fine(stage):
        for e in range(2):
            for n in range(2):
                i, j = e * (NI - 1), n * (NJ - 1)
                for k in range(8):
                    cor[k : k + 1] = fine_st[i, j : j + 1, 128 * k : 128 * k + 128]
                s_c[stage, 2 * e + n] = cor[...].astype(BF16)
        for n in range(2):
            j = n * (NJ - 1)
            for i in range(NI):
                col[i : i + 1, 0:512] = fine_st[i, j : j + 1, 0:512]
                col[NI + i : NI + i + 1, 0:512] = fine_st[i, j : j + 1, 512:1024]
            s_n[stage, n, :, 0:512] = col[:, 0:512].astype(BF16)
        for e in range(2):
            s_e[stage, e, :, 0:LANES] = fine_st[e * (NI - 1)].astype(BF16)

    def pack_volume():
        for n in range(2):
            for i in range(NI):
                for m in range(2):
                    j = n * (NJ - 2) + m
                    colw[NI * m + i : NI * m + i + 1, :] = fine_st[i, j : j + 1, :]
            sv_n[n] = colw[...].astype(BF16)
        for e in range(2):
            for n in range(2):
                for cell in range(4):
                    i, j = e * (NI - 2) + cell // 2, n * (NJ - 2) + cell % 2
                    for k in range(4):
                        corw[4 * k + cell : 4 * k + cell + 1, :] = fine_st[i, j : j + 1, 256 * k : 256 * k + 256]
                sv_c[2 * e + n] = corw[...].astype(BF16)

    gx_low, gx_high, gy_low, gy_high = gx > 0, gx < 7, gy > 0, gy < 7
    to_x, to_y = (gx_low, gx_high), (gy_low, gy_high)

    def to_sides(n_src, n_dst, n_sems, c_src, c_dst, c_sems, e_src, e_dst, e_sems):
        copies = []
        for e in range(2):
            for n in range(2):
                c = 2 * e + n
                copies.append((to_x[e] & to_y[n], to_x[1 - e] & to_y[1 - n], pltpu.make_async_remote_copy(
                    c_src(c), c_dst(c), c_sems[0].at[c], c_sems[1].at[c],
                    device_id=near(steps[e], steps[n]), device_id_type=MESH)))
        for n in range(2):
            copies.append((to_y[n], to_y[1 - n], pltpu.make_async_remote_copy(
                n_src(n), n_dst(n), n_sems[0].at[n], n_sems[1].at[n],
                device_id=near(0, steps[n]), device_id_type=MESH)))
        for e in range(2):
            copies.append((to_x[e], to_x[1 - e], pltpu.make_async_remote_copy(
                e_src(e), e_dst(e), e_sems[0].at[e], e_sems[1].at[e],
                device_id=near(steps[e], 0), device_id_type=MESH)))
        return copies

    def rim_copies(stage, with_fine):
        lanes_e, lanes_n = (pl.ds(0, 1024), pl.ds(0, 512)) if with_fine else (pl.ds(1024, 256), pl.ds(512, 128))
        return to_sides(
            lambda n: s_n.at[stage, n, :, lanes_n], lambda n: r_n.at[stage, n, :, lanes_n], (sn_sem.at[stage], rn_sem.at[stage]),
            lambda c: s_c.at[stage, c], lambda c: r_c.at[stage, c], (sc_sem.at[stage], rc_sem.at[stage]),
            lambda e: s_e.at[stage, e, :, lanes_e], lambda e: r_e.at[stage, e, :, lanes_e], (se_sem.at[stage], re_sem.at[stage]))

    def volume_copies():
        return to_sides(
            lambda n: sv_n.at[n], lambda n: rv_n.at[n], (sn_sem.at[3], rn_sem.at[3]),
            lambda c: sv_c.at[c], lambda c: rv_c.at[c], (sc_sem.at[3], rc_sem.at[3]),
            lambda e: vol.at[pl.ds(e * (NI - 2), 2)], lambda e: rv_e.at[e], (se_sem.at[3], re_sem.at[3]))

    def send(copies):
        for there, _, copy in copies:
            pl.when(there)(copy.start)

    def receive(copies):
        for _, there, copy in copies:
            pl.when(there)(copy.wait_recv)

    def place(dst, index, value, low, high, rows):
        at = lax.broadcasted_iota(jnp.int32, value.shape, 0)
        dst[0, index, :, PAD : PAD + value.shape[1]] = jnp.where(
            at == 0, jnp.broadcast_to(low, value.shape), pltpu.roll(value, 1, 0)).astype(dst.dtype)
        dst[1, index, :, PAD : PAD + value.shape[1]] = value.astype(dst.dtype)
        dst[2, index, :, PAD : PAD + value.shape[1]] = jnp.where(
            at == rows - 1, jnp.broadcast_to(high, value.shape), pltpu.roll(value, rows - 1, 0)).astype(dst.dtype)

    def keep(here, value):
        return jnp.where(here, value, 0.0)

    def unpack_rims(stage):
        for n in range(2):
            colr[n] = r_n[stage, n].astype(F32)
        for c in range(4):
            corr[c] = r_c[stage, c].astype(F32)

    def corner(c, first, count):
        return jnp.concatenate([corr[c, first + k : first + k + 1, :] for k in range(count)], axis=1)

    def assemble_fine(stage, dst):
        def body(i, carry):
            low = jnp.concatenate([colr[1, pl.ds(i, 1), 0:512], colr[1, pl.ds(i + NI, 1), 0:512]], axis=1)
            high = jnp.concatenate([colr[0, pl.ds(i, 1), 0:512], colr[0, pl.ds(i + NI, 1), 0:512]], axis=1)
            place(dst, i + 1, fine_st[i], keep(gy_low, low), keep(gy_high, high), NJ)
            return carry

        lax.fori_loop(0, NI, body, 0)
        for e, index, here in ((1, 0, gx_low), (0, NI + 1, gx_high)):
            value = keep(here, r_e[stage, e, :, 0:LANES].astype(F32))
            low = keep(here & gy_low, corner(2 * e + 1, 0, 8))
            high = keep(here & gy_high, corner(2 * e, 0, 8))
            place(dst, index, value, low, high, NJ)

    def assemble_volume():
        for n in range(2):
            colv[n] = rv_n[n].astype(F32)
        for c in range(4):
            corv[c] = rv_c[c].astype(F32)

        def body(i, carry):
            low, high = colv[1, pl.ds(i + NI, 1), :], colv[0, pl.ds(i, 1), :]
            place(xv, i + 2, fine_st[i], keep(gy_low, low), keep(gy_high, high), NJ)
            return carry

        lax.fori_loop(0, NI, body, 0)

        def cells(c, cell):
            return jnp.concatenate([corv[c, 4 * k + cell : 4 * k + cell + 1, :] for k in range(4)], axis=1)

        for m in range(2):
            colx[0, m, 2:10, :] = keep(gy_low, colv[1, NI * m : NI * m + NI, :])
            colx[1, 1 + m, 2:10, :] = keep(gy_high, colv[0, NI * m : NI * m + NI, :])
        for i in range(NI):
            colx[0, 2, i + 2 : i + 3, :] = fine_st[i, 0:1, :]
            colx[1, 0, i + 2 : i + 3, :] = fine_st[i, NJ - 1 : NJ, :]
        for e, first_row, here in ((1, 0, gx_low), (0, NI + 2, gx_high)):
            for m in range(2):
                at = first_row + m
                value = keep(here, rv_e[e, m].astype(F32))
                low = [keep(here & gy_low, cells(2 * e + 1, 2 * m + j)) for j in range(2)]
                high = [keep(here & gy_high, cells(2 * e, 2 * m + j)) for j in range(2)]
                place(xv, at, value, low[1], high[0], NJ)
                for j in range(2):
                    colx[0, j, at : at + 1, :] = low[j]
                    colx[1, 1 + j, at : at + 1, :] = high[j]
                colx[0, 2, at : at + 1, :] = value[0:1]
                colx[1, 0, at : at + 1, :] = value[NJ - 1 : NJ]
        for a in range(3):
            for b in range(3):
                for m in range(2):
                    strip = colx[m, b]
                    strip = strip if a == 0 else pltpu.roll(strip, 16 - a, 0)
                    xvc[3 * a + b, 16 * m : 16 * m + 16, PAD : PAD + LANES] = strip.astype(BF16)

    def assemble_hidden():
        def body(at, carry):
            here = ((at > 0) | gx_low) & ((at < NI + 1) | gx_high)
            low, high = hid[NI + 2, pl.ds(at, 1), :], hid[NI + 3, pl.ds(at, 1), :]
            place(xh, at, keep(here, hid[at]), keep(here & gy_low, low), keep(here & gy_high, high), NJ)
            return carry

        lax.fori_loop(0, NI + 2, body, 0)

    def assemble_coarse(stage, dst):
        for i in range(CI):
            low = jnp.concatenate([colr[1, 4 * k + i : 4 * k + i + 1, 512:640] for k in range(4)], axis=1)
            high = jnp.concatenate([colr[0, 4 * k + i : 4 * k + i + 1, 512:640] for k in range(4)], axis=1)
            place(dst, i + 1, coarse_st[i], keep(gy_low, low), keep(gy_high, high), CJ)
        for e, index, here in ((1, 0, gx_low), (0, CI + 1, gx_high)):
            row = r_e[stage, e, :, LANES:].astype(F32)
            value = keep(here, jnp.concatenate([row[:CJ], row[CJ:]], axis=1))
            low = keep(here & gy_low, corner(2 * e + 1, 8, 4))
            high = keep(here & gy_high, corner(2 * e, 8, 4))
            place(dst, index, value, low, high, CJ)

    def wide_window(a, b):
        parts = []
        for g in range(4):
            lanes = slice(GROUP * g, GROUP * g + WINDOW)
            parts += [xv[b, pl.ds(a, NI + 2), :, lanes].reshape((NI + 2) * NJ, WINDOW), xvc[3 * a + b, :, lanes]]
        return jnp.concatenate(parts, axis=0)

    def fine_window(src, a, b):
        return jnp.concatenate(
            [src[b, pl.ds(a, NI), :, GROUP * g : GROUP * g + WINDOW].reshape(NI * NJ, WINDOW) for g in range(4)], axis=0)

    def coarse_window(src, a, b):
        return jnp.concatenate(
            [src[b, pl.ds(a, CI), :, GROUP * g : GROUP * g + WINDOW].reshape(CI * CJ, WINDOW) for g in range(2)],
            axis=0).astype(BF16)

    def three(body, looped):
        if looped:
            lax.fori_loop(0, 3, body, 0)
        else:
            for a in range(3):
                body(a, 0)

    def conv(window, weights, rows, looped):
        if not looped:
            total = dot(window(0, 0), weights[0])
            for t in range(1, TAPS):
                total = total + dot(window(t // 3, t % 3), weights[t])
            return total
        acc[0:rows] = jnp.zeros((rows, GROUP), F32)

        def body(a, carry):
            total = acc[0:rows]
            for b in range(3):
                total = total + dot(window(a, b), weights[3 * a + b])
            acc[0:rows] = total
            return carry

        lax.fori_loop(0, 3, body, 0)
        return acc[0:rows]

    def joined(window, weights):
        wide = jnp.concatenate([window(t // 3, t % 3) for t in range(TAPS)], axis=1)
        return dot(wide, weights[...].reshape(TAPS * WINDOW, GROUP))

    def by_group(window, weights, rows):
        def body(g, carry):
            lanes = pl.ds(pl.multiple_of(g * GROUP, GROUP), WINDOW)
            total = dot(window(0, 0, lanes), weights[0])
            for t in range(1, TAPS):
                total = total + dot(window(t // 3, t % 3, lanes), weights[t])
            acc[pl.ds(pl.multiple_of(g * rows, 16), rows)] = total
            return carry

        lax.fori_loop(0, 4, body, 0)
        return acc[0 : 4 * rows]

    def group_window(src):
        return lambda a, b, lanes: src[b, a : a + NI, :, lanes].reshape(NI * NJ, WINDOW)

    def wide_group_window(a, b, lanes):
        own = xv[b, a : a + NI + 2, :, lanes].reshape((NI + 2) * NJ, WINDOW)
        return jnp.concatenate([own, xvc[3 * a + b, :, lanes]], axis=0)

    def grads(window, slopes, store, looped):
        def body(a, carry):
            for b in range(3):
                g = dot(slopes[...], window(a, b))
                even = g[0:64, 0:384] + g[128:192, 128:512]
                odd = g[64:128, 128:384] + g[192:256, 256:512]
                shifted = jnp.concatenate([even[:, 64:192], even[:, 192:320]], axis=1)
                total = odd + shifted
                store(3 * a + b, total[:, 0:128].astype(BF16))
                half[3 * a + b] = total[:, 128:256]
            return carry

        three(body, looped)
        lane = lax.broadcasted_iota(jnp.int32, (64, 128), 1)
        for u in range(5):
            left = half[2 * u]
            right = pltpu.roll(half[2 * u + 1], 64, 1) if u < 4 else jnp.zeros_like(left)
            store(TAPS + u, jnp.where(lane < 64, left, right).astype(BF16))

    def pool_matrix(rows, columns, flip):
        r = lax.broadcasted_iota(jnp.int32, (rows, columns), 1 if flip else 0)
        s = lax.broadcasted_iota(jnp.int32, (rows, columns), 0 if flip else 1)
        r = r & 31
        return jnp.where(r == (s >> 5) * 8 + ((s & 15) >> 1), 1.0, 0.0).astype(BF16)

    def pool(value):
        sums = dot(pool_matrix(32, 128, False), value)
        lane = lax.broadcasted_iota(jnp.int32, (32, 128), 1)
        tiles = []
        for k in range(4):
            pair = []
            for m in range(2):
                tile = sums[:, 256 * k + 128 * m : 256 * k + 128 * m + 128]
                pair.append(tile + pltpu.roll(tile, 64, 1))
            tiles.append(jnp.where(lane < 64, pair[0], pair[1]))
        return jnp.concatenate(tiles, axis=1).reshape(CI, CJ, CLANES)

    def spread(value):
        lane = lax.broadcasted_iota(jnp.int32, (32, 128), 1)
        tiles = []
        for k in range(4):
            tile = value[:, 128 * k : 128 * k + 128]
            turned = pltpu.roll(tile, 64, 1)
            tiles += [jnp.where(lane < 64, tile, turned), jnp.where(lane < 64, turned, tile)]
        return jnp.concatenate(tiles, axis=1)

    def ungroup(value, rows):
        return jnp.concatenate([value[rows * g : rows * (g + 1)] for g in range(value.shape[0] // rows)], axis=1)

    def make_sum(part, in1, b2, in2, in3, res, send, got):
        def c1(r):
            return pltpu.make_async_remote_copy(part.at[pl.ds((1 - core) * 16, 16)], in1, send.at[0], got.at[0],
                                                device_id=other_core, device_id_type=MESH)

        def c2(r):
            w, peer = w_peer(r)
            return pltpu.make_async_remote_copy(b2.at[w], in2.at[r - 1], send.at[r], got.at[r],
                                                device_id=peer, device_id_type=MESH)

        def c3(r):
            _, peer = z_peer(r)
            return pltpu.make_async_remote_copy(in3.at[z_at], in3.at[z_at], send.at[15 + r], got.at[15 + r],
                                                device_id=peer, device_id_type=MESH)

        mine = core * 16 + w_at

        def c4(r):
            _, peer = w_peer(r)
            return pltpu.make_async_remote_copy(res.at[mine], res.at[mine], send.at[22 + r], got.at[22 + r],
                                                device_id=peer, device_id_type=MESH)

        def c5(r):
            own = pl.ds(core * 16, 16)
            return pltpu.make_async_remote_copy(res.at[own], res.at[own], send.at[38], got.at[38],
                                                device_id=other_core, device_id_type=MESH)

        def start(make, count):
            for r in FARTHEST[count]:
                make(r).start()

        def finish(make, count):
            for r in range(1, count):
                make(r).wait_recv()

        def s1():
            start(c1, 2)

        def s2():
            finish(c1, 2)
            b2[...] = (part[pl.ds(core * 16, 16)].astype(F32) + in1[...].astype(F32)).astype(BF16)
            start(c2, 16)

        def s3():
            finish(c2, 16)
            total = b2[w_at].astype(F32)
            for r in range(15):
                total = total + in2[r].astype(F32)
            in3[z_at] = total.astype(BF16)
            start(c3, 8)

        def s4():
            finish(c3, 8)
            total = in3[0].astype(F32)
            for r in range(1, 8):
                total = total + in3[r].astype(F32)
            res[mine] = total.astype(BF16)
            start(c4, 16)

        def s5():
            finish(c4, 16)
            start(c5, 2)

        def s6():
            finish(c5, 2)

        def s7():
            for make, count in ((c1, 2), (c2, 16), (c3, 8), (c4, 16), (c5, 2)):
                for r in range(1, count):
                    make(r).wait_send()

        return s1, s2, s3, s4, s5, s6, s7

    sum_sc = make_sum(part_sc, in1_sc, b2_sc, in2_sc, in3_sc, res_sc, s_sc, g_sc)
    sum_f = make_sum(part_f, in1_f, b2_f, in2_f, in3_f, res_f, s_f, g_f)

    cor[...] = jnp.zeros_like(cor)
    col[...] = jnp.zeros_like(col)
    loads[1].wait()
    coarse_st[...] = pool(cot[...].reshape(NI * NJ, LANES)).astype(BF16).astype(F32)
    pack_coarse(0)
    loads[0].wait()
    fine_st[...] = vol[...].astype(F32)
    pack_volume()
    pl.semaphore_wait(barrier, len(partners))
    send(rim_copies(0, False))
    send(volume_copies())

    def build(k, fwd, bwd):
        for w in (fwd, bwd):
            if w is not None:
                w[...] = jnp.zeros_like(w)

        def band(w, t, c0, c1, c2):
            zero = jnp.zeros_like(c0)
            pairs = ((c0, zero), (c1, c0), (c2, c1), (zero, c2))
            for m, tile in enumerate(jnp.concatenate(pair, axis=1) for pair in pairs):
                for pair in range(2):
                    row = 64 * (2 * pair + 1 + m)
                    w[t, row : row + 64, 128 * pair : 128 * pair + 128] = tile

        def body(t, carry):
            taps = [k[3 * t + c] for c in range(3)]
            band(fwd, t, *taps)
            if bwd is not None:
                c0, c1, c2 = (v.astype(F32).T.astype(BF16) for v in taps)
                band(bwd, 8 - t, c2, c1, c0)
            return carry

        lax.fori_loop(0, TAPS, body, 0)

    loads[2].wait()
    build(k1, w1, None)
    loads[3].wait()
    build(k2, w2, w2b)
    loads[4].wait()
    build(kc, wc, wcb)
    for padded in (xv, xh, xs, xp, xc):
        rows, tail = padded.shape[2], padded.shape[3] - PAD
        padded[:, :, :, 0:PAD] = jnp.zeros((3, padded.shape[1], rows, PAD), padded.dtype)
        padded[:, :, :, tail:] = jnp.zeros((3, padded.shape[1], rows, PAD), padded.dtype)
    xvc[:, :, 0:PAD] = jnp.zeros((TAPS, 32, PAD), BF16)
    xvc[:, :, PAD + LANES :] = jnp.zeros((TAPS, 32, PAD), BF16)
    part_sc[28:32] = jnp.zeros((4, 64, 128), BF16)
    part_f[28:32] = jnp.zeros((4, 32, 128), BF16)

    def widen(value):
        wide = spread(value)
        top = wide.astype(BF16)
        rest = (wide - top.astype(F32)).astype(BF16)
        return dot(pool_matrix(128, 64, True), jnp.concatenate([top, rest], axis=0))

    receive(rim_copies(0, False))
    unpack_rims(0)
    assemble_coarse(0, xc)
    pooled_slope = ungroup(joined(lambda a, b: coarse_window(xc, a, b), wcb), CI * CJ)
    upstream[...] = (cot[...].reshape(NI * NJ, LANES).astype(F32) + widen(pooled_slope) * 0.125).astype(BF16).astype(F32)

    receive(volume_copies())
    assemble_volume()

    first = ungroup(conv(wide_window, w1, 4 * (NI + 4) * NJ, 'c1' in LOOPED), (NI + 4) * NJ)
    sigma = sigmoid(first)
    hid[...] = (first * sigma).astype(BF16).astype(F32).reshape(NI + 4, NJ, LANES)
    own, own_sigma = first[NJ : NJ + NI * NJ], sigma[NJ : NJ + NI * NJ]
    slope1[...] = own_sigma * (1.0 + own * (1.0 - own_sigma))
    assemble_hidden()

    second = ungroup(conv(lambda a, b: fine_window(xh, a, b), w2, 4 * NI * NJ, 'c2' in LOOPED), NI * NJ)
    sigma = sigmoid(second)
    second_slope = (upstream[...] * (sigma * (1.0 + second * (1.0 - sigma)))).astype(BF16).astype(F32)
    fine_st[...] = second_slope.reshape(NI, NJ, LANES)
    pack_fine(1)
    send(rim_copies(1, True))
    fine = (second * sigma).astype(BF16)
    fine_keep[...] = fine
    coarse_st[...] = (pool(fine) * 0.125).astype(BF16).astype(F32)
    pack_coarse(2)
    send(rim_copies(2, False))

    def grouped_t(value, groups):
        return jnp.concatenate([value[:, GROUP * g : GROUP * (g + 1)] for g in range(groups)], axis=0).T.astype(BF16)

    slopes_t[...] = grouped_t(fine_st[...].reshape(NI * NJ, LANES), 4)

    def store_second(n, value):
        part_sc[n] = value

    def store_coarse(n, value):
        part_sc[14 + n] = value

    def store_first(n, value):
        part_f[pl.ds(2 * n, 2)] = value.reshape(2, 32, 128)

    grads(lambda a, b: fine_window(xh, a, b), slopes_t, store_second, 'g2' in LOOPED)
    pooled_t[...] = grouped_t(coarse_st[...].reshape(CI * CJ, CLANES), 2)
    grads(lambda a, b: coarse_window(xc, a, b), pooled_t, store_coarse, 'gc' in LOOPED)
    sum_sc[0]()
    sum_sc[1]()

    receive(rim_copies(1, True))
    unpack_rims(1)
    assemble_fine(1, xs)

    hidden_slope = ungroup(conv(lambda a, b: fine_window(xs, a, b), w2b, 4 * NI * NJ, 'c3' in LOOPED), NI * NJ)
    first_slope = (hidden_slope * slope1[...]).astype(BF16).astype(F32)
    slopes_t[...] = grouped_t(first_slope, 4)
    grads(lambda a, b: fine_window(xv, a + 1, b), slopes_t, store_first, 'g1' in LOOPED)
    sum_f[0]()
    sum_sc[2]()
    sum_f[1]()

    receive(rim_copies(2, False))
    unpack_rims(2)
    assemble_coarse(2, xp)
    coarse = ungroup(joined(lambda a, b: coarse_window(xp, a, b), wc), CI * CJ).astype(BF16)
    wide = spread(coarse.astype(F32)).astype(BF16)
    repeated = dot(pool_matrix(128, 32, True), wide)
    field[...] = (fine_keep[...].astype(F32) + repeated).astype(BF16).reshape(NI, NJ, LANES)

    sum_sc[3]()
    sum_f[2]()
    sum_f[3]()
    sum_sc[4]()
    sum_f[4]()
    sum_sc[5]()
    unpack_taps(lambda n: res_sc[n], out_second)
    unpack_reversed(lambda n: res_sc[14 + n], out_coarse)
    sum_f[5]()
    out_f[...] = res_f[...]
    sum_sc[6]()
    sum_f[6]()
    for there, _, copy in rim_copies(0, False) + volume_copies() + rim_copies(1, True) + rim_copies(2, False):
        pl.when(there)(copy.wait_send)


def unpack_kernel(held, second, coarse, f, field, first_out, second_out, coarse_out, first_grad, sem):
    copies = [
        pltpu.make_async_copy(src, dst, sem.at[n])
        for n, (src, dst) in enumerate((
            (held, field), (second, second_out), (coarse, coarse_out), (first_grad, first_out),
        ))
    ]
    for copy in copies[:3]:
        copy.start()
    unpack_taps(lambda n: f[2 * n : 2 * n + 2].reshape(64, 128), first_grad)
    copies[3].start()
    for copy in copies:
        copy.wait()


def per_device(volume, cotangent, first_kernel, second_kernel, coarse_kernel):
    in_hbm, in_vmem = (pl.BlockSpec(memory_space=space) for space in (pltpu.HBM, pltpu.VMEM))
    dma = pltpu.SemaphoreType.DMA

    def sum_buffers(rows):
        return [
            pltpu.VMEM((32, rows, 128), BF16), pltpu.VMEM((16, rows, 128), BF16), pltpu.VMEM((16, rows, 128), BF16),
            pltpu.VMEM((15, rows, 128), BF16), pltpu.VMEM((8, rows, 128), BF16), pltpu.VMEM((32, rows, 128), BF16),
        ]

    sc_bufs, f_bufs = sum_buffers(64), sum_buffers(32)
    mixed = [b for pair in zip(sc_bufs, f_bufs) for b in pair]
    scratch = [
        pltpu.VMEM((NI, NJ, LANES), F32),
        pltpu.VMEM((CI, CJ, CLANES), F32),
        pltpu.VMEM((3, NI + 4, NJ, LANES + 2 * PAD), BF16),
        pltpu.VMEM((3, NI + 2, NJ, LANES + 2 * PAD), BF16),
        pltpu.VMEM((3, NI + 2, NJ, LANES + 2 * PAD), BF16),
        pltpu.VMEM((3, CI + 2, CJ, CLANES + 2 * PAD), F32),
        pltpu.VMEM((3, CI + 2, CJ, CLANES + 2 * PAD), F32),
        pltpu.VMEM((NI * NJ, LANES), F32),
        pltpu.VMEM((NI * NJ, LANES), F32),
        pltpu.VMEM((NI * NJ, LANES), BF16),
        pltpu.VMEM((GROUP, 4 * NI * NJ), BF16),
        pltpu.VMEM((4 * (NI + 4) * NJ, GROUP), F32),
        pltpu.VMEM((TAPS, WINDOW, GROUP), BF16),
        pltpu.VMEM((TAPS, WINDOW, GROUP), BF16),
        pltpu.VMEM((TAPS, WINDOW, GROUP), BF16),
        pltpu.VMEM((TAPS, WINDOW, GROUP), BF16),
        pltpu.VMEM((TAPS, WINDOW, GROUP), BF16),
        pltpu.VMEM((3, 2, 16, 1280), BF16), pltpu.VMEM((3, 2, 16, 1280), BF16),
        pltpu.VMEM((3, 2, 16, 640), BF16), pltpu.VMEM((3, 2, 16, 640), BF16),
        pltpu.VMEM((3, 4, 16, 128), BF16), pltpu.VMEM((3, 4, 16, 128), BF16),
        pltpu.VMEM((16, 640), F32), pltpu.VMEM((2, 16, 640), F32),
        pltpu.VMEM((16, 128), F32), pltpu.VMEM((4, 16, 128), F32),
        *mixed,
        pltpu.VMEM((TAPS, 64, 128), F32),
        dma((4, 2)), dma((4, 2)), dma((4, 2)), dma((4, 2)), dma((4, 4)), dma((4, 4)),
        dma((39,)), dma((39,)), dma((39,)), dma((39,)), dma((5,)),
        pltpu.VMEM(volume.shape[1:], BF16), pltpu.VMEM(volume.shape[1:], BF16),
        *[pltpu.VMEM((27, 64, 64), BF16)] * 3,
        pltpu.VMEM((GROUP, 2 * CI * CJ), BF16),
        pltpu.VMEM((NI + 4, NJ, LANES), F32),
        pltpu.VMEM((TAPS, 32, LANES + 2 * PAD), BF16),
        pltpu.VMEM((16, LANES), F32), pltpu.VMEM((16, 256), F32),
        pltpu.VMEM((2, 16, LANES), F32), pltpu.VMEM((4, 16, 256), F32),
        pltpu.VMEM((2, 3, 16, LANES), F32),
        pltpu.VMEM((2, 16, LANES), BF16), pltpu.VMEM((2, 16, LANES), BF16),
        pltpu.VMEM((4, 16, 256), BF16), pltpu.VMEM((4, 16, 256), BF16),
        pltpu.VMEM((2, 2, NJ, LANES), BF16),
    ]
    block = volume.shape[1:]
    taps = (27, 64, 64)
    kernels = (first_kernel, second_kernel, coarse_kernel)
    operands = (volume[0], cotangent[0], *(k.reshape(taps) for k in kernels))
    field, second_grad, coarse_grad, f = pl.pallas_call(
        kernel,
        out_shape=(
            jax.ShapeDtypeStruct(block, BF16),
            jax.ShapeDtypeStruct(taps, F32),
            jax.ShapeDtypeStruct(taps, F32),
            jax.ShapeDtypeStruct((32, 32, 128), BF16),
        ),
        in_specs=[in_hbm] * 5,
        out_specs=(in_vmem,) * 4,
        scratch_shapes=scratch,
        compiler_params=pltpu.CompilerParams(
            collective_id=0, has_side_effects=True, vmem_limit_bytes=48 * 1024 * 1024
        ),
        name="block",
    )(*(pltpu.with_memory_space_constraint(v, pltpu.HBM) for v in operands))
    field, first_grad, second_grad, coarse_grad = pl.pallas_call(
        unpack_kernel,
        out_shape=(jax.ShapeDtypeStruct(block, BF16),) + (jax.ShapeDtypeStruct(taps, F32),) * 3,
        in_specs=[in_vmem] * 4,
        out_specs=(in_hbm,) * 4,
        scratch_shapes=[
            pltpu.VMEM(taps, F32), dma((4,)),
        ],
        compiler_params=pltpu.CompilerParams(vmem_limit_bytes=32 * 1024 * 1024),
        name="unpack",
    )(field, second_grad, coarse_grad, f)
    kernel_shape = first_kernel.shape
    return (
        field[None],
        first_grad.reshape(kernel_shape),
        second_grad.reshape(kernel_shape),
        coarse_grad.reshape(kernel_shape),
    )


def solution(mesh):
    in_specs = (P("dp", "gx", "gy", None), P("dp", "gx", "gy", None), P(), P(), P())
    out_specs = (P("dp", "gx", "gy", None), P(), P(), P())
    return jax.shard_map(
        per_device, mesh=mesh, in_specs=in_specs, out_specs=out_specs, check_vma=False
    )
```

```python
import jax
import jax.numpy as jnp
from jax import lax
from jax.experimental import pallas as pl
from jax.experimental.pallas import tpu as pltpu
from jax.sharding import PartitionSpec as P

MESH = pl.DeviceIdType.MESH

FARTHEST = {
    2: (1,),
    16: sorted(range(1, 16), key=lambda r: -(min(r // 4, 4 - r // 4) + min(r % 4, 4 - r % 4))),
    8: sorted(range(1, 8), key=lambda r: -min(r, 8 - r)),
}
F32 = jnp.float32
BF16 = jnp.bfloat16

NI, NJ, LANES = 8, 16, 1024
CI, CJ, CLANES = 4, 8, 512
PAD = 128
GROUP = 256
WINDOW = 512
TAPS = 9
LOOPED = ('c2', 'g1', 'c3')


def dot(a, b, dims=((1,), (0,))):
    return lax.dot_general(a, b, (dims, ((), ())), preferred_element_type=F32)


def sigmoid(v):
    return 1.0 / (1.0 + jnp.exp(-v))


def unpack_taps(read, out):
    for t in range(TAPS):
        block = read(t).astype(F32).T
        out[3 * t] = block[0:64]
        out[3 * t + 1] = block[64:128]
    for u in range(5):
        block = read(TAPS + u).astype(F32).T
        out[6 * u + 2] = block[0:64]
        if u < 4:
            out[6 * u + 5] = block[64:128]


def unpack_reversed(read, out):
    for t in range(TAPS):
        block = read(t).astype(F32)
        out[26 - 3 * t] = block[:, 0:64]
        out[25 - 3 * t] = block[:, 64:128]
    for u in range(5):
        block = read(TAPS + u).astype(F32)
        out[24 - 6 * u] = block[:, 0:64]
        if u < 4:
            out[21 - 6 * u] = block[:, 64:128]


def kernel(
    vol_in, cot_in, k1_in, k2_in, kc_in,
    field, out_second, out_coarse, out_f,
    fine_st, coarse_st, xv, xh, xs, xp, xc, slope1, upstream, fine_keep, slopes_t, acc,
    w1, w2, w2b, wc, wcb,
    s_e, r_e, s_n, r_n, s_c, r_c, col, colr, cor, corr,
    part_sc, part_f, in1_sc, in1_f, b2_sc, b2_f, in2_sc, in2_f, in3_sc, in3_f, res_sc, res_f, half,
    se_sem, re_sem, sn_sem, rn_sem, sc_sem, rc_sem,
    s_sc, g_sc, s_f, g_f, in_sem,
    vol, cot, k1, k2, kc,
    strips, pooled_t, hid, xvc, colw, corw, colv, corv, colx, sv_n, rv_n, sv_c, rv_c, rv_e,
):
    loads = [
        pltpu.make_async_copy(src, dst, in_sem.at[n])
        for n, (src, dst) in enumerate(((vol_in, vol), (cot_in, cot), (k1_in, k1), (k2_in, k2), (kc_in, kc)))
    ]
    for load in loads:
        load.start()

    gx, gy, dp = lax.axis_index("gx"), lax.axis_index("gy"), lax.axis_index("dp")
    x_at, z_hi = lax.div(gy, 2), lax.rem(gy, 2)
    z_lo, core = lax.div(gx, 2), lax.rem(gx, 2)
    w_at = x_at * 4 + dp
    z_at = z_hi * 4 + z_lo

    def side(at, step):
        return lax.rem(at + step + 8, 8)

    def near(di, dj):
        return {"gx": side(gx, di), "gy": side(gy, dj)}

    def w_peer(r):
        x, y = lax.rem(x_at + r // 4, 4), lax.rem(dp + r % 4, 4)
        return x * 4 + y, {"gy": x * 2 + z_hi, "dp": y}

    other_core = {"gx": z_lo * 2 + 1 - core}

    def z_peer(r):
        z = lax.rem(z_at + r, 8)
        return z, {"gx": lax.rem(z, 4) * 2 + core, "gy": x_at * 2 + lax.div(z, 4)}

    steps = (-1, 1)
    barrier = pltpu.get_barrier_semaphore()
    partners = [near(s, t) for s in steps for t in steps] + [near(0, s) for s in steps]
    partners += [z_peer(r)[1] for r in FARTHEST[8]] + [w_peer(r)[1] for r in FARTHEST[16]]
    partners += [near(s, 0) for s in steps] + [other_core]
    for partner in partners:
        pl.semaphore_signal(barrier, inc=1, device_id=partner, device_id_type=MESH)

    def pack_coarse(stage):
        for e in range(2):
            row = coarse_st[e * (CI - 1)]
            s_e[stage, e, :, LANES:] = jnp.concatenate([row[:, :256], row[:, 256:]], axis=0).astype(BF16)
        for n in range(2):
            cj = n * (CJ - 1)
            for i in range(CI):
                for k in range(4):
                    col[4 * k + i : 4 * k + i + 1, 512:640] = coarse_st[i, cj : cj + 1, 128 * k : 128 * k + 128]
            s_n[stage, n, :, 512:640] = col[:, 512:640].astype(BF16)
        for e in range(2):
            for n in range(2):
                cj = n * (CJ - 1)
                for k in range(4):
                    cor[8 + k : 9 + k] = coarse_st[e * (CI - 1), cj : cj + 1, 128 * k : 128 * k + 128]
                s_c[stage, 2 * e + n] = cor[...].astype(BF16)

    def pack_fine(stage):
        for e in range(2):
            for n in range(2):
                i, j = e * (NI - 1), n * (NJ - 1)
                for k in range(8):
                    cor[k : k + 1] = fine_st[i, j : j + 1, 128 * k : 128 * k + 128]
                s_c[stage, 2 * e + n] = cor[...].astype(BF16)
        for n in range(2):
            j = n * (NJ - 1)
            for i in range(NI):
                col[i : i + 1, 0:512] = fine_st[i, j : j + 1, 0:512]
                col[NI + i : NI + i + 1, 0:512] = fine_st[i, j : j + 1, 512:1024]
            s_n[stage, n, :, 0:512] = col[:, 0:512].astype(BF16)
        for e in range(2):
            s_e[stage, e, :, 0:LANES] = fine_st[e * (NI - 1)].astype(BF16)

    def pack_volume():
        for n in range(2):
            for i in range(NI):
                for m in range(2):
                    j = n * (NJ - 2) + m
                    colw[NI * m + i : NI * m + i + 1, :] = fine_st[i, j : j + 1, :]
            sv_n[n] = colw[...].astype(BF16)
        for e in range(2):
            for n in range(2):
                for cell in range(4):
                    i, j = e * (NI - 2) + cell // 2, n * (NJ - 2) + cell % 2
                    for k in range(4):
                        corw[4 * k + cell : 4 * k + cell + 1, :] = fine_st[i, j : j + 1, 256 * k : 256 * k + 256]
                sv_c[2 * e + n] = corw[...].astype(BF16)

    gx_low, gx_high, gy_low, gy_high = gx > 0, gx < 7, gy > 0, gy < 7
    to_x, to_y = (gx_low, gx_high), (gy_low, gy_high)

    def to_sides(n_src, n_dst, n_sems, c_src, c_dst, c_sems, e_src, e_dst, e_sems):
        copies = []
        for e in range(2):
            for n in range(2):
                c = 2 * e + n
                copies.append((to_x[e] & to_y[n], to_x[1 - e] & to_y[1 - n], pltpu.make_async_remote_copy(
                    c_src(c), c_dst(c), c_sems[0].at[c], c_sems[1].at[c],
                    device_id=near(steps[e], steps[n]), device_id_type=MESH)))
        for n in range(2):
            copies.append((to_y[n], to_y[1 - n], pltpu.make_async_remote_copy(
                n_src(n), n_dst(n), n_sems[0].at[n], n_sems[1].at[n],
                device_id=near(0, steps[n]), device_id_type=MESH)))
        for e in range(2):
            copies.append((to_x[e], to_x[1 - e], pltpu.make_async_remote_copy(
                e_src(e), e_dst(e), e_sems[0].at[e], e_sems[1].at[e],
                device_id=near(steps[e], 0), device_id_type=MESH)))
        return copies

    def rim_copies(stage, with_fine):
        lanes_e, lanes_n = (pl.ds(0, 1024), pl.ds(0, 512)) if with_fine else (pl.ds(1024, 256), pl.ds(512, 128))
        return to_sides(
            lambda n: s_n.at[stage, n, :, lanes_n], lambda n: r_n.at[stage, n, :, lanes_n], (sn_sem.at[stage], rn_sem.at[stage]),
            lambda c: s_c.at[stage, c], lambda c: r_c.at[stage, c], (sc_sem.at[stage], rc_sem.at[stage]),
            lambda e: s_e.at[stage, e, :, lanes_e], lambda e: r_e.at[stage, e, :, lanes_e], (se_sem.at[stage], re_sem.at[stage]))

    def volume_copies():
        return to_sides(
            lambda n: sv_n.at[n], lambda n: rv_n.at[n], (sn_sem.at[3], rn_sem.at[3]),
            lambda c: sv_c.at[c], lambda c: rv_c.at[c], (sc_sem.at[3], rc_sem.at[3]),
            lambda e: vol.at[pl.ds(e * (NI - 2), 2)], lambda e: rv_e.at[e], (se_sem.at[3], re_sem.at[3]))

    def send(copies):
        for there, _, copy in copies:
            pl.when(there)(copy.start)

    def receive(copies):
        for _, there, copy in copies:
            pl.when(there)(copy.wait_recv)

    def place(dst, index, value, low, high, rows):
        at = lax.broadcasted_iota(jnp.int32, value.shape, 0)
        dst[0, index, :, PAD : PAD + value.shape[1]] = jnp.where(
            at == 0, jnp.broadcast_to(low, value.shape), pltpu.roll(value, 1, 0)).astype(dst.dtype)
        dst[1, index, :, PAD : PAD + value.shape[1]] = value.astype(dst.dtype)
        dst[2, index, :, PAD : PAD + value.shape[1]] = jnp.where(
            at == rows - 1, jnp.broadcast_to(high, value.shape), pltpu.roll(value, rows - 1, 0)).astype(dst.dtype)

    def keep(here, value):
        return jnp.where(here, value, 0.0)

    def unpack_rims(stage):
        for n in range(2):
            colr[n] = r_n[stage, n].astype(F32)
        for c in range(4):
            corr[c] = r_c[stage, c].astype(F32)

    def corner(c, first, count):
        return jnp.concatenate([corr[c, first + k : first + k + 1, :] for k in range(count)], axis=1)

    def assemble_rows(stage, dst):
        none = jnp.zeros((1, LANES), F32)

        def body(i, carry):
            place(dst, i + 1, fine_st[i], none, none, NJ)
            return carry

        lax.fori_loop(0, NI, body, 0)
        for e, index, here in ((1, 0, gx_low), (0, NI + 1, gx_high)):
            place(dst, index, keep(here, r_e[stage, e, :, 0:LANES].astype(F32)), none, none, NJ)

    def assemble_strips():
        strips[:, :, 0:PAD] = jnp.zeros((2, 16, PAD), F32)
        strips[:, :, PAD + LANES :] = jnp.zeros((2, 16, PAD), F32)
        for m, there in ((0, gy_low), (1, gy_high)):
            n = 1 - m
            value = jnp.concatenate([colr[n, 0:NI, 0:512], colr[n, NI : 2 * NI, 0:512]], axis=1)
            strips[m, 1 : NI + 1, PAD : PAD + LANES] = keep(there, value)
            strips[m, 0:1, PAD : PAD + LANES] = keep(there & gx_low, corner(2 + n, 0, 8))
            strips[m, NI + 1 : NI + 2, PAD : PAD + LANES] = keep(there & gx_high, corner(n, 0, 8))

    def add_strips(weights):
        for m in range(2):
            total = None
            for a in range(3):
                window = jnp.concatenate(
                    [strips[m, a : a + NI, GROUP * g : GROUP * g + WINDOW] for g in range(4)], axis=0).astype(BF16)
                part = dot(window, weights[3 * a + 2 * m])
                total = part if a == 0 else total + part
            for g in range(4):
                for i in range(NI):
                    row = g * NI * NJ + i * NJ + m * (NJ - 1)
                    acc[row : row + 1, :] += total[g * NI + i : g * NI + i + 1, :]

    def assemble_volume():
        for n in range(2):
            colv[n] = rv_n[n].astype(F32)
        for c in range(4):
            corv[c] = rv_c[c].astype(F32)

        def body(i, carry):
            low, high = colv[1, pl.ds(i + NI, 1), :], colv[0, pl.ds(i, 1), :]
            place(xv, i + 2, fine_st[i], keep(gy_low, low), keep(gy_high, high), NJ)
            return carry

        lax.fori_loop(0, NI, body, 0)

        def cells(c, cell):
            return jnp.concatenate([corv[c, 4 * k + cell : 4 * k + cell + 1, :] for k in range(4)], axis=1)

        for m in range(2):
            colx[0, m, 2:10, :] = keep(gy_low, colv[1, NI * m : NI * m + NI, :])
            colx[1, 1 + m, 2:10, :] = keep(gy_high, colv[0, NI * m : NI * m + NI, :])
        for i in range(NI):
            colx[0, 2, i + 2 : i + 3, :] = fine_st[i, 0:1, :]
            colx[1, 0, i + 2 : i + 3, :] = fine_st[i, NJ - 1 : NJ, :]
        for e, first_row, here in ((1, 0, gx_low), (0, NI + 2, gx_high)):
            for m in range(2):
                at = first_row + m
                value = keep(here, rv_e[e, m].astype(F32))
                low = [keep(here & gy_low, cells(2 * e + 1, 2 * m + j)) for j in range(2)]
                high = [keep(here & gy_high, cells(2 * e, 2 * m + j)) for j in range(2)]
                place(xv, at, value, low[1], high[0], NJ)
                for j in range(2):
                    colx[0, j, at : at + 1, :] = low[j]
                    colx[1, 1 + j, at : at + 1, :] = high[j]
                colx[0, 2, at : at + 1, :] = value[0:1]
                colx[1, 0, at : at + 1, :] = value[NJ - 1 : NJ]
        for a in range(3):
            for b in range(3):
                for m in range(2):
                    strip = colx[m, b]
                    strip = strip if a == 0 else pltpu.roll(strip, 16 - a, 0)
                    xvc[3 * a + b, 16 * m : 16 * m + 16, PAD : PAD + LANES] = strip.astype(BF16)

    def assemble_hidden():
        def body(at, carry):
            here = ((at > 0) | gx_low) & ((at < NI + 1) | gx_high)
            low, high = hid[NI + 2, pl.ds(at, 1), :], hid[NI + 3, pl.ds(at, 1), :]
            place(xh, at, keep(here, hid[at]), keep(here & gy_low, low), keep(here & gy_high, high), NJ)
            return carry

        lax.fori_loop(0, NI + 2, body, 0)

    def assemble_coarse(stage, dst):
        for i in range(CI):
            low = jnp.concatenate([colr[1, 4 * k + i : 4 * k + i + 1, 512:640] for k in range(4)], axis=1)
            high = jnp.concatenate([colr[0, 4 * k + i : 4 * k + i + 1, 512:640] for k in range(4)], axis=1)
            place(dst, i + 1, coarse_st[i], keep(gy_low, low), keep(gy_high, high), CJ)
        for e, index, here in ((1, 0, gx_low), (0, CI + 1, gx_high)):
            row = r_e[stage, e, :, LANES:].astype(F32)
            value = keep(here, jnp.concatenate([row[:CJ], row[CJ:]], axis=1))
            low = keep(here & gy_low, corner(2 * e + 1, 8, 4))
            high = keep(here & gy_high, corner(2 * e, 8, 4))
            place(dst, index, value, low, high, CJ)

    def wide_window(a, b):
        parts = []
        for g in range(4):
            lanes = slice(GROUP * g, GROUP * g + WINDOW)
            parts += [xv[b, pl.ds(a, NI + 2), :, lanes].reshape((NI + 2) * NJ, WINDOW), xvc[3 * a + b, :, lanes]]
        return jnp.concatenate(parts, axis=0)

    def fine_window(src, a, b):
        return jnp.concatenate(
            [src[b, pl.ds(a, NI), :, GROUP * g : GROUP * g + WINDOW].reshape(NI * NJ, WINDOW) for g in range(4)], axis=0)

    def coarse_window(src, a, b):
        return jnp.concatenate(
            [src[b, pl.ds(a, CI), :, GROUP * g : GROUP * g + WINDOW].reshape(CI * CJ, WINDOW) for g in range(2)],
            axis=0).astype(BF16)

    def three(body, looped):
        if looped:
            lax.fori_loop(0, 3, body, 0)
        else:
            for a in range(3):
                body(a, 0)

    def conv(window, weights, rows, looped):
        if not looped:
            total = dot(window(0, 0), weights[0])
            for t in range(1, TAPS):
                total = total + dot(window(t // 3, t % 3), weights[t])
            return total
        acc[0:rows] = jnp.zeros((rows, GROUP), F32)

        def body(a, carry):
            total = acc[0:rows]
            for b in range(3):
                total = total + dot(window(a, b), weights[3 * a + b])
            acc[0:rows] = total
            return carry

        lax.fori_loop(0, 3, body, 0)
        return acc[0:rows]

    def joined(window, weights):
        wide = jnp.concatenate([window(t // 3, t % 3) for t in range(TAPS)], axis=1)
        return dot(wide, weights[...].reshape(TAPS * WINDOW, GROUP))

    def by_group(window, weights, rows):
        def body(g, carry):
            lanes = pl.ds(pl.multiple_of(g * GROUP, GROUP), WINDOW)
            total = dot(window(0, 0, lanes), weights[0])
            for t in range(1, TAPS):
                total = total + dot(window(t // 3, t % 3, lanes), weights[t])
            acc[pl.ds(pl.multiple_of(g * rows, 16), rows)] = total
            return carry

        lax.fori_loop(0, 4, body, 0)
        return acc[0 : 4 * rows]

    def group_window(src):
        return lambda a, b, lanes: src[b, a : a + NI, :, lanes].reshape(NI * NJ, WINDOW)

    def wide_group_window(a, b, lanes):
        own = xv[b, a : a + NI + 2, :, lanes].reshape((NI + 2) * NJ, WINDOW)
        return jnp.concatenate([own, xvc[3 * a + b, :, lanes]], axis=0)

    def grads(window, slopes, store, looped):
        def body(a, carry):
            for b in range(3):
                g = dot(slopes[...], window(a, b))
                even = g[0:64, 0:384] + g[128:192, 128:512]
                odd = g[64:128, 128:384] + g[192:256, 256:512]
                shifted = jnp.concatenate([even[:, 64:192], even[:, 192:320]], axis=1)
                total = odd + shifted
                store(3 * a + b, total[:, 0:128].astype(BF16))
                half[3 * a + b] = total[:, 128:256]
            return carry

        three(body, looped)
        lane = lax.broadcasted_iota(jnp.int32, (64, 128), 1)
        for u in range(5):
            left = half[2 * u]
            right = pltpu.roll(half[2 * u + 1], 64, 1) if u < 4 else jnp.zeros_like(left)
            store(TAPS + u, jnp.where(lane < 64, left, right).astype(BF16))

    def pool_matrix(rows, columns, flip):
        r = lax.broadcasted_iota(jnp.int32, (rows, columns), 1 if flip else 0)
        s = lax.broadcasted_iota(jnp.int32, (rows, columns), 0 if flip else 1)
        r = r & 31
        return jnp.where(r == (s >> 5) * 8 + ((s & 15) >> 1), 1.0, 0.0).astype(BF16)

    def pool(value):
        sums = dot(pool_matrix(32, 128, False), value)
        lane = lax.broadcasted_iota(jnp.int32, (32, 128), 1)
        tiles = []
        for k in range(4):
            pair = []
            for m in range(2):
                tile = sums[:, 256 * k + 128 * m : 256 * k + 128 * m + 128]
                pair.append(tile + pltpu.roll(tile, 64, 1))
            tiles.append(jnp.where(lane < 64, pair[0], pair[1]))
        return jnp.concatenate(tiles, axis=1).reshape(CI, CJ, CLANES)

    def spread(value):
        lane = lax.broadcasted_iota(jnp.int32, (32, 128), 1)
        tiles = []
        for k in range(4):
            tile = value[:, 128 * k : 128 * k + 128]
            turned = pltpu.roll(tile, 64, 1)
            tiles += [jnp.where(lane < 64, tile, turned), jnp.where(lane < 64, turned, tile)]
        return jnp.concatenate(tiles, axis=1)

    def ungroup(value, rows):
        return jnp.concatenate([value[rows * g : rows * (g + 1)] for g in range(value.shape[0] // rows)], axis=1)

    def make_sum(part, in1, b2, in2, in3, res, send, got):
        def c1(r):
            return pltpu.make_async_remote_copy(part.at[pl.ds((1 - core) * 16, 16)], in1, send.at[0], got.at[0],
                                                device_id=other_core, device_id_type=MESH)

        def c2(r):
            w, peer = w_peer(r)
            return pltpu.make_async_remote_copy(b2.at[w], in2.at[r - 1], send.at[r], got.at[r],
                                                device_id=peer, device_id_type=MESH)

        def c3(r):
            _, peer = z_peer(r)
            return pltpu.make_async_remote_copy(in3.at[z_at], in3.at[z_at], send.at[15 + r], got.at[15 + r],
                                                device_id=peer, device_id_type=MESH)

        mine = core * 16 + w_at

        def c4(r):
            _, peer = w_peer(r)
            return pltpu.make_async_remote_copy(res.at[mine], res.at[mine], send.at[22 + r], got.at[22 + r],
                                                device_id=peer, device_id_type=MESH)

        def c5(r):
            own = pl.ds(core * 16, 16)
            return pltpu.make_async_remote_copy(res.at[own], res.at[own], send.at[38], got.at[38],
                                                device_id=other_core, device_id_type=MESH)

        def start(make, count):
            for r in FARTHEST[count]:
                make(r).start()

        def finish(make, count):
            for r in range(1, count):
                make(r).wait_recv()

        def s1():
            start(c1, 2)

        def s2():
            finish(c1, 2)
            b2[...] = (part[pl.ds(core * 16, 16)].astype(F32) + in1[...].astype(F32)).astype(BF16)
            start(c2, 16)

        def s3():
            finish(c2, 16)
            total = b2[w_at].astype(F32)
            for r in range(15):
                total = total + in2[r].astype(F32)
            in3[z_at] = total.astype(BF16)
            start(c3, 8)

        def s4():
            finish(c3, 8)
            total = in3[0].astype(F32)
            for r in range(1, 8):
                total = total + in3[r].astype(F32)
            res[mine] = total.astype(BF16)
            start(c4, 16)

        def s5():
            finish(c4, 16)
            start(c5, 2)

        def s6():
            finish(c5, 2)

        def s7():
            for make, count in ((c1, 2), (c2, 16), (c3, 8), (c4, 16), (c5, 2)):
                for r in range(1, count):
                    make(r).wait_send()

        return s1, s2, s3, s4, s5, s6, s7

    sum_sc = make_sum(part_sc, in1_sc, b2_sc, in2_sc, in3_sc, res_sc, s_sc, g_sc)
    sum_f = make_sum(part_f, in1_f, b2_f, in2_f, in3_f, res_f, s_f, g_f)

    cor[...] = jnp.zeros_like(cor)
    col[...] = jnp.zeros_like(col)
    loads[1].wait()
    coarse_st[...] = pool(cot[...].reshape(NI * NJ, LANES)).astype(BF16).astype(F32)
    pack_coarse(0)
    loads[0].wait()
    fine_st[...] = vol[...].astype(F32)
    pack_volume()
    pl.semaphore_wait(barrier, len(partners))
    send(rim_copies(0, False))
    send(volume_copies())

    def build(k, fwd, bwd):
        for w in (fwd, bwd):
            if w is not None:
                w[...] = jnp.zeros_like(w)

        def band(w, t, c0, c1, c2):
            zero = jnp.zeros_like(c0)
            pairs = ((c0, zero), (c1, c0), (c2, c1), (zero, c2))
            for m, tile in enumerate(jnp.concatenate(pair, axis=1) for pair in pairs):
                for pair in range(2):
                    row = 64 * (2 * pair + 1 + m)
                    w[t, row : row + 64, 128 * pair : 128 * pair + 128] = tile

        def body(t, carry):
            taps = [k[3 * t + c] for c in range(3)]
            band(fwd, t, *taps)
            if bwd is not None:
                c0, c1, c2 = (v.astype(F32).T.astype(BF16) for v in taps)
                band(bwd, 8 - t, c2, c1, c0)
            return carry

        lax.fori_loop(0, TAPS, body, 0)

    loads[2].wait()
    build(k1, w1, None)
    loads[3].wait()
    build(k2, w2, w2b)
    loads[4].wait()
    build(kc, wc, wcb)
    for padded in (xv, xh, xs, xp, xc):
        rows, tail = padded.shape[2], padded.shape[3] - PAD
        padded[:, :, :, 0:PAD] = jnp.zeros((3, padded.shape[1], rows, PAD), padded.dtype)
        padded[:, :, :, tail:] = jnp.zeros((3, padded.shape[1], rows, PAD), padded.dtype)
    xvc[:, :, 0:PAD] = jnp.zeros((TAPS, 32, PAD), BF16)
    xvc[:, :, PAD + LANES :] = jnp.zeros((TAPS, 32, PAD), BF16)
    part_sc[28:32] = jnp.zeros((4, 64, 128), BF16)
    part_f[28:32] = jnp.zeros((4, 32, 128), BF16)

    def widen(value):
        wide = spread(value)
        top = wide.astype(BF16)
        rest = (wide - top.astype(F32)).astype(BF16)
        return dot(pool_matrix(128, 64, True), jnp.concatenate([top, rest], axis=0))

    receive(rim_copies(0, False))
    unpack_rims(0)
    assemble_coarse(0, xc)
    pooled_slope = ungroup(joined(lambda a, b: coarse_window(xc, a, b), wcb), CI * CJ)
    upstream[...] = (cot[...].reshape(NI * NJ, LANES).astype(F32) + widen(pooled_slope) * 0.125).astype(BF16).astype(F32)

    receive(volume_copies())
    assemble_volume()

    first = ungroup(conv(wide_window, w1, 4 * (NI + 4) * NJ, 'c1' in LOOPED), (NI + 4) * NJ)
    sigma = sigmoid(first)
    hid[...] = (first * sigma).astype(BF16).astype(F32).reshape(NI + 4, NJ, LANES)
    own, own_sigma = first[NJ : NJ + NI * NJ], sigma[NJ : NJ + NI * NJ]
    slope1[...] = own_sigma * (1.0 + own * (1.0 - own_sigma))
    assemble_hidden()

    second = ungroup(conv(lambda a, b: fine_window(xh, a, b), w2, 4 * NI * NJ, 'c2' in LOOPED), NI * NJ)
    sigma = sigmoid(second)
    second_slope = (upstream[...] * (sigma * (1.0 + second * (1.0 - sigma)))).astype(BF16).astype(F32)
    fine_st[...] = second_slope.reshape(NI, NJ, LANES)
    pack_fine(1)
    send(rim_copies(1, True))
    fine = (second * sigma).astype(BF16)
    fine_keep[...] = fine
    coarse_st[...] = (pool(fine) * 0.125).astype(BF16).astype(F32)
    pack_coarse(2)
    send(rim_copies(2, False))

    def grouped_t(value, groups):
        return jnp.concatenate([value[:, GROUP * g : GROUP * (g + 1)] for g in range(groups)], axis=0).T.astype(BF16)

    slopes_t[...] = grouped_t(fine_st[...].reshape(NI * NJ, LANES), 4)

    def store_second(n, value):
        part_sc[n] = value

    def store_coarse(n, value):
        part_sc[14 + n] = value

    def store_first(n, value):
        part_f[pl.ds(2 * n, 2)] = value.reshape(2, 32, 128)

    grads(lambda a, b: fine_window(xh, a, b), slopes_t, store_second, 'g2' in LOOPED)
    pooled_t[...] = grouped_t(coarse_st[...].reshape(CI * CJ, CLANES), 2)
    grads(lambda a, b: coarse_window(xc, a, b), pooled_t, store_coarse, 'gc' in LOOPED)
    sum_sc[0]()

    rims = rim_copies(1, True)
    receive(rims[6:])
    assemble_rows(1, xs)
    sum_sc[1]()
    acc[0 : 4 * NI * NJ] = conv(lambda a, b: fine_window(xs, a, b), w2b, 4 * NI * NJ, "c3" in LOOPED)
    receive(rims[:6])
    unpack_rims(1)
    assemble_strips()
    add_strips(w2b)
    hidden_slope = ungroup(acc[0 : 4 * NI * NJ], NI * NJ)
    first_slope = (hidden_slope * slope1[...]).astype(BF16).astype(F32)
    slopes_t[...] = grouped_t(first_slope, 4)
    grads(lambda a, b: fine_window(xv, a + 1, b), slopes_t, store_first, 'g1' in LOOPED)
    sum_f[0]()
    sum_sc[2]()
    sum_f[1]()

    receive(rim_copies(2, False))
    unpack_rims(2)
    assemble_coarse(2, xp)
    coarse = ungroup(joined(lambda a, b: coarse_window(xp, a, b), wc), CI * CJ).astype(BF16)
    wide = spread(coarse.astype(F32)).astype(BF16)
    repeated = dot(pool_matrix(128, 32, True), wide)
    field[...] = (fine_keep[...].astype(F32) + repeated).astype(BF16).reshape(NI, NJ, LANES)

    sum_sc[3]()
    sum_f[2]()
    sum_f[3]()
    sum_sc[4]()
    sum_f[4]()
    sum_sc[5]()
    unpack_taps(lambda n: res_sc[n], out_second)
    unpack_reversed(lambda n: res_sc[14 + n], out_coarse)
    sum_f[5]()
    out_f[...] = res_f[...]
    sum_sc[6]()
    sum_f[6]()
    for there, _, copy in rim_copies(0, False) + volume_copies() + rim_copies(1, True) + rim_copies(2, False):
        pl.when(there)(copy.wait_send)


def unpack_kernel(held, second, coarse, f, field, first_out, second_out, coarse_out, first_grad, sem):
    copies = [
        pltpu.make_async_copy(src, dst, sem.at[n])
        for n, (src, dst) in enumerate((
            (held, field), (second, second_out), (coarse, coarse_out), (first_grad, first_out),
        ))
    ]
    for copy in copies[:3]:
        copy.start()
    unpack_taps(lambda n: f[2 * n : 2 * n + 2].reshape(64, 128), first_grad)
    copies[3].start()
    for copy in copies:
        copy.wait()


def per_device(volume, cotangent, first_kernel, second_kernel, coarse_kernel):
    in_hbm, in_vmem = (pl.BlockSpec(memory_space=space) for space in (pltpu.HBM, pltpu.VMEM))
    dma = pltpu.SemaphoreType.DMA

    def sum_buffers(rows):
        return [
            pltpu.VMEM((32, rows, 128), BF16), pltpu.VMEM((16, rows, 128), BF16), pltpu.VMEM((16, rows, 128), BF16),
            pltpu.VMEM((15, rows, 128), BF16), pltpu.VMEM((8, rows, 128), BF16), pltpu.VMEM((32, rows, 128), BF16),
        ]

    sc_bufs, f_bufs = sum_buffers(64), sum_buffers(32)
    mixed = [b for pair in zip(sc_bufs, f_bufs) for b in pair]
    scratch = [
        pltpu.VMEM((NI, NJ, LANES), F32),
        pltpu.VMEM((CI, CJ, CLANES), F32),
        pltpu.VMEM((3, NI + 4, NJ, LANES + 2 * PAD), BF16),
        pltpu.VMEM((3, NI + 2, NJ, LANES + 2 * PAD), BF16),
        pltpu.VMEM((3, NI + 2, NJ, LANES + 2 * PAD), BF16),
        pltpu.VMEM((3, CI + 2, CJ, CLANES + 2 * PAD), F32),
        pltpu.VMEM((3, CI + 2, CJ, CLANES + 2 * PAD), F32),
        pltpu.VMEM((NI * NJ, LANES), F32),
        pltpu.VMEM((NI * NJ, LANES), F32),
        pltpu.VMEM((NI * NJ, LANES), BF16),
        pltpu.VMEM((GROUP, 4 * NI * NJ), BF16),
        pltpu.VMEM((4 * (NI + 4) * NJ, GROUP), F32),
        pltpu.VMEM((TAPS, WINDOW, GROUP), BF16),
        pltpu.VMEM((TAPS, WINDOW, GROUP), BF16),
        pltpu.VMEM((TAPS, WINDOW, GROUP), BF16),
        pltpu.VMEM((TAPS, WINDOW, GROUP), BF16),
        pltpu.VMEM((TAPS, WINDOW, GROUP), BF16),
        pltpu.VMEM((3, 2, 16, 1280), BF16), pltpu.VMEM((3, 2, 16, 1280), BF16),
        pltpu.VMEM((3, 2, 16, 640), BF16), pltpu.VMEM((3, 2, 16, 640), BF16),
        pltpu.VMEM((3, 4, 16, 128), BF16), pltpu.VMEM((3, 4, 16, 128), BF16),
        pltpu.VMEM((16, 640), F32), pltpu.VMEM((2, 16, 640), F32),
        pltpu.VMEM((16, 128), F32), pltpu.VMEM((4, 16, 128), F32),
        *mixed,
        pltpu.VMEM((TAPS, 64, 128), F32),
        dma((4, 2)), dma((4, 2)), dma((4, 2)), dma((4, 2)), dma((4, 4)), dma((4, 4)),
        dma((39,)), dma((39,)), dma((39,)), dma((39,)), dma((5,)),
        pltpu.VMEM(volume.shape[1:], BF16), pltpu.VMEM(volume.shape[1:], BF16),
        *[pltpu.VMEM((27, 64, 64), BF16)] * 3,
        pltpu.VMEM((2, 16, LANES + 2 * PAD), F32),
        pltpu.VMEM((GROUP, 2 * CI * CJ), BF16),
        pltpu.VMEM((NI + 4, NJ, LANES), F32),
        pltpu.VMEM((TAPS, 32, LANES + 2 * PAD), BF16),
        pltpu.VMEM((16, LANES), F32), pltpu.VMEM((16, 256), F32),
        pltpu.VMEM((2, 16, LANES), F32), pltpu.VMEM((4, 16, 256), F32),
        pltpu.VMEM((2, 3, 16, LANES), F32),
        pltpu.VMEM((2, 16, LANES), BF16), pltpu.VMEM((2, 16, LANES), BF16),
        pltpu.VMEM((4, 16, 256), BF16), pltpu.VMEM((4, 16, 256), BF16),
        pltpu.VMEM((2, 2, NJ, LANES), BF16),
    ]
    block = volume.shape[1:]
    taps = (27, 64, 64)
    kernels = (first_kernel, second_kernel, coarse_kernel)
    operands = (volume[0], cotangent[0], *(k.reshape(taps) for k in kernels))
    field, second_grad, coarse_grad, f = pl.pallas_call(
        kernel,
        out_shape=(
            jax.ShapeDtypeStruct(block, BF16),
            jax.ShapeDtypeStruct(taps, F32),
            jax.ShapeDtypeStruct(taps, F32),
            jax.ShapeDtypeStruct((32, 32, 128), BF16),
        ),
        in_specs=[in_hbm] * 5,
        out_specs=(in_vmem,) * 4,
        scratch_shapes=scratch,
        compiler_params=pltpu.CompilerParams(
            collective_id=0, has_side_effects=True, vmem_limit_bytes=48 * 1024 * 1024
        ),
        name="block",
    )(*(pltpu.with_memory_space_constraint(v, pltpu.HBM) for v in operands))
    field, first_grad, second_grad, coarse_grad = pl.pallas_call(
        unpack_kernel,
        out_shape=(jax.ShapeDtypeStruct(block, BF16),) + (jax.ShapeDtypeStruct(taps, F32),) * 3,
        in_specs=[in_vmem] * 4,
        out_specs=(in_hbm,) * 4,
        scratch_shapes=[
            pltpu.VMEM(taps, F32), dma((4,)),
        ],
        compiler_params=pltpu.CompilerParams(vmem_limit_bytes=32 * 1024 * 1024),
        name="unpack",
    )(field, second_grad, coarse_grad, f)
    kernel_shape = first_kernel.shape
    return (
        field[None],
        first_grad.reshape(kernel_shape),
        second_grad.reshape(kernel_shape),
        coarse_grad.reshape(kernel_shape),
    )


def solution(mesh):
    in_specs = (P("dp", "gx", "gy", None), P("dp", "gx", "gy", None), P(), P(), P())
    out_specs = (P("dp", "gx", "gy", None), P(), P(), P())
    return jax.shard_map(
        per_device, mesh=mesh, in_specs=in_specs, out_specs=out_specs, check_vma=False
    )
```

```python
import jax
import jax.numpy as jnp
from jax import lax
from jax.experimental import pallas as pl
from jax.experimental.pallas import tpu as pltpu
from jax.sharding import PartitionSpec as P

MESH = pl.DeviceIdType.MESH

FARTHEST = {
    2: (1,),
    16: sorted(range(1, 16), key=lambda r: -(min(r // 4, 4 - r // 4) + min(r % 4, 4 - r % 4))),
    8: sorted(range(1, 8), key=lambda r: -min(r, 8 - r)),
}
F32 = jnp.float32
BF16 = jnp.bfloat16

NI, NJ, LANES = 8, 16, 1024
CI, CJ, CLANES = 4, 8, 512
PAD = 128
GROUP = 256
WINDOW = 512
TAPS = 9
LOOPED = ('c2', 'g1', 'c3')


def dot(a, b, dims=((1,), (0,))):
    return lax.dot_general(a, b, (dims, ((), ())), preferred_element_type=F32)


def sigmoid(v):
    return 1.0 / (1.0 + jnp.exp(-v))


def unpack_taps(read, out):
    for t in range(TAPS):
        block = read(t).astype(F32).T
        out[3 * t] = block[0:64]
        out[3 * t + 1] = block[64:128]
    for u in range(5):
        block = read(TAPS + u).astype(F32).T
        out[6 * u + 2] = block[0:64]
        if u < 4:
            out[6 * u + 5] = block[64:128]


def unpack_reversed(read, out):
    for t in range(TAPS):
        block = read(t).astype(F32)
        out[26 - 3 * t] = block[:, 0:64]
        out[25 - 3 * t] = block[:, 64:128]
    for u in range(5):
        block = read(TAPS + u).astype(F32)
        out[24 - 6 * u] = block[:, 0:64]
        if u < 4:
            out[21 - 6 * u] = block[:, 64:128]


def kernel(
    vol_in, cot_in, k1_in, k2_in, kc_in,
    field, out_second, out_coarse, out_f,
    fine_st, coarse_st, xv, xh, xs, xp, xc, slope1, upstream, fine_keep, slopes_t, acc,
    w1, w2, w2b, wc, wcb,
    s_e, r_e, s_n, r_n, s_c, r_c, col, colr, cor, corr,
    part_sc, part_f, in1_sc, in1_f, b2_sc, b2_f, in2_sc, in2_f, in3_sc, in3_f, res_sc, res_f, half,
    se_sem, re_sem, sn_sem, rn_sem, sc_sem, rc_sem,
    s_sc, g_sc, s_f, g_f, in_sem,
    vol, cot, k1, k2, kc,
    strips, pooled_t, hid, xvc, colw, corw, colv, corv, colx, sv_n, rv_n, sv_c, rv_c, rv_e,
):
    loads = [
        pltpu.make_async_copy(src, dst, in_sem.at[n])
        for n, (src, dst) in enumerate(((vol_in, vol), (cot_in, cot), (k1_in, k1), (k2_in, k2), (kc_in, kc)))
    ]
    for load in loads:
        load.start()

    gx, gy, dp = lax.axis_index("gx"), lax.axis_index("gy"), lax.axis_index("dp")
    x_at, z_hi = lax.div(gy, 2), lax.rem(gy, 2)
    z_lo, core = lax.div(gx, 2), lax.rem(gx, 2)
    w_at = x_at * 4 + dp
    z_at = z_hi * 4 + z_lo

    def side(at, step):
        return lax.rem(at + step + 8, 8)

    def near(di, dj):
        return {"gx": side(gx, di), "gy": side(gy, dj)}

    def w_peer(r):
        x, y = lax.rem(x_at + r // 4, 4), lax.rem(dp + r % 4, 4)
        return x * 4 + y, {"gy": x * 2 + z_hi, "dp": y}

    other_core = {"gx": z_lo * 2 + 1 - core}

    def z_peer(r):
        z = lax.rem(z_at + r, 8)
        return z, {"gx": lax.rem(z, 4) * 2 + core, "gy": x_at * 2 + lax.div(z, 4)}

    steps = (-1, 1)
    barrier = pltpu.get_barrier_semaphore()
    partners = [near(s, t) for s in steps for t in steps] + [near(0, s) for s in steps]
    partners += [z_peer(r)[1] for r in FARTHEST[8]] + [w_peer(r)[1] for r in FARTHEST[16]]
    partners += [near(s, 0) for s in steps] + [other_core]
    for partner in partners:
        pl.semaphore_signal(barrier, inc=1, device_id=partner, device_id_type=MESH)

    def pack_coarse(stage):
        for e in range(2):
            row = coarse_st[e * (CI - 1)]
            s_e[stage, e, :, LANES:] = jnp.concatenate([row[:, :256], row[:, 256:]], axis=0).astype(BF16)
        for n in range(2):
            cj = n * (CJ - 1)
            for i in range(CI):
                for k in range(4):
                    col[4 * k + i : 4 * k + i + 1, 512:640] = coarse_st[i, cj : cj + 1, 128 * k : 128 * k + 128]
            s_n[stage, n, :, 512:640] = col[:, 512:640].astype(BF16)
        for e in range(2):
            for n in range(2):
                cj = n * (CJ - 1)
                for k in range(4):
                    cor[8 + k : 9 + k] = coarse_st[e * (CI - 1), cj : cj + 1, 128 * k : 128 * k + 128]
                s_c[stage, 2 * e + n] = cor[...].astype(BF16)

    def pack_fine(stage):
        for e in range(2):
            for n in range(2):
                i, j = e * (NI - 1), n * (NJ - 1)
                for k in range(8):
                    cor[k : k + 1] = fine_st[i, j : j + 1, 128 * k : 128 * k + 128]
                s_c[stage, 2 * e + n] = cor[...].astype(BF16)
        for n in range(2):
            j = n * (NJ - 1)
            for i in range(NI):
                col[i : i + 1, 0:512] = fine_st[i, j : j + 1, 0:512]
                col[NI + i : NI + i + 1, 0:512] = fine_st[i, j : j + 1, 512:1024]
            s_n[stage, n, :, 0:512] = col[:, 0:512].astype(BF16)
        for e in range(2):
            s_e[stage, e, :, 0:LANES] = fine_st[e * (NI - 1)].astype(BF16)

    def pack_volume():
        for n in range(2):
            for i in range(NI):
                for m in range(2):
                    j = n * (NJ - 2) + m
                    colw[NI * m + i : NI * m + i + 1, :] = fine_st[i, j : j + 1, :]
            sv_n[n] = colw[...].astype(BF16)
        for e in range(2):
            for n in range(2):
                for cell in range(4):
                    i, j = e * (NI - 2) + cell // 2, n * (NJ - 2) + cell % 2
                    for k in range(4):
                        corw[4 * k + cell : 4 * k + cell + 1, :] = fine_st[i, j : j + 1, 256 * k : 256 * k + 256]
                sv_c[2 * e + n] = corw[...].astype(BF16)

    gx_low, gx_high, gy_low, gy_high = gx > 0, gx < 7, gy > 0, gy < 7
    to_x, to_y = (gx_low, gx_high), (gy_low, gy_high)

    def to_sides(n_src, n_dst, n_sems, c_src, c_dst, c_sems, e_src, e_dst, e_sems):
        copies = []
        for e in range(2):
            for n in range(2):
                c = 2 * e + n
                copies.append((to_x[e] & to_y[n], to_x[1 - e] & to_y[1 - n], pltpu.make_async_remote_copy(
                    c_src(c), c_dst(c), c_sems[0].at[c], c_sems[1].at[c],
                    device_id=near(steps[e], steps[n]), device_id_type=MESH)))
        for n in range(2):
            copies.append((to_y[n], to_y[1 - n], pltpu.make_async_remote_copy(
                n_src(n), n_dst(n), n_sems[0].at[n], n_sems[1].at[n],
                device_id=near(0, steps[n]), device_id_type=MESH)))
        for e in range(2):
            copies.append((to_x[e], to_x[1 - e], pltpu.make_async_remote_copy(
                e_src(e), e_dst(e), e_sems[0].at[e], e_sems[1].at[e],
                device_id=near(steps[e], 0), device_id_type=MESH)))
        return copies

    def rim_copies(stage, with_fine):
        lanes_e, lanes_n = (pl.ds(0, 1024), pl.ds(0, 512)) if with_fine else (pl.ds(1024, 256), pl.ds(512, 128))
        return to_sides(
            lambda n: s_n.at[stage, n, :, lanes_n], lambda n: r_n.at[stage, n, :, lanes_n], (sn_sem.at[stage], rn_sem.at[stage]),
            lambda c: s_c.at[stage, c], lambda c: r_c.at[stage, c], (sc_sem.at[stage], rc_sem.at[stage]),
            lambda e: s_e.at[stage, e, :, lanes_e], lambda e: r_e.at[stage, e, :, lanes_e], (se_sem.at[stage], re_sem.at[stage]))

    def volume_copies():
        return to_sides(
            lambda n: sv_n.at[n], lambda n: rv_n.at[n], (sn_sem.at[3], rn_sem.at[3]),
            lambda c: sv_c.at[c], lambda c: rv_c.at[c], (sc_sem.at[3], rc_sem.at[3]),
            lambda e: vol.at[pl.ds(e * (NI - 2), 2)], lambda e: rv_e.at[e], (se_sem.at[3], re_sem.at[3]))

    def send(copies):
        for there, _, copy in copies:
            pl.when(there)(copy.start)

    def receive(copies):
        for _, there, copy in copies:
            pl.when(there)(copy.wait_recv)

    def place(dst, index, value, low, high, rows):
        at = lax.broadcasted_iota(jnp.int32, value.shape, 0)
        dst[0, index, :, PAD : PAD + value.shape[1]] = jnp.where(
            at == 0, jnp.broadcast_to(low, value.shape), pltpu.roll(value, 1, 0)).astype(dst.dtype)
        dst[1, index, :, PAD : PAD + value.shape[1]] = value.astype(dst.dtype)
        dst[2, index, :, PAD : PAD + value.shape[1]] = jnp.where(
            at == rows - 1, jnp.broadcast_to(high, value.shape), pltpu.roll(value, rows - 1, 0)).astype(dst.dtype)

    def keep(here, value):
        return jnp.where(here, value, 0.0)

    def unpack_rims(stage):
        for n in range(2):
            colr[n] = r_n[stage, n].astype(F32)
        for c in range(4):
            corr[c] = r_c[stage, c].astype(F32)

    def corner(c, first, count):
        return jnp.concatenate([corr[c, first + k : first + k + 1, :] for k in range(count)], axis=1)

    def assemble_rows(stage, dst):
        none = jnp.zeros((1, LANES), F32)

        def body(i, carry):
            place(dst, i + 1, fine_st[i], none, none, NJ)
            return carry

        lax.fori_loop(0, NI, body, 0)
        for e, index, here in ((1, 0, gx_low), (0, NI + 1, gx_high)):
            place(dst, index, keep(here, r_e[stage, e, :, 0:LANES].astype(F32)), none, none, NJ)

    def assemble_strips():
        strips[:, :, 0:PAD] = jnp.zeros((2, 16, PAD), F32)
        strips[:, :, PAD + LANES :] = jnp.zeros((2, 16, PAD), F32)
        for m, there in ((0, gy_low), (1, gy_high)):
            n = 1 - m
            value = jnp.concatenate([colr[n, 0:NI, 0:512], colr[n, NI : 2 * NI, 0:512]], axis=1)
            strips[m, 1 : NI + 1, PAD : PAD + LANES] = keep(there, value)
            strips[m, 0:1, PAD : PAD + LANES] = keep(there & gx_low, corner(2 + n, 0, 8))
            strips[m, NI + 1 : NI + 2, PAD : PAD + LANES] = keep(there & gx_high, corner(n, 0, 8))

    def add_strips(weights):
        for m in range(2):
            total = None
            for a in range(3):
                window = jnp.concatenate(
                    [strips[m, a : a + NI, GROUP * g : GROUP * g + WINDOW] for g in range(4)], axis=0).astype(BF16)
                part = dot(window, weights[3 * a + 2 * m])
                total = part if a == 0 else total + part
            for g in range(4):
                for i in range(NI):
                    row = g * NI * NJ + i * NJ + m * (NJ - 1)
                    acc[row : row + 1, :] += total[g * NI + i : g * NI + i + 1, :]

    def assemble_volume():
        for n in range(2):
            colv[n] = rv_n[n].astype(F32)
        for c in range(4):
            corv[c] = rv_c[c].astype(F32)

        def body(i, carry):
            low, high = colv[1, pl.ds(i + NI, 1), :], colv[0, pl.ds(i, 1), :]
            place(xv, i + 2, fine_st[i], keep(gy_low, low), keep(gy_high, high), NJ)
            return carry

        lax.fori_loop(0, NI, body, 0)

        def cells(c, cell):
            return jnp.concatenate([corv[c, 4 * k + cell : 4 * k + cell + 1, :] for k in range(4)], axis=1)

        for m in range(2):
            colx[0, m, 2:10, :] = keep(gy_low, colv[1, NI * m : NI * m + NI, :])
            colx[1, 1 + m, 2:10, :] = keep(gy_high, colv[0, NI * m : NI * m + NI, :])
        for i in range(NI):
            colx[0, 2, i + 2 : i + 3, :] = fine_st[i, 0:1, :]
            colx[1, 0, i + 2 : i + 3, :] = fine_st[i, NJ - 1 : NJ, :]
        for e, first_row, here in ((1, 0, gx_low), (0, NI + 2, gx_high)):
            for m in range(2):
                at = first_row + m
                value = keep(here, rv_e[e, m].astype(F32))
                low = [keep(here & gy_low, cells(2 * e + 1, 2 * m + j)) for j in range(2)]
                high = [keep(here & gy_high, cells(2 * e, 2 * m + j)) for j in range(2)]
                place(xv, at, value, low[1], high[0], NJ)
                for j in range(2):
                    colx[0, j, at : at + 1, :] = low[j]
                    colx[1, 1 + j, at : at + 1, :] = high[j]
                colx[0, 2, at : at + 1, :] = value[0:1]
                colx[1, 0, at : at + 1, :] = value[NJ - 1 : NJ]
        for a in range(3):
            for b in range(3):
                for m in range(2):
                    strip = colx[m, b]
                    strip = strip if a == 0 else pltpu.roll(strip, 16 - a, 0)
                    xvc[3 * a + b, 16 * m : 16 * m + 16, PAD : PAD + LANES] = strip.astype(BF16)

    def assemble_hidden():
        def body(at, carry):
            here = ((at > 0) | gx_low) & ((at < NI + 1) | gx_high)
            low, high = hid[NI + 2, pl.ds(at, 1), :], hid[NI + 3, pl.ds(at, 1), :]
            place(xh, at, keep(here, hid[at]), keep(here & gy_low, low), keep(here & gy_high, high), NJ)
            return carry

        lax.fori_loop(0, NI + 2, body, 0)

    def assemble_coarse(stage, dst):
        for i in range(CI):
            low = jnp.concatenate([colr[1, 4 * k + i : 4 * k + i + 1, 512:640] for k in range(4)], axis=1)
            high = jnp.concatenate([colr[0, 4 * k + i : 4 * k + i + 1, 512:640] for k in range(4)], axis=1)
            place(dst, i + 1, coarse_st[i], keep(gy_low, low), keep(gy_high, high), CJ)
        for e, index, here in ((1, 0, gx_low), (0, CI + 1, gx_high)):
            row = r_e[stage, e, :, LANES:].astype(F32)
            value = keep(here, jnp.concatenate([row[:CJ], row[CJ:]], axis=1))
            low = keep(here & gy_low, corner(2 * e + 1, 8, 4))
            high = keep(here & gy_high, corner(2 * e, 8, 4))
            place(dst, index, value, low, high, CJ)

    def wide_window(a, b):
        parts = []
        for g in range(4):
            lanes = slice(GROUP * g, GROUP * g + WINDOW)
            parts += [xv[b, pl.ds(a, NI + 2), :, lanes].reshape((NI + 2) * NJ, WINDOW), xvc[3 * a + b, :, lanes]]
        return jnp.concatenate(parts, axis=0)

    def fine_window(src, a, b):
        return jnp.concatenate(
            [src[b, pl.ds(a, NI), :, GROUP * g : GROUP * g + WINDOW].reshape(NI * NJ, WINDOW) for g in range(4)], axis=0)

    def coarse_window(src, a, b):
        return jnp.concatenate(
            [src[b, pl.ds(a, CI), :, GROUP * g : GROUP * g + WINDOW].reshape(CI * CJ, WINDOW) for g in range(2)],
            axis=0).astype(BF16)

    def three(body, looped):
        if looped:
            lax.fori_loop(0, 3, body, 0)
        else:
            for a in range(3):
                body(a, 0)

    def conv(window, weights, rows, looped):
        if not looped:
            total = dot(window(0, 0), weights[0])
            for t in range(1, TAPS):
                total = total + dot(window(t // 3, t % 3), weights[t])
            return total
        acc[0:rows] = jnp.zeros((rows, GROUP), F32)

        def body(a, carry):
            total = acc[0:rows]
            for b in range(3):
                total = total + dot(window(a, b), weights[3 * a + b])
            acc[0:rows] = total
            return carry

        lax.fori_loop(0, 3, body, 0)
        return acc[0:rows]

    def joined(window, weights):
        wide = jnp.concatenate([window(t // 3, t % 3) for t in range(TAPS)], axis=1)
        return dot(wide, weights[...].reshape(TAPS * WINDOW, GROUP))

    def by_group(window, weights, rows):
        def body(g, carry):
            lanes = pl.ds(pl.multiple_of(g * GROUP, GROUP), WINDOW)
            total = dot(window(0, 0, lanes), weights[0])
            for t in range(1, TAPS):
                total = total + dot(window(t // 3, t % 3, lanes), weights[t])
            acc[pl.ds(pl.multiple_of(g * rows, 16), rows)] = total
            return carry

        lax.fori_loop(0, 4, body, 0)
        return acc[0 : 4 * rows]

    def group_window(src):
        return lambda a, b, lanes: src[b, a : a + NI, :, lanes].reshape(NI * NJ, WINDOW)

    def wide_group_window(a, b, lanes):
        own = xv[b, a : a + NI + 2, :, lanes].reshape((NI + 2) * NJ, WINDOW)
        return jnp.concatenate([own, xvc[3 * a + b, :, lanes]], axis=0)

    def grads(window, slopes, store, looped):
        def body(a, carry):
            for b in range(3):
                g = dot(slopes[...], window(a, b))
                even = g[0:64, 0:384] + g[128:192, 128:512]
                odd = g[64:128, 128:384] + g[192:256, 256:512]
                shifted = jnp.concatenate([even[:, 64:192], even[:, 192:320]], axis=1)
                total = odd + shifted
                store(3 * a + b, total[:, 0:128].astype(BF16))
                half[3 * a + b] = total[:, 128:256]
            return carry

        three(body, looped)
        lane = lax.broadcasted_iota(jnp.int32, (64, 128), 1)
        for u in range(5):
            left = half[2 * u]
            right = pltpu.roll(half[2 * u + 1], 64, 1) if u < 4 else jnp.zeros_like(left)
            store(TAPS + u, jnp.where(lane < 64, left, right).astype(BF16))

    def pool_matrix(rows, columns, flip):
        r = lax.broadcasted_iota(jnp.int32, (rows, columns), 1 if flip else 0)
        s = lax.broadcasted_iota(jnp.int32, (rows, columns), 0 if flip else 1)
        r = r & 31
        return jnp.where(r == (s >> 5) * 8 + ((s & 15) >> 1), 1.0, 0.0).astype(BF16)

    def pool(value):
        sums = dot(pool_matrix(32, 128, False), value)
        lane = lax.broadcasted_iota(jnp.int32, (32, 128), 1)
        tiles = []
        for k in range(4):
            pair = []
            for m in range(2):
                tile = sums[:, 256 * k + 128 * m : 256 * k + 128 * m + 128]
                pair.append(tile + pltpu.roll(tile, 64, 1))
            tiles.append(jnp.where(lane < 64, pair[0], pair[1]))
        return jnp.concatenate(tiles, axis=1).reshape(CI, CJ, CLANES)

    def spread(value):
        lane = lax.broadcasted_iota(jnp.int32, (32, 128), 1)
        tiles = []
        for k in range(4):
            tile = value[:, 128 * k : 128 * k + 128]
            turned = pltpu.roll(tile, 64, 1)
            tiles += [jnp.where(lane < 64, tile, turned), jnp.where(lane < 64, turned, tile)]
        return jnp.concatenate(tiles, axis=1)

    def ungroup(value, rows):
        return jnp.concatenate([value[rows * g : rows * (g + 1)] for g in range(value.shape[0] // rows)], axis=1)

    def make_sum(part, in1, b2, in2, in3, res, send, got):
        def c1(r):
            return pltpu.make_async_remote_copy(part.at[pl.ds((1 - core) * 16, 16)], in1, send.at[0], got.at[0],
                                                device_id=other_core, device_id_type=MESH)

        def c2(r):
            w, peer = w_peer(r)
            return pltpu.make_async_remote_copy(b2.at[w], in2.at[r - 1], send.at[r], got.at[r],
                                                device_id=peer, device_id_type=MESH)

        def c3(r):
            _, peer = z_peer(r)
            return pltpu.make_async_remote_copy(in3.at[z_at], in3.at[z_at], send.at[15 + r], got.at[15 + r],
                                                device_id=peer, device_id_type=MESH)

        mine = core * 16 + w_at

        def c4(r):
            _, peer = w_peer(r)
            return pltpu.make_async_remote_copy(res.at[mine], res.at[mine], send.at[22 + r], got.at[22 + r],
                                                device_id=peer, device_id_type=MESH)

        def c5(r):
            own = pl.ds(core * 16, 16)
            return pltpu.make_async_remote_copy(res.at[own], res.at[own], send.at[38], got.at[38],
                                                device_id=other_core, device_id_type=MESH)

        def start(make, count):
            for r in FARTHEST[count]:
                make(r).start()

        def finish(make, count):
            for r in range(1, count):
                make(r).wait_recv()

        def s1():
            start(c1, 2)

        def s2():
            finish(c1, 2)
            b2[...] = (part[pl.ds(core * 16, 16)].astype(F32) + in1[...].astype(F32)).astype(BF16)
            start(c2, 16)

        def s3():
            finish(c2, 16)
            total = b2[w_at].astype(F32)
            for r in range(15):
                total = total + in2[r].astype(F32)
            in3[z_at] = total.astype(BF16)
            start(c3, 8)

        def s4():
            finish(c3, 8)
            total = in3[0].astype(F32)
            for r in range(1, 8):
                total = total + in3[r].astype(F32)
            res[mine] = total.astype(BF16)
            start(c4, 16)

        def s5():
            finish(c4, 16)
            start(c5, 2)

        def s6():
            finish(c5, 2)

        def s7():
            for make, count in ((c1, 2), (c2, 16), (c3, 8), (c4, 16), (c5, 2)):
                for r in range(1, count):
                    make(r).wait_send()

        return s1, s2, s3, s4, s5, s6, s7

    sum_sc = make_sum(part_sc, in1_sc, b2_sc, in2_sc, in3_sc, res_sc, s_sc, g_sc)
    sum_f = make_sum(part_f, in1_f, b2_f, in2_f, in3_f, res_f, s_f, g_f)

    cor[...] = jnp.zeros_like(cor)
    col[...] = jnp.zeros_like(col)
    loads[1].wait()
    coarse_st[...] = pool(cot[...].reshape(NI * NJ, LANES)).astype(BF16).astype(F32)
    pack_coarse(0)
    loads[0].wait()
    fine_st[...] = vol[...].astype(F32)
    pack_volume()
    pl.semaphore_wait(barrier, len(partners))
    coarse_rims, volume_rims = rim_copies(0, False), volume_copies()
    send(coarse_rims[:6] + volume_rims[:6] + volume_rims[6:] + coarse_rims[6:])

    def build(k, fwd, bwd):
        for w in (fwd, bwd):
            if w is not None:
                w[...] = jnp.zeros_like(w)

        def band(w, t, c0, c1, c2):
            zero = jnp.zeros_like(c0)
            pairs = ((c0, zero), (c1, c0), (c2, c1), (zero, c2))
            for m, tile in enumerate(jnp.concatenate(pair, axis=1) for pair in pairs):
                for pair in range(2):
                    row = 64 * (2 * pair + 1 + m)
                    w[t, row : row + 64, 128 * pair : 128 * pair + 128] = tile

        def body(t, carry):
            taps = [k[3 * t + c] for c in range(3)]
            band(fwd, t, *taps)
            if bwd is not None:
                c0, c1, c2 = (v.astype(F32).T.astype(BF16) for v in taps)
                band(bwd, 8 - t, c2, c1, c0)
            return carry

        lax.fori_loop(0, TAPS, body, 0)

    loads[2].wait()
    build(k1, w1, None)
    loads[3].wait()
    build(k2, w2, w2b)
    loads[4].wait()
    build(kc, wc, wcb)
    for padded in (xv, xh, xs, xp, xc):
        rows, tail = padded.shape[2], padded.shape[3] - PAD
        padded[:, :, :, 0:PAD] = jnp.zeros((3, padded.shape[1], rows, PAD), padded.dtype)
        padded[:, :, :, tail:] = jnp.zeros((3, padded.shape[1], rows, PAD), padded.dtype)
    xvc[:, :, 0:PAD] = jnp.zeros((TAPS, 32, PAD), BF16)
    xvc[:, :, PAD + LANES :] = jnp.zeros((TAPS, 32, PAD), BF16)
    part_sc[28:32] = jnp.zeros((4, 64, 128), BF16)
    part_f[28:32] = jnp.zeros((4, 32, 128), BF16)

    def widen(value):
        wide = spread(value)
        top = wide.astype(BF16)
        rest = (wide - top.astype(F32)).astype(BF16)
        return dot(pool_matrix(128, 64, True), jnp.concatenate([top, rest], axis=0))

    receive(rim_copies(0, False))
    unpack_rims(0)
    assemble_coarse(0, xc)
    pooled_slope = ungroup(joined(lambda a, b: coarse_window(xc, a, b), wcb), CI * CJ)
    upstream[...] = (cot[...].reshape(NI * NJ, LANES).astype(F32) + widen(pooled_slope) * 0.125).astype(BF16).astype(F32)

    receive(volume_copies())
    assemble_volume()

    first = ungroup(conv(wide_window, w1, 4 * (NI + 4) * NJ, 'c1' in LOOPED), (NI + 4) * NJ)
    sigma = sigmoid(first)
    hid[...] = (first * sigma).astype(BF16).astype(F32).reshape(NI + 4, NJ, LANES)
    own, own_sigma = first[NJ : NJ + NI * NJ], sigma[NJ : NJ + NI * NJ]
    slope1[...] = own_sigma * (1.0 + own * (1.0 - own_sigma))
    assemble_hidden()

    second = ungroup(conv(lambda a, b: fine_window(xh, a, b), w2, 4 * NI * NJ, 'c2' in LOOPED), NI * NJ)
    sigma = sigmoid(second)
    second_slope = (upstream[...] * (sigma * (1.0 + second * (1.0 - sigma)))).astype(BF16).astype(F32)
    fine_st[...] = second_slope.reshape(NI, NJ, LANES)
    pack_fine(1)
    send(rim_copies(1, True))
    fine = (second * sigma).astype(BF16)
    fine_keep[...] = fine
    coarse_st[...] = (pool(fine) * 0.125).astype(BF16).astype(F32)
    pack_coarse(2)
    send(rim_copies(2, False))

    def grouped_t(value, groups):
        return jnp.concatenate([value[:, GROUP * g : GROUP * (g + 1)] for g in range(groups)], axis=0).T.astype(BF16)

    slopes_t[...] = grouped_t(fine_st[...].reshape(NI * NJ, LANES), 4)

    def store_second(n, value):
        part_sc[n] = value

    def store_coarse(n, value):
        part_sc[14 + n] = value

    def store_first(n, value):
        part_f[pl.ds(2 * n, 2)] = value.reshape(2, 32, 128)

    grads(lambda a, b: fine_window(xh, a, b), slopes_t, store_second, 'g2' in LOOPED)
    pooled_t[...] = grouped_t(coarse_st[...].reshape(CI * CJ, CLANES), 2)
    grads(lambda a, b: coarse_window(xc, a, b), pooled_t, store_coarse, 'gc' in LOOPED)
    sum_sc[0]()

    rims = rim_copies(1, True)
    receive(rims[6:])
    assemble_rows(1, xs)
    sum_sc[1]()
    acc[0 : 4 * NI * NJ] = conv(lambda a, b: fine_window(xs, a, b), w2b, 4 * NI * NJ, "c3" in LOOPED)
    receive(rims[:6])
    unpack_rims(1)
    assemble_strips()
    add_strips(w2b)
    hidden_slope = ungroup(acc[0 : 4 * NI * NJ], NI * NJ)
    first_slope = (hidden_slope * slope1[...]).astype(BF16).astype(F32)
    slopes_t[...] = grouped_t(first_slope, 4)
    grads(lambda a, b: fine_window(xv, a + 1, b), slopes_t, store_first, 'g1' in LOOPED)
    sum_f[0]()
    sum_sc[2]()
    sum_f[1]()

    receive(rim_copies(2, False))
    unpack_rims(2)
    assemble_coarse(2, xp)
    coarse = ungroup(joined(lambda a, b: coarse_window(xp, a, b), wc), CI * CJ).astype(BF16)
    wide = spread(coarse.astype(F32)).astype(BF16)
    repeated = dot(pool_matrix(128, 32, True), wide)
    field[...] = (fine_keep[...].astype(F32) + repeated).astype(BF16).reshape(NI, NJ, LANES)

    sum_sc[3]()
    sum_f[2]()
    sum_f[3]()
    sum_sc[4]()
    sum_f[4]()
    sum_sc[5]()
    unpack_taps(lambda n: res_sc[n], out_second)
    unpack_reversed(lambda n: res_sc[14 + n], out_coarse)
    sum_f[5]()
    out_f[...] = res_f[...]
    sum_sc[6]()
    sum_f[6]()
    for there, _, copy in rim_copies(0, False) + volume_copies() + rim_copies(1, True) + rim_copies(2, False):
        pl.when(there)(copy.wait_send)


def unpack_kernel(held, second, coarse, f, field, first_out, second_out, coarse_out, first_grad, sem):
    copies = [
        pltpu.make_async_copy(src, dst, sem.at[n])
        for n, (src, dst) in enumerate((
            (held, field), (second, second_out), (coarse, coarse_out), (first_grad, first_out),
        ))
    ]
    for copy in copies[:3]:
        copy.start()
    unpack_taps(lambda n: f[2 * n : 2 * n + 2].reshape(64, 128), first_grad)
    copies[3].start()
    for copy in copies:
        copy.wait()


def per_device(volume, cotangent, first_kernel, second_kernel, coarse_kernel):
    in_hbm, in_vmem = (pl.BlockSpec(memory_space=space) for space in (pltpu.HBM, pltpu.VMEM))
    dma = pltpu.SemaphoreType.DMA

    def sum_buffers(rows):
        return [
            pltpu.VMEM((32, rows, 128), BF16), pltpu.VMEM((16, rows, 128), BF16), pltpu.VMEM((16, rows, 128), BF16),
            pltpu.VMEM((15, rows, 128), BF16), pltpu.VMEM((8, rows, 128), BF16), pltpu.VMEM((32, rows, 128), BF16),
        ]

    sc_bufs, f_bufs = sum_buffers(64), sum_buffers(32)
    mixed = [b for pair in zip(sc_bufs, f_bufs) for b in pair]
    scratch = [
        pltpu.VMEM((NI, NJ, LANES), F32),
        pltpu.VMEM((CI, CJ, CLANES), F32),
        pltpu.VMEM((3, NI + 4, NJ, LANES + 2 * PAD), BF16),
        pltpu.VMEM((3, NI + 2, NJ, LANES + 2 * PAD), BF16),
        pltpu.VMEM((3, NI + 2, NJ, LANES + 2 * PAD), BF16),
        pltpu.VMEM((3, CI + 2, CJ, CLANES + 2 * PAD), F32),
        pltpu.VMEM((3, CI + 2, CJ, CLANES + 2 * PAD), F32),
        pltpu.VMEM((NI * NJ, LANES), F32),
        pltpu.VMEM((NI * NJ, LANES), F32),
        pltpu.VMEM((NI * NJ, LANES), BF16),
        pltpu.VMEM((GROUP, 4 * NI * NJ), BF16),
        pltpu.VMEM((4 * (NI + 4) * NJ, GROUP), F32),
        pltpu.VMEM((TAPS, WINDOW, GROUP), BF16),
        pltpu.VMEM((TAPS, WINDOW, GROUP), BF16),
        pltpu.VMEM((TAPS, WINDOW, GROUP), BF16),
        pltpu.VMEM((TAPS, WINDOW, GROUP), BF16),
        pltpu.VMEM((TAPS, WINDOW, GROUP), BF16),
        pltpu.VMEM((3, 2, 16, 1280), BF16), pltpu.VMEM((3, 2, 16, 1280), BF16),
        pltpu.VMEM((3, 2, 16, 640), BF16), pltpu.VMEM((3, 2, 16, 640), BF16),
        pltpu.VMEM((3, 4, 16, 128), BF16), pltpu.VMEM((3, 4, 16, 128), BF16),
        pltpu.VMEM((16, 640), F32), pltpu.VMEM((2, 16, 640), F32),
        pltpu.VMEM((16, 128), F32), pltpu.VMEM((4, 16, 128), F32),
        *mixed,
        pltpu.VMEM((TAPS, 64, 128), F32),
        dma((4, 2)), dma((4, 2)), dma((4, 2)), dma((4, 2)), dma((4, 4)), dma((4, 4)),
        dma((39,)), dma((39,)), dma((39,)), dma((39,)), dma((5,)),
        pltpu.VMEM(volume.shape[1:], BF16), pltpu.VMEM(volume.shape[1:], BF16),
        *[pltpu.VMEM((27, 64, 64), BF16)] * 3,
        pltpu.VMEM((2, 16, LANES + 2 * PAD), F32),
        pltpu.VMEM((GROUP, 2 * CI * CJ), BF16),
        pltpu.VMEM((NI + 4, NJ, LANES), F32),
        pltpu.VMEM((TAPS, 32, LANES + 2 * PAD), BF16),
        pltpu.VMEM((16, LANES), F32), pltpu.VMEM((16, 256), F32),
        pltpu.VMEM((2, 16, LANES), F32), pltpu.VMEM((4, 16, 256), F32),
        pltpu.VMEM((2, 3, 16, LANES), F32),
        pltpu.VMEM((2, 16, LANES), BF16), pltpu.VMEM((2, 16, LANES), BF16),
        pltpu.VMEM((4, 16, 256), BF16), pltpu.VMEM((4, 16, 256), BF16),
        pltpu.VMEM((2, 2, NJ, LANES), BF16),
    ]
    block = volume.shape[1:]
    taps = (27, 64, 64)
    kernels = (first_kernel, second_kernel, coarse_kernel)
    operands = (volume[0], cotangent[0], *(k.reshape(taps) for k in kernels))
    field, second_grad, coarse_grad, f = pl.pallas_call(
        kernel,
        out_shape=(
            jax.ShapeDtypeStruct(block, BF16),
            jax.ShapeDtypeStruct(taps, F32),
            jax.ShapeDtypeStruct(taps, F32),
            jax.ShapeDtypeStruct((32, 32, 128), BF16),
        ),
        in_specs=[in_hbm] * 5,
        out_specs=(in_vmem,) * 4,
        scratch_shapes=scratch,
        compiler_params=pltpu.CompilerParams(
            collective_id=0, has_side_effects=True, vmem_limit_bytes=48 * 1024 * 1024
        ),
        name="block",
    )(*(pltpu.with_memory_space_constraint(v, pltpu.HBM) for v in operands))
    field, first_grad, second_grad, coarse_grad = pl.pallas_call(
        unpack_kernel,
        out_shape=(jax.ShapeDtypeStruct(block, BF16),) + (jax.ShapeDtypeStruct(taps, F32),) * 3,
        in_specs=[in_vmem] * 4,
        out_specs=(in_hbm,) * 4,
        scratch_shapes=[
            pltpu.VMEM(taps, F32), dma((4,)),
        ],
        compiler_params=pltpu.CompilerParams(vmem_limit_bytes=32 * 1024 * 1024),
        name="unpack",
    )(field, second_grad, coarse_grad, f)
    kernel_shape = first_kernel.shape
    return (
        field[None],
        first_grad.reshape(kernel_shape),
        second_grad.reshape(kernel_shape),
        coarse_grad.reshape(kernel_shape),
    )


def solution(mesh):
    in_specs = (P("dp", "gx", "gy", None), P("dp", "gx", "gy", None), P(), P(), P())
    out_specs = (P("dp", "gx", "gy", None), P(), P(), P())
    return jax.shard_map(
        per_device, mesh=mesh, in_specs=in_specs, out_specs=out_specs, check_vma=False
    )
```
